32 devices in a mesh: img: 16 (over z, x, core), seq: 2 (over y).
Axes of the slice: x: 2, y: 2, z: 4, core: 2. Of those that a mesh axis runs over, the one named last changes fastest.
Arguments:
- tokens: bfloat16 [32, 656, 768], P('img', 'seq'), may hold values from -6 to 6
- token_mask: int32 [32, 656], P('img', 'seq'), may hold values from 0 to 1, as said below
- ln1_gain: bfloat16 [768], P('img'), may hold values from 0.25 to 1.75
- ln1_bias: bfloat16 [768], P('img'), may hold values from -1.75 to 1.75
- w_qkv: bfloat16 [768, 2304], P('img'), may hold values from -0.21875 to 0.21875
- bias_q: bfloat16 [768], P('img'), may hold values from -1.75 to 1.75
- bias_v: bfloat16 [768], P('img'), may hold values from -1.75 to 1.75
- w_out: bfloat16 [768, 768], P('img'), may hold values from -3 to 3
- bias_out: bfloat16 [768], P('img'), may hold values from -1.75 to 1.75
- ln2_gain: bfloat16 [768], P('img'), may hold values from 0.25 to 1.75
- ln2_bias: bfloat16 [768], P('img'), may hold values from -1.75 to 1.75
- w_up: bfloat16 [768, 3072], P('img'), may hold values from -0.21875 to 0.21875
- bias_up: bfloat16 [3072], P('img'), may hold values from -1.75 to 1.75
- w_down: bfloat16 [3072, 768], P('img'), may hold values from -0.109375 to 0.109375
- bias_down: bfloat16 [768], P('img'), may hold values from -1.75 to 1.75
- cotangent: bfloat16 [32, 656, 768], P('img', 'seq'), may hold values from -8 to 8
Outputs:
- output: float32 [32, 656, 768], P('img', 'seq')
- input_grad: float32 [32, 656, 768], P('img', 'seq')
- grad_ln1_gain: float32 [768], P('img')
- grad_ln1_bias: float32 [768], P('img')
- grad_w_qkv: float32 [768, 2304], P('img')
- grad_bias_q: float32 [768], P('img')
- grad_bias_v: float32 [768], P('img')
- grad_w_out: float32 [768, 768], P('img')
- grad_bias_out: float32 [768], P('img')
- grad_ln2_gain: float32 [768], P('img')
- grad_ln2_bias: float32 [768], P('img')
- grad_w_up: float32 [768, 3072], P('img')
- grad_bias_up: float32 [3072], P('img')
- grad_w_down: float32 [3072, 768], P('img')
- grad_bias_down: float32 [768], P('img')
The draws below stay inside these ranges and needn't reach their ends.
Inputs may be any that keep to these rules, and one draw needn't show every extreme that they name: `token_mask`: each image has between 492 and 655 real tokens, spread over its 2 blocks of 328 rows as evenly as possible, the earlier blocks taking the extra ones; in every block the real tokens come first.
All inputs are finite; a program needn't handle non-finite values.
Results may differ from the reference program's by a relative error of at most 0.01.
Values may be sent and summed in bfloat16 or wider, within the bound.
No kernel may reach another device: no remote copies, remote signals or barrier semaphores. Data moves between devices by JAX's collectives and lax.ppermute only.
A program may use at most 128 MiB of HBM per device.

```python
import jax
import jax.numpy as jnp
from jax import lax

HEADS = 12
HEAD_DIM = 64
FF = 3072
SHARD = 328
D = 768
SEQ = 656
IMAGES = 32


def draw_token_mask(key, part):
    key = jax.random.fold_in(key, 7)
    shard_count = SEQ // SHARD
    lengths = jax.random.randint(key, (IMAGES,), SEQ - SEQ // 4, SEQ)
    positions = jnp.arange(SEQ)
    shard_of = positions // SHARD
    within = positions % SHARD
    counts = (lengths[:, None] + shard_count - 1 - shard_of[None, :]) // shard_count
    return (within[None, :] < counts).astype(jnp.int32)


def spiked(array, rng, source, target, shards_of, factor):
    def block_of(dim):
        return (jnp.arange(array.shape[dim]) // (array.shape[dim] // shards_of)).reshape((-1,) + (1,) * (array.ndim - 1 - dim))

    first = jax.random.permutation(rng, shards_of)[block_of(target)]
    second = (block_of(target) + shards_of // 2) % shards_of
    return jnp.where((block_of(source) == first) | (block_of(source) == second), factor * array, array)


def block_scale(key, shape, shards, low, high):
    def one(position, shards_of):
        heights = jax.random.uniform(jax.random.fold_in(jax.random.fold_in(key, 6), position), (shards_of,), jnp.float32, low / len(shards), high / len(shards))
        return jnp.repeat(jnp.exp(heights), shape[position] // shards_of).reshape((-1,) + (1,) * (len(shape) - position - 1))

    factor_of = one(*shards[0])
    for cut in shards[1:]:
        factor_of = factor_of * one(*cut)
    return factor_of


def scatter_about(own_key, extent, deviation, limit, cuts=(), held_as=jnp.bfloat16):
    result = jax.random.normal(own_key, extent, jnp.float32) * deviation
    if len(cuts) > 0:
        result = block_scale(own_key, extent, cuts, -0.22, 0.18) * result
    return jnp.clip(result, min=-limit, max=limit).astype(held_as)


def bell_draw_with(stream_key, dims, width, bound, shards, heavy, held_as=jnp.bfloat16):
    entries = width * jax.random.normal(stream_key, dims, jnp.float32)
    if shards:
        entries = entries * block_scale(stream_key, dims, shards, -0.22, 0.18)
    return jnp.clip(spiked(entries, jax.random.fold_in(stream_key, 3), *heavy), -bound, bound).astype(held_as)


def setup_inputs(seed: int = 0) -> dict:
    seeds = jax.random.split(jax.random.key(seed), 17)
    return {
        "tokens": scatter_about(seeds[0], (IMAGES, SEQ, D), 1.0, 6.0, ((0, 16), (1, 2))),
        "token_mask": draw_token_mask(jax.random.fold_in(seeds[16], 71), 0),
        "ln1_gain": jnp.clip(1.0 + 0.15 * jax.random.normal(seeds[2], (D,), jnp.float32), 0.25, 1.75).astype(jnp.bfloat16),
        "ln1_bias": scatter_about(seeds[3], (D,), 0.3, 1.75, ((0, 16),)),
        "w_qkv": scatter_about(seeds[4], (D, 3 * D), D ** -0.5, 0.21875, ((0, 16),)),
        "bias_q": scatter_about(seeds[5], (D,), 0.3, 1.75, ((0, 16),)),
        "bias_v": scatter_about(seeds[6], (D,), 0.3, 1.75, ((0, 16),)),
        "w_out": scatter_about(seeds[7], (D, D), (max(1, 4 * D // SEQ)) ** -0.5, 3.0, ((0, 16),)),
        "bias_out": scatter_about(seeds[8], (D,), 0.3, 1.75, ((0, 16),)),
        "ln2_gain": jnp.clip(1.0 + 0.15 * jax.random.normal(seeds[9], (D,), jnp.float32), 0.25, 1.75).astype(jnp.bfloat16),
        "ln2_bias": scatter_about(seeds[10], (D,), 0.3, 1.75, ((0, 16),)),
        "w_up": scatter_about(seeds[11], (D, FF), D ** -0.5, 0.21875, ((0, 16),)),
        "bias_up": scatter_about(seeds[12], (FF,), 0.3, 1.75, ((0, 16),)),
        "w_down": scatter_about(seeds[13], (FF, D), FF ** -0.5, 0.109375, ((0, 16),)),
        "bias_down": scatter_about(seeds[14], (D,), 0.3, 1.75, ((0, 16),)),
        "cotangent": bell_draw_with(seeds[15], (IMAGES, SEQ, D), 1.0, 8.0, ((0, 16), (1, 2)), (0, 2, 16, 2.0)),
    }


@jax.custom_vjp
def low(v):
    return lax.optimization_barrier(v.astype(jnp.bfloat16)).astype(jnp.float32)

@jax.custom_vjp
def low_back(v):
    return v

def low_keep(v):
    return (low(v), None)

def low_pass(kept, grad):
    return (grad,)

def back_keep(v):
    return (v, None)

def back_low(kept, grad):
    return (low(grad),)
low.defvjp(low_keep, low_pass)
low_back.defvjp(back_keep, back_low)
epsilon = 1e-06

def layer_norm(values, gain, shift):
    center = lax.optimization_barrier(jnp.mean(values, axis=-1, keepdims=True))
    offset = values - center
    spread = lax.optimization_barrier(jnp.mean(offset * offset, axis=-1, keepdims=True))
    return offset * lax.rsqrt(spread + epsilon) * gain + shift

def product(left, right):
    return jnp.dot(left, right, precision=lax.Precision.HIGHEST, preferred_element_type=jnp.float32)

def attend_head(query_head, key_head, value_head, key_mask):
    scaling = HEAD_DIM ** (-0.5)
    scores = low_back(scaling * product(query_head, key_head.T))
    scores = jnp.where(key_mask[None, :] > 0.5, scores, -1000000000.0)
    highest = lax.optimization_barrier(jnp.max(scores, axis=-1, keepdims=True))
    weights = jnp.exp(scores - highest)
    weights = weights / lax.optimization_barrier(jnp.sum(weights, axis=-1, keepdims=True))
    return product(low(weights), value_head)

def block(inputs, key_mask, params):
    gain_one, shift_one, qkv_full, query_bias, value_bias, out_full, out_bias, gain_two, shift_two, up_full, up_bias, down_full, down_bias = params
    normed = low(layer_norm(inputs, gain_one, shift_one))
    projected = product(normed, qkv_full)
    query_part = projected[:, :D] + query_bias
    key_part = projected[:, D:2 * D]
    value_part = projected[:, 2 * D:] + value_bias
    stacked = low_back(low(jnp.stack([query_part, key_part, value_part])))
    per_head = stacked.reshape(3, SEQ, HEADS, HEAD_DIM).transpose(2, 0, 1, 3)

    def one_head(triple):
        return attend_head(triple[0], triple[1], triple[2], key_mask)
    attended = lax.map(jax.checkpoint(one_head), per_head)
    merged = low_back(low(attended.transpose(1, 0, 2).reshape(SEQ, D)))
    branch = low_back(product(merged, out_full) + out_bias)
    middle = inputs + branch
    second = low(layer_norm(middle, gain_two, shift_two))
    pre_act = low_back(product(second, up_full) + up_bias)
    hidden = low(jax.nn.gelu(pre_act, approximate=False))
    return middle + low_back(product(hidden, down_full) + down_bias)

def reference(tokens, token_mask, ln1_gain, ln1_bias, w_qkv, bias_q, bias_v, w_out, bias_out, ln2_gain, ln2_bias, w_up, bias_up, w_down, bias_down, cotangent):
    params = tuple((tensor.astype(jnp.float32) for tensor in (ln1_gain, ln1_bias, w_qkv, bias_q, bias_v, w_out, bias_out, ln2_gain, ln2_bias, w_up, bias_up, w_down, bias_down)))

    def image_step(running, pieces):
        picture, key_mask, upstream = pieces
        mask_float = key_mask.astype(jnp.float32)

        def forward(image_in, *weights):
            return block(image_in, mask_float, weights)
        output, pullback = jax.vjp(forward, picture.astype(jnp.float32), *params)
        gradients = pullback(upstream.astype(jnp.float32) * mask_float[:, None])
        running = tuple((before + grad_part for before, grad_part in zip(running, gradients[1:])))
        return (running, (output, gradients[0]))
    zero_sums = tuple((jnp.zeros(tensor.shape, jnp.float32) for tensor in params))
    summed, (outputs, input_grads) = lax.scan(image_step, zero_sums, (tokens, token_mask, cotangent))
    return (outputs, input_grads, summed[0], summed[1], summed[2], summed[3], summed[4], summed[5], summed[6], summed[7], summed[8], summed[9], summed[10], summed[11], summed[12])
```

```python
import functools
import jax
import jax.numpy as jnp
from jax import lax
from jax.experimental import pallas as pl
from jax.experimental.pallas import tpu as pltpu
from jax.sharding import PartitionSpec as P

HEADS = 12
epsilon = 1e-06


def layer_norm(values, gain, shift):
    center = jnp.mean(values, axis=-1, keepdims=True)
    offset = values - center
    spread = jnp.mean(offset * offset, axis=-1, keepdims=True)
    return offset * lax.rsqrt(spread + epsilon) * gain + shift


def gelu_exact(pre_value):
    return jax.nn.gelu(pre_value, approximate=False)


def split_heads(tensor, head_count):
    images, row_count, columns = tensor.shape
    head_size = columns // head_count
    moved = tensor.reshape(images, row_count, head_count, head_size).transpose(0, 2, 1, 3)
    return moved.reshape(images * head_count, row_count, head_size)


def join_heads(tensor, images):
    combined, row_count, head_size = tensor.shape
    heads_here = combined // images
    moved = tensor.reshape(images, heads_here, row_count, head_size).transpose(0, 2, 1, 3)
    return moved.reshape(images, row_count, heads_here * head_size)


def attend_forward(query_head, key_head, value_head, key_mask):
    scaling = query_head.shape[-1] ** (-0.5)
    row_count = query_head.shape[0]
    blocks = max(1, 2 * row_count // key_head.shape[0])

    def one_block(query_block):
        scores = (
            jnp.einsum("qd,kd->qk", query_block, key_head, preferred_element_type=jnp.float32)
            * scaling
        )
        scores = jnp.where(key_mask[None, :] > 0.5, scores, -1000000000.0)
        highest = jnp.max(scores, axis=-1, keepdims=True)
        weights = jnp.exp(scores - highest)
        totals = jnp.sum(weights, axis=-1, keepdims=True)
        mixed = jnp.dot(
            (weights / totals).astype(jnp.bfloat16), value_head, preferred_element_type=jnp.float32
        )
        return (mixed, (highest + jnp.log(totals))[:, 0])

    mixed, log_sums = lax.map(one_block, query_head.reshape(blocks, row_count // blocks, -1))
    return (mixed.reshape(row_count, -1), log_sums.reshape(row_count))


def attend_backward(query_head, key_head, value_head, key_mask, log_sums, out_grad):
    scaling = query_head.shape[-1] ** (-0.5)
    row_count = query_head.shape[0]
    blocks = max(1, 2 * row_count // key_head.shape[0])
    block_rows = row_count // blocks

    def one_block(carry, pieces):
        key_grad, value_grad = carry
        query_block, log_block, grad_block = pieces
        scores = (
            jnp.einsum("qd,kd->qk", query_block, key_head, preferred_element_type=jnp.float32)
            * scaling
        )
        scores = jnp.where(key_mask[None, :] > 0.5, scores, -1000000000.0)
        weights = jnp.exp(scores - log_block[:, None])
        value_grad = value_grad + jnp.einsum(
            "qk,qd->kd",
            weights.astype(jnp.bfloat16),
            grad_block,
            preferred_element_type=jnp.float32,
        )
        weight_grad = jnp.einsum(
            "qd,kd->qk", grad_block, value_head, preferred_element_type=jnp.float32
        )
        centered = jnp.sum(weights * weight_grad, axis=-1, keepdims=True)
        score_grad = (weights * (weight_grad - centered)).astype(jnp.bfloat16)
        query_grad = jnp.dot(score_grad, key_head, preferred_element_type=jnp.float32) * scaling
        key_grad = (
            key_grad
            + jnp.einsum("qk,qd->kd", score_grad, query_block, preferred_element_type=jnp.float32)
            * scaling
        )
        return ((key_grad, value_grad), query_grad)

    zeros_init = jnp.zeros(key_head.shape, jnp.float32)
    (key_grad, value_grad), query_grad = lax.scan(
        one_block,
        (zeros_init, zeros_init),
        (
            query_head.reshape(blocks, block_rows, -1),
            log_sums.reshape(blocks, block_rows),
            out_grad.reshape(blocks, block_rows, -1),
        ),
    )
    return (query_grad.reshape(row_count, -1), key_grad, value_grad)


def heads_forward(query_heads, key_heads, value_heads, key_masks):
    return lax.map(
        lambda pieces: attend_forward(pieces[0], pieces[1], pieces[2], pieces[3]),
        (query_heads, key_heads, value_heads, key_masks),
    )


def heads_backward(query_heads, key_heads, value_heads, key_masks, log_sums, out_grads):
    return lax.map(
        lambda pieces: attend_backward(
            pieces[0], pieces[1], pieces[2], pieces[3], pieces[4], pieces[5]
        ),
        (query_heads, key_heads, value_heads, key_masks, log_sums, out_grads),
    )


def column_sum(tensor):
    return jnp.sum(tensor.astype(jnp.float32), axis=(0, 1))


def general_body(
    tokens,
    token_mask,
    ln1_gain,
    ln1_bias,
    w_qkv,
    bias_q,
    bias_v,
    w_out,
    bias_out,
    ln2_gain,
    ln2_bias,
    w_up,
    bias_up,
    w_down,
    bias_down,
    cotangent,
):
    (
        gain_one,
        shift_one,
        qkv_full,
        query_bias,
        value_bias,
        out_full,
        out_bias,
        gain_two,
        shift_two,
        up_full,
        up_bias,
        down_full,
        down_bias,
    ) = (
        lax.all_gather(ln1_gain, "img", axis=0, tiled=True),
        lax.all_gather(ln1_bias, "img", axis=0, tiled=True),
        lax.all_gather(w_qkv, "img", axis=0, tiled=True),
        lax.all_gather(bias_q, "img", axis=0, tiled=True),
        lax.all_gather(bias_v, "img", axis=0, tiled=True),
        lax.all_gather(w_out, "img", axis=0, tiled=True),
        lax.all_gather(bias_out, "img", axis=0, tiled=True),
        lax.all_gather(ln2_gain, "img", axis=0, tiled=True),
        lax.all_gather(ln2_bias, "img", axis=0, tiled=True),
        lax.all_gather(w_up, "img", axis=0, tiled=True),
        lax.all_gather(bias_up, "img", axis=0, tiled=True),
        lax.all_gather(w_down, "img", axis=0, tiled=True),
        lax.all_gather(bias_down, "img", axis=0, tiled=True),
    )
    images, shard_rows, model_dim = tokens.shape
    seq_parts = lax.axis_size("seq")
    inputs = tokens.astype(jnp.float32)
    mask_float = token_mask.astype(jnp.float32)
    normed, norm_one_pull = jax.vjp(
        layer_norm, inputs, gain_one.astype(jnp.float32), shift_one.astype(jnp.float32)
    )
    normed_low = normed.astype(jnp.bfloat16)
    projected = jnp.einsum("bsd,de->bse", normed_low, qkv_full, preferred_element_type=jnp.float32)
    query_tok = (projected[..., :model_dim] + query_bias.astype(jnp.float32)).astype(jnp.bfloat16)
    key_tok = projected[..., model_dim : 2 * model_dim].astype(jnp.bfloat16)
    value_tok = (projected[..., 2 * model_dim :] + value_bias.astype(jnp.float32)).astype(
        jnp.bfloat16
    )
    mask_low = token_mask.astype(jnp.bfloat16)
    local_heads = HEADS // seq_parts
    stacked = jnp.stack([query_tok, key_tok, value_tok], axis=2)
    mask_tile = jnp.broadcast_to(mask_low[:, :, None, None], (images, shard_rows, 1, seq_parts))
    stacked_heads, mask_heads = (
        lax.all_to_all(stacked, "seq", split_axis=3, concat_axis=1, tiled=True),
        lax.all_to_all(mask_tile, "seq", split_axis=3, concat_axis=1, tiled=True),
    )
    query_heads = split_heads(stacked_heads[:, :, 0], local_heads)
    key_heads = split_heads(stacked_heads[:, :, 1], local_heads)
    value_heads = split_heads(stacked_heads[:, :, 2], local_heads)
    key_masks = jnp.repeat(mask_heads[:, :, 0, 0].astype(jnp.float32), local_heads, axis=0)
    attended, log_sums = heads_forward(query_heads, key_heads, value_heads, key_masks)
    merged_heads = join_heads(attended, images).astype(jnp.bfloat16)
    merged = lax.all_to_all(merged_heads, "seq", split_axis=1, concat_axis=2, tiled=True)
    branch = jnp.einsum(
        "bsd,de->bse", merged, out_full, preferred_element_type=jnp.float32
    ) + out_bias.astype(jnp.float32)
    middle = inputs + branch
    second, norm_two_pull = jax.vjp(
        layer_norm, middle, gain_two.astype(jnp.float32), shift_two.astype(jnp.float32)
    )
    second_low = second.astype(jnp.bfloat16)
    pre_act = jnp.einsum(
        "bsd,df->bsf", second_low, up_full, preferred_element_type=jnp.float32
    ) + up_bias.astype(jnp.float32)
    hidden, gelu_pull = jax.vjp(gelu_exact, pre_act)
    hidden_low = hidden.astype(jnp.bfloat16)
    output = (
        middle
        + jnp.einsum("bsf,fd->bsd", hidden_low, down_full, preferred_element_type=jnp.float32)
        + down_bias.astype(jnp.float32)
    )
    upstream = cotangent.astype(jnp.float32) * mask_float[..., None]
    down_in = upstream.astype(jnp.bfloat16)
    grad_down = jnp.einsum("bsf,bsd->fd", hidden_low, down_in, preferred_element_type=jnp.float32)
    grad_down_bias = column_sum(down_in)
    hidden_grad = jnp.einsum("bsd,fd->bsf", down_in, down_full, preferred_element_type=jnp.float32)
    pre_grad = gelu_pull(hidden_grad)[0].astype(jnp.bfloat16)
    grad_up = jnp.einsum("bsd,bsf->df", second_low, pre_grad, preferred_element_type=jnp.float32)
    grad_up_bias = column_sum(pre_grad)
    second_grad = jnp.einsum("bsf,df->bsd", pre_grad, up_full, preferred_element_type=jnp.float32)
    middle_ln_grad, grad_gain_two, grad_shift_two = norm_two_pull(second_grad)
    middle_grad = upstream + middle_ln_grad
    branch_grad = middle_grad.astype(jnp.bfloat16)
    grad_out = jnp.einsum("bsd,bse->de", merged, branch_grad, preferred_element_type=jnp.float32)
    grad_out_bias = column_sum(branch_grad)
    merged_grad = jnp.einsum(
        "bse,de->bsd", branch_grad, out_full, preferred_element_type=jnp.float32
    ).astype(jnp.bfloat16)
    grad_heads_in = lax.all_to_all(merged_grad, "seq", split_axis=2, concat_axis=1, tiled=True)
    query_grad, key_grad, value_grad = heads_backward(
        query_heads,
        key_heads,
        value_heads,
        key_masks,
        log_sums,
        split_heads(grad_heads_in, local_heads),
    )
    triple = jnp.stack(
        [
            join_heads(query_grad, images),
            join_heads(key_grad, images),
            join_heads(value_grad, images),
        ],
        axis=2,
    ).astype(jnp.bfloat16)
    qkv_grad = lax.all_to_all(triple, "seq", split_axis=1, concat_axis=3, tiled=True)
    qkv_flat = qkv_grad.reshape(images, shard_rows, 3 * model_dim)
    grad_qkv = jnp.einsum("bsd,bse->de", normed_low, qkv_flat, preferred_element_type=jnp.float32)
    grad_query_bias = column_sum(qkv_grad[:, :, 0])
    grad_value_bias = column_sum(qkv_grad[:, :, 2])
    normed_grad = jnp.einsum("bse,de->bsd", qkv_flat, qkv_full, preferred_element_type=jnp.float32)
    input_ln_grad, grad_gain_one, grad_shift_one = norm_one_pull(normed_grad)
    input_grad = middle_grad + input_ln_grad
    shards_all = (
        lax.psum_scatter(grad_gain_one, "img", scatter_dimension=0, tiled=True),
        lax.psum_scatter(grad_shift_one, "img", scatter_dimension=0, tiled=True),
        lax.psum_scatter(grad_qkv, "img", scatter_dimension=0, tiled=True),
        lax.psum_scatter(grad_query_bias, "img", scatter_dimension=0, tiled=True),
        lax.psum_scatter(grad_value_bias, "img", scatter_dimension=0, tiled=True),
        lax.psum_scatter(grad_out, "img", scatter_dimension=0, tiled=True),
        lax.psum_scatter(grad_out_bias, "img", scatter_dimension=0, tiled=True),
        lax.psum_scatter(grad_gain_two, "img", scatter_dimension=0, tiled=True),
        lax.psum_scatter(grad_shift_two, "img", scatter_dimension=0, tiled=True),
        lax.psum_scatter(grad_up, "img", scatter_dimension=0, tiled=True),
        lax.psum_scatter(grad_up_bias, "img", scatter_dimension=0, tiled=True),
        lax.psum_scatter(grad_down, "img", scatter_dimension=0, tiled=True),
        lax.psum_scatter(grad_down_bias, "img", scatter_dimension=0, tiled=True),
    )
    summed_all = lax.psum(
        (
            shards_all[0],
            shards_all[1],
            shards_all[2],
            shards_all[3],
            shards_all[4],
            shards_all[5],
            shards_all[6],
            shards_all[7],
            shards_all[8],
            shards_all[9],
            shards_all[10],
            shards_all[11],
            shards_all[12],
        ),
        "seq",
    )
    return (
        output,
        input_grad,
        summed_all[0],
        summed_all[1],
        summed_all[2],
        summed_all[3],
        summed_all[4],
        summed_all[5],
        summed_all[6],
        summed_all[7],
        summed_all[8],
        summed_all[9],
        summed_all[10],
        summed_all[11],
        summed_all[12],
    )


LOW = jnp.bfloat16
F32 = jnp.float32
VMEM = 56 * 1024 * 1024


def dot_nt(left, right):
    return lax.dot_general(left, right, (((1,), (1,)), ((), ())), preferred_element_type=F32)


def dot_nn(left, right):
    return lax.dot_general(left, right, (((1,), (0,)), ((), ())), preferred_element_type=F32)


def dot_tn(left, right):
    return lax.dot_general(left, right, (((0,), (0,)), ((), ())), preferred_element_type=F32)


def attention_forward_kernel(scale, size, query_ref, key_ref, value_ref, mask_ref, out_ref, log_ref):
    real = mask_ref[...] > 0.5
    query = query_ref[...] * jnp.asarray(scale, LOW)
    key = jnp.where(real, key_ref[...], key_ref[0:1, :])
    value = value_ref[...]
    lane = lax.broadcasted_iota(jnp.int32, key.shape, 1)
    pieces = []
    for head in range(2):
        mine = (lane // size) == head
        scores = dot_nt(jnp.where(mine, key, jnp.zeros_like(key)), query)
        highest = jnp.max(scores, axis=0, keepdims=True)
        weights = jnp.exp(scores - highest).astype(LOW)
        extended = jnp.where(real, jnp.where(mine, value, jnp.ones_like(value)), jnp.zeros_like(value))
        mixed = dot_tn(extended, weights)
        own, other = head * size, (1 - head) * size
        totals = mixed[other : other + size, :]
        pieces.append(mixed[own : own + size, :] / totals)
        log_ref[0, head : head + 1, :] = highest + jnp.log(totals[0:1, :])
    out_ref[...] = jnp.concatenate(pieces, axis=0).T.astype(LOW)


def attention_forward(qkv, mask_column):
    rows, width = qkv.shape
    dim = width // 3
    size = dim // HEADS
    pairs = HEADS // 2
    block = (rows, 2 * size)
    return pl.pallas_call(
        functools.partial(attention_forward_kernel, size ** (-0.5), size),
        grid=(pairs,),
        in_specs=[
            pl.BlockSpec(block, lambda p: (0, p)),
            pl.BlockSpec(block, lambda p: (0, pairs + p)),
            pl.BlockSpec(block, lambda p: (0, 2 * pairs + p)),
            pl.BlockSpec((rows, 1), lambda p: (0, 0)),
        ],
        out_specs=[
            pl.BlockSpec(block, lambda p: (0, p)),
            pl.BlockSpec((1, 2, rows), lambda p: (p, 0, 0)),
        ],
        out_shape=[
            jax.ShapeDtypeStruct((rows, dim), LOW),
            jax.ShapeDtypeStruct((pairs, 2, rows), F32),
        ],
        compiler_params=pltpu.CompilerParams(vmem_limit_bytes=VMEM),
        cost_estimate=pl.CostEstimate(
            flops=8 * rows * rows * dim, bytes_accessed=8 * rows * dim, transcendentals=HEADS * rows * rows
        ),
        name="attention_forward",
    )(qkv, qkv, qkv, mask_column)


def attention_backward_kernel(
    scale, size, query_ref, key_ref, value_ref, mask_ref, log_ref, grad_ref, dq_ref, dk_ref, dv_ref
):
    real = mask_ref[...] > 0.5
    query = query_ref[...] * jnp.asarray(scale, LOW)
    zeros = jnp.zeros_like(query)
    key_kept = jnp.where(real, key_ref[...], zeros)
    key = jnp.where(real, key_kept, key_ref[0:1, :])
    value = jnp.where(real, value_ref[...], zeros)
    grad = grad_ref[...]
    lane = lax.broadcasted_iota(jnp.int32, key.shape, 1)
    totals = None
    for head in range(2):
        mine = (lane // size) == head
        scores = dot_nt(jnp.where(mine, key, zeros), query)
        weights = jnp.exp(scores - log_ref[0, head : head + 1, :])
        grad_here = jnp.where(mine, grad, zeros)
        value_grad = dot_nn(weights.astype(LOW), grad_here)
        weight_grad = dot_nt(value, grad_here)
        centered = jnp.sum(weights * weight_grad, axis=0, keepdims=True)
        score_grad = (weights * (weight_grad - centered)).astype(LOW)
        key_grad = dot_nn(score_grad, jnp.where(mine, query, zeros))
        query_grad = dot_tn(jnp.where(mine, key_kept, zeros), score_grad)
        if totals is None:
            totals = (query_grad, key_grad, value_grad)
        else:
            totals = tuple(a + b for a, b in zip(totals, (query_grad, key_grad, value_grad)))
    query_grad, key_grad, value_grad = totals
    dq_ref[...] = (query_grad * scale).T.astype(LOW)
    dk_ref[...] = jnp.where(real, key_grad, 0.0).astype(LOW)
    dv_ref[...] = jnp.where(real, value_grad, 0.0).astype(LOW)


def attention_backward(qkv, mask_column, logs, grad):
    rows, width = qkv.shape
    dim = width // 3
    size = dim // HEADS
    pairs = HEADS // 2
    block = (rows, 2 * size)
    spec = pl.BlockSpec(block, lambda p: (0, p))
    return pl.pallas_call(
        functools.partial(attention_backward_kernel, size ** (-0.5), size),
        grid=(pairs,),
        in_specs=[
            spec,
            pl.BlockSpec(block, lambda p: (0, pairs + p)),
            pl.BlockSpec(block, lambda p: (0, 2 * pairs + p)),
            pl.BlockSpec((rows, 1), lambda p: (0, 0)),
            pl.BlockSpec((1, 2, rows), lambda p: (p, 0, 0)),
            spec,
        ],
        out_specs=[spec, spec, spec],
        out_shape=[jax.ShapeDtypeStruct((rows, dim), LOW)] * 3,
        compiler_params=pltpu.CompilerParams(vmem_limit_bytes=VMEM),
        cost_estimate=pl.CostEstimate(
            flops=20 * rows * rows * dim, bytes_accessed=16 * rows * dim, transcendentals=HEADS * rows * rows
        ),
        name="attention_backward",
    )(qkv, qkv, qkv, mask_column, logs, grad)


def mlp_kernel(
    second_ref, dz_ref, up_ref, up_bias_ref, down_ref,
    out_ref, second_grad_ref, down_grad_ref, up_grad_ref, up_bias_grad_ref,
):
    step = pl.program_id(0)
    second = second_ref[...]
    dz = dz_ref[...]
    up = up_ref[...]
    down = down_ref[...]
    pre_act = dot_nn(second, up) + up_bias_ref[...]
    hidden_grad = dot_nt(dz, down)
    cumulative = 0.5 + 0.5 * lax.erf(pre_act * (0.5 ** 0.5))
    density = jnp.exp(-0.5 * pre_act * pre_act) * 0.3989422804014327
    hidden = (pre_act * cumulative).astype(LOW)
    pre_grad = hidden_grad * (cumulative + pre_act * density)
    pre_grad_low = pre_grad.astype(LOW)
    up_bias_grad_ref[...] = jnp.sum(pre_grad_low.astype(F32), axis=0, keepdims=True)
    out_part = dot_nn(hidden, down)
    second_part = dot_nt(pre_grad_low, up)
    down_grad_ref[...] = dot_tn(hidden, dz).astype(LOW)
    up_grad_ref[...] = dot_tn(second, pre_grad_low).astype(LOW)

    @pl.when(step == 0)
    def _():
        out_ref[...] = out_part
        second_grad_ref[...] = second_part

    @pl.when(step > 0)
    def _():
        out_ref[...] += out_part
        second_grad_ref[...] += second_part


def mlp_both(second, dz, up, up_bias, down, block=512):
    rows, dim = second.shape
    width = up.shape[1]
    whole = pl.BlockSpec((rows, dim), lambda j: (0, 0))
    return pl.pallas_call(
        mlp_kernel,
        grid=(width // block,),
        in_specs=[
            whole,
            whole,
            pl.BlockSpec((dim, block), lambda j: (0, j)),
            pl.BlockSpec((1, block), lambda j: (0, j)),
            pl.BlockSpec((block, dim), lambda j: (j, 0)),
        ],
        out_specs=[
            whole,
            whole,
            pl.BlockSpec((block, dim), lambda j: (j, 0)),
            pl.BlockSpec((dim, block), lambda j: (0, j)),
            pl.BlockSpec((1, block), lambda j: (0, j)),
        ],
        out_shape=[
            jax.ShapeDtypeStruct((rows, dim), F32),
            jax.ShapeDtypeStruct((rows, dim), F32),
            jax.ShapeDtypeStruct((width, dim), LOW),
            jax.ShapeDtypeStruct((dim, width), LOW),
            jax.ShapeDtypeStruct((1, width), F32),
        ],
        compiler_params=pltpu.CompilerParams(vmem_limit_bytes=VMEM),
        cost_estimate=pl.CostEstimate(
            flops=12 * rows * dim * width, bytes_accessed=16 * dim * width, transcendentals=3 * rows * width
        ),
        name="mlp_both",
    )(second, dz, up, up_bias, down)


def exchange_rows(blocks):
    here = lax.axis_index("seq")
    own = lax.dynamic_index_in_dim(blocks, here, 0, keepdims=False)
    away = lax.dynamic_index_in_dim(blocks, 1 - here, 0, keepdims=False)
    return own, lax.ppermute(away, "seq", [(0, 1), (1, 0)])


def return_rows(rows):
    here = lax.axis_index("seq")
    half = rows.shape[0] // 2
    own = rows[:half]
    back = lax.ppermute(rows[half:].astype(LOW), "seq", [(0, 1), (1, 0)]).astype(F32)
    return jnp.where(here == 0, jnp.stack([own, back]), jnp.stack([back, own]))


def gather(block):
    return lax.all_gather(block, "img", axis=0, tiled=True)


def reduce(total):
    part = lax.psum_scatter(total, "img", scatter_dimension=0, tiled=True)
    return part.astype(F32) + lax.ppermute(part, "seq", [(0, 1), (1, 0)]).astype(F32)


def norm_parts(values):
    offset = values - jnp.mean(values, axis=-1, keepdims=True)
    inverse = lax.rsqrt(jnp.mean(offset * offset, axis=-1, keepdims=True) + epsilon)
    return offset * inverse, inverse


def norm_back(unit, inverse, gain, grad):
    scaled = grad * gain
    across = jnp.mean(scaled, axis=-1, keepdims=True)
    along = jnp.mean(scaled * unit, axis=-1, keepdims=True)
    return inverse * (scaled - across - unit * along), jnp.sum(grad * unit, axis=0), jnp.sum(grad, axis=0)


SMALL_PAD = 256


def image_body(
    tokens, token_mask, ln1_gain, ln1_bias, w_qkv, bias_q, bias_v, w_out, bias_out,
    ln2_gain, ln2_bias, w_up, bias_up, w_down, bias_down, cotangent,
):
    shard_rows, dim = tokens.shape[1:]
    owners = lax.axis_size("img")
    shard = dim // owners
    width = bias_up.shape[0] * owners
    smalls = (ln1_gain, ln1_bias, bias_q, bias_v, bias_out, ln2_gain, ln2_bias, bias_down, bias_up)
    sizes = [s.shape[0] for s in smalls]
    columns = sum(sizes) // shard

    packed = jnp.concatenate(smalls).reshape(shard, columns)
    first = gather(jnp.concatenate([w_qkv, jnp.pad(packed, ((0, 0), (0, 128 - columns)))], axis=1))
    qkv_full = first[:, : 3 * dim]
    small_full = first[:, 3 * dim : 3 * dim + columns].reshape(owners, shard * columns).astype(F32)
    cuts = [sum(sizes[:i]) for i in range(len(sizes) + 1)]
    (gain_one, shift_one, query_bias, value_bias, out_bias, gain_two, shift_two, down_bias, up_bias) = [
        small_full[:, a:b].reshape(-1) for a, b in zip(cuts[:-1], cuts[1:])
    ]
    second_gather = gather(jnp.concatenate([w_out, w_up], axis=1))
    out_full, up_full = second_gather[:, :dim], second_gather[:, dim:]
    down_full = gather(w_down)

    mask_rows = jnp.broadcast_to(
        jnp.pad(token_mask.astype(LOW), ((0, 0), (0, dim - shard_rows)))[:, None, :], (2, 16, dim)
    )
    own, away = exchange_rows(jnp.concatenate([tokens, mask_rows], axis=1))
    both = jnp.stack([own, away])
    inputs = both[:, :shard_rows].reshape(2 * shard_rows, dim).astype(F32)
    mask_column = both[:, shard_rows, :shard_rows].astype(F32).reshape(2 * shard_rows, 1)
    masked = jnp.where(token_mask[..., None] > 0, cotangent, jnp.zeros_like(cotangent))
    down_in = jnp.concatenate(exchange_rows(masked), axis=0)

    unit_one, inverse_one = norm_parts(inputs)
    normed = (unit_one * gain_one + shift_one).astype(LOW)
    qkv_bias = jnp.concatenate([query_bias, jnp.zeros_like(query_bias), value_bias])
    qkv = (dot_nn(normed, qkv_full) + qkv_bias).astype(LOW)
    merged, logs = attention_forward(qkv, mask_column)
    middle = inputs + dot_nn(merged, out_full) + out_bias
    unit_two, inverse_two = norm_parts(middle)
    second = (unit_two * gain_two + shift_two).astype(LOW)
    mlp_out, second_grad, grad_down, grad_up, grad_up_bias = mlp_both(
        second, down_in, up_full, up_bias.reshape(1, width), down_full
    )
    output = middle + mlp_out + down_bias
    upstream = down_in.astype(F32)
    grad_down_bias = jnp.sum(upstream, axis=0)
    middle_ln, grad_gain_two, grad_shift_two = norm_back(unit_two, inverse_two, gain_two, second_grad)
    middle_grad = upstream + middle_ln
    branch_grad = middle_grad.astype(LOW)
    grad_out = dot_tn(merged, branch_grad).astype(LOW)
    grad_out_bias = jnp.sum(branch_grad.astype(F32), axis=0)
    merged_grad = dot_nt(branch_grad, out_full).astype(LOW)
    query_grad, key_grad, value_grad = attention_backward(qkv, mask_column, logs, merged_grad)
    qkv_grad = jnp.concatenate([query_grad, key_grad, value_grad], axis=1)
    grad_qkv = dot_tn(normed, qkv_grad).astype(LOW)
    grad_query_bias = jnp.sum(query_grad.astype(F32), axis=0)
    grad_value_bias = jnp.sum(value_grad.astype(F32), axis=0)
    normed_grad = dot_nt(qkv_grad, qkv_full)
    input_ln, grad_gain_one, grad_shift_one = norm_back(unit_one, inverse_one, gain_one, normed_grad)
    input_grad = middle_grad + input_ln

    small_grads = (
        grad_gain_one, grad_shift_one, grad_query_bias, grad_value_bias, grad_out_bias,
        grad_gain_two, grad_shift_two, grad_down_bias, grad_up_bias.reshape(-1),
    )
    small_packed = jnp.concatenate([g.reshape(owners, -1) for g in small_grads], axis=1)
    small_packed = jnp.pad(small_packed.reshape(dim, columns), ((0, 0), (0, SMALL_PAD - columns))).astype(LOW)
    down_sum = reduce(grad_down)
    up_sum = reduce(jnp.concatenate([grad_out, grad_up], axis=1))
    qkv_sum = reduce(jnp.concatenate([grad_qkv, small_packed], axis=1))
    small_sum = qkv_sum[:, 3 * dim : 3 * dim + columns].reshape(-1)
    (sum_gain_one, sum_shift_one, sum_query, sum_value, sum_out, sum_gain_two, sum_shift_two, sum_down, sum_up) = [
        small_sum[a:b] for a, b in zip(cuts[:-1], cuts[1:])
    ]
    return (
        return_rows(output), return_rows(input_grad), sum_gain_one, sum_shift_one, qkv_sum[:, : 3 * dim],
        sum_query, sum_value, up_sum[:, :dim], sum_out, sum_gain_two, sum_shift_two, up_sum[:, dim:],
        sum_up, down_sum, sum_down,
    )


def solution(mesh):
    in_specs = (
        P("img", "seq", None),
        P("img", "seq"),
        P("img"),
        P("img"),
        P("img", None),
        P("img"),
        P("img"),
        P("img", None),
        P("img"),
        P("img"),
        P("img"),
        P("img", None),
        P("img"),
        P("img", None),
        P("img"),
        P("img", "seq", None),
    )
    out_specs = (
        P("img", "seq", None),
        P("img", "seq", None),
        P("img"),
        P("img"),
        P("img", None),
        P("img"),
        P("img"),
        P("img", None),
        P("img"),
        P("img"),
        P("img"),
        P("img", None),
        P("img"),
        P("img", None),
        P("img"),
    )
    def body(*blocks):
        one_each = blocks[0].shape[0] == mesh.shape["seq"] == 2
        plan = image_body if one_each and mesh.shape["img"] == 16 else general_body
        return plan(*blocks)

    return jax.shard_map(body, mesh=mesh, in_specs=in_specs, out_specs=out_specs, check_vma=False)
```

```python
import functools
import jax
import jax.numpy as jnp
from jax import lax
from jax.experimental import pallas as pl
from jax.experimental.pallas import tpu as pltpu
from jax.sharding import PartitionSpec as P

HEADS = 12
epsilon = 1e-06


def layer_norm(values, gain, shift):
    center = jnp.mean(values, axis=-1, keepdims=True)
    offset = values - center
    spread = jnp.mean(offset * offset, axis=-1, keepdims=True)
    return offset * lax.rsqrt(spread + epsilon) * gain + shift


def gelu_exact(pre_value):
    return jax.nn.gelu(pre_value, approximate=False)


def split_heads(tensor, head_count):
    images, row_count, columns = tensor.shape
    head_size = columns // head_count
    moved = tensor.reshape(images, row_count, head_count, head_size).transpose(0, 2, 1, 3)
    return moved.reshape(images * head_count, row_count, head_size)


def join_heads(tensor, images):
    combined, row_count, head_size = tensor.shape
    heads_here = combined // images
    moved = tensor.reshape(images, heads_here, row_count, head_size).transpose(0, 2, 1, 3)
    return moved.reshape(images, row_count, heads_here * head_size)


def attend_forward(query_head, key_head, value_head, key_mask):
    scaling = query_head.shape[-1] ** (-0.5)
    row_count = query_head.shape[0]
    blocks = max(1, 2 * row_count // key_head.shape[0])

    def one_block(query_block):
        scores = (
            jnp.einsum("qd,kd->qk", query_block, key_head, preferred_element_type=jnp.float32)
            * scaling
        )
        scores = jnp.where(key_mask[None, :] > 0.5, scores, -1000000000.0)
        highest = jnp.max(scores, axis=-1, keepdims=True)
        weights = jnp.exp(scores - highest)
        totals = jnp.sum(weights, axis=-1, keepdims=True)
        mixed = jnp.dot(
            (weights / totals).astype(jnp.bfloat16), value_head, preferred_element_type=jnp.float32
        )
        return (mixed, (highest + jnp.log(totals))[:, 0])

    mixed, log_sums = lax.map(one_block, query_head.reshape(blocks, row_count // blocks, -1))
    return (mixed.reshape(row_count, -1), log_sums.reshape(row_count))


def attend_backward(query_head, key_head, value_head, key_mask, log_sums, out_grad):
    scaling = query_head.shape[-1] ** (-0.5)
    row_count = query_head.shape[0]
    blocks = max(1, 2 * row_count // key_head.shape[0])
    block_rows = row_count // blocks

    def one_block(carry, pieces):
        key_grad, value_grad = carry
        query_block, log_block, grad_block = pieces
        scores = (
            jnp.einsum("qd,kd->qk", query_block, key_head, preferred_element_type=jnp.float32)
            * scaling
        )
        scores = jnp.where(key_mask[None, :] > 0.5, scores, -1000000000.0)
        weights = jnp.exp(scores - log_block[:, None])
        value_grad = value_grad + jnp.einsum(
            "qk,qd->kd",
            weights.astype(jnp.bfloat16),
            grad_block,
            preferred_element_type=jnp.float32,
        )
        weight_grad = jnp.einsum(
            "qd,kd->qk", grad_block, value_head, preferred_element_type=jnp.float32
        )
        centered = jnp.sum(weights * weight_grad, axis=-1, keepdims=True)
        score_grad = (weights * (weight_grad - centered)).astype(jnp.bfloat16)
        query_grad = jnp.dot(score_grad, key_head, preferred_element_type=jnp.float32) * scaling
        key_grad = (
            key_grad
            + jnp.einsum("qk,qd->kd", score_grad, query_block, preferred_element_type=jnp.float32)
            * scaling
        )
        return ((key_grad, value_grad), query_grad)

    zeros_init = jnp.zeros(key_head.shape, jnp.float32)
    (key_grad, value_grad), query_grad = lax.scan(
        one_block,
        (zeros_init, zeros_init),
        (
            query_head.reshape(blocks, block_rows, -1),
            log_sums.reshape(blocks, block_rows),
            out_grad.reshape(blocks, block_rows, -1),
        ),
    )
    return (query_grad.reshape(row_count, -1), key_grad, value_grad)


def heads_forward(query_heads, key_heads, value_heads, key_masks):
    return lax.map(
        lambda pieces: attend_forward(pieces[0], pieces[1], pieces[2], pieces[3]),
        (query_heads, key_heads, value_heads, key_masks),
    )


def heads_backward(query_heads, key_heads, value_heads, key_masks, log_sums, out_grads):
    return lax.map(
        lambda pieces: attend_backward(
            pieces[0], pieces[1], pieces[2], pieces[3], pieces[4], pieces[5]
        ),
        (query_heads, key_heads, value_heads, key_masks, log_sums, out_grads),
    )


def column_sum(tensor):
    return jnp.sum(tensor.astype(jnp.float32), axis=(0, 1))


def general_body(
    tokens,
    token_mask,
    ln1_gain,
    ln1_bias,
    w_qkv,
    bias_q,
    bias_v,
    w_out,
    bias_out,
    ln2_gain,
    ln2_bias,
    w_up,
    bias_up,
    w_down,
    bias_down,
    cotangent,
):
    (
        gain_one,
        shift_one,
        qkv_full,
        query_bias,
        value_bias,
        out_full,
        out_bias,
        gain_two,
        shift_two,
        up_full,
        up_bias,
        down_full,
        down_bias,
    ) = (
        lax.all_gather(ln1_gain, "img", axis=0, tiled=True),
        lax.all_gather(ln1_bias, "img", axis=0, tiled=True),
        lax.all_gather(w_qkv, "img", axis=0, tiled=True),
        lax.all_gather(bias_q, "img", axis=0, tiled=True),
        lax.all_gather(bias_v, "img", axis=0, tiled=True),
        lax.all_gather(w_out, "img", axis=0, tiled=True),
        lax.all_gather(bias_out, "img", axis=0, tiled=True),
        lax.all_gather(ln2_gain, "img", axis=0, tiled=True),
        lax.all_gather(ln2_bias, "img", axis=0, tiled=True),
        lax.all_gather(w_up, "img", axis=0, tiled=True),
        lax.all_gather(bias_up, "img", axis=0, tiled=True),
        lax.all_gather(w_down, "img", axis=0, tiled=True),
        lax.all_gather(bias_down, "img", axis=0, tiled=True),
    )
    images, shard_rows, model_dim = tokens.shape
    seq_parts = lax.axis_size("seq")
    inputs = tokens.astype(jnp.float32)
    mask_float = token_mask.astype(jnp.float32)
    normed, norm_one_pull = jax.vjp(
        layer_norm, inputs, gain_one.astype(jnp.float32), shift_one.astype(jnp.float32)
    )
    normed_low = normed.astype(jnp.bfloat16)
    projected = jnp.einsum("bsd,de->bse", normed_low, qkv_full, preferred_element_type=jnp.float32)
    query_tok = (projected[..., :model_dim] + query_bias.astype(jnp.float32)).astype(jnp.bfloat16)
    key_tok = projected[..., model_dim : 2 * model_dim].astype(jnp.bfloat16)
    value_tok = (projected[..., 2 * model_dim :] + value_bias.astype(jnp.float32)).astype(
        jnp.bfloat16
    )
    mask_low = token_mask.astype(jnp.bfloat16)
    local_heads = HEADS // seq_parts
    stacked = jnp.stack([query_tok, key_tok, value_tok], axis=2)
    mask_tile = jnp.broadcast_to(mask_low[:, :, None, None], (images, shard_rows, 1, seq_parts))
    stacked_heads, mask_heads = (
        lax.all_to_all(stacked, "seq", split_axis=3, concat_axis=1, tiled=True),
        lax.all_to_all(mask_tile, "seq", split_axis=3, concat_axis=1, tiled=True),
    )
    query_heads = split_heads(stacked_heads[:, :, 0], local_heads)
    key_heads = split_heads(stacked_heads[:, :, 1], local_heads)
    value_heads = split_heads(stacked_heads[:, :, 2], local_heads)
    key_masks = jnp.repeat(mask_heads[:, :, 0, 0].astype(jnp.float32), local_heads, axis=0)
    attended, log_sums = heads_forward(query_heads, key_heads, value_heads, key_masks)
    merged_heads = join_heads(attended, images).astype(jnp.bfloat16)
    merged = lax.all_to_all(merged_heads, "seq", split_axis=1, concat_axis=2, tiled=True)
    branch = jnp.einsum(
        "bsd,de->bse", merged, out_full, preferred_element_type=jnp.float32
    ) + out_bias.astype(jnp.float32)
    middle = inputs + branch
    second, norm_two_pull = jax.vjp(
        layer_norm, middle, gain_two.astype(jnp.float32), shift_two.astype(jnp.float32)
    )
    second_low = second.astype(jnp.bfloat16)
    pre_act = jnp.einsum(
        "bsd,df->bsf", second_low, up_full, preferred_element_type=jnp.float32
    ) + up_bias.astype(jnp.float32)
    hidden, gelu_pull = jax.vjp(gelu_exact, pre_act)
    hidden_low = hidden.astype(jnp.bfloat16)
    output = (
        middle
        + jnp.einsum("bsf,fd->bsd", hidden_low, down_full, preferred_element_type=jnp.float32)
        + down_bias.astype(jnp.float32)
    )
    upstream = cotangent.astype(jnp.float32) * mask_float[..., None]
    down_in = upstream.astype(jnp.bfloat16)
    grad_down = jnp.einsum("bsf,bsd->fd", hidden_low, down_in, preferred_element_type=jnp.float32)
    grad_down_bias = column_sum(down_in)
    hidden_grad = jnp.einsum("bsd,fd->bsf", down_in, down_full, preferred_element_type=jnp.float32)
    pre_grad = gelu_pull(hidden_grad)[0].astype(jnp.bfloat16)
    grad_up = jnp.einsum("bsd,bsf->df", second_low, pre_grad, preferred_element_type=jnp.float32)
    grad_up_bias = column_sum(pre_grad)
    second_grad = jnp.einsum("bsf,df->bsd", pre_grad, up_full, preferred_element_type=jnp.float32)
    middle_ln_grad, grad_gain_two, grad_shift_two = norm_two_pull(second_grad)
    middle_grad = upstream + middle_ln_grad
    branch_grad = middle_grad.astype(jnp.bfloat16)
    grad_out = jnp.einsum("bsd,bse->de", merged, branch_grad, preferred_element_type=jnp.float32)
    grad_out_bias = column_sum(branch_grad)
    merged_grad = jnp.einsum(
        "bse,de->bsd", branch_grad, out_full, preferred_element_type=jnp.float32
    ).astype(jnp.bfloat16)
    grad_heads_in = lax.all_to_all(merged_grad, "seq", split_axis=2, concat_axis=1, tiled=True)
    query_grad, key_grad, value_grad = heads_backward(
        query_heads,
        key_heads,
        value_heads,
        key_masks,
        log_sums,
        split_heads(grad_heads_in, local_heads),
    )
    triple = jnp.stack(
        [
            join_heads(query_grad, images),
            join_heads(key_grad, images),
            join_heads(value_grad, images),
        ],
        axis=2,
    ).astype(jnp.bfloat16)
    qkv_grad = lax.all_to_all(triple, "seq", split_axis=1, concat_axis=3, tiled=True)
    qkv_flat = qkv_grad.reshape(images, shard_rows, 3 * model_dim)
    grad_qkv = jnp.einsum("bsd,bse->de", normed_low, qkv_flat, preferred_element_type=jnp.float32)
    grad_query_bias = column_sum(qkv_grad[:, :, 0])
    grad_value_bias = column_sum(qkv_grad[:, :, 2])
    normed_grad = jnp.einsum("bse,de->bsd", qkv_flat, qkv_full, preferred_element_type=jnp.float32)
    input_ln_grad, grad_gain_one, grad_shift_one = norm_one_pull(normed_grad)
    input_grad = middle_grad + input_ln_grad
    shards_all = (
        lax.psum_scatter(grad_gain_one, "img", scatter_dimension=0, tiled=True),
        lax.psum_scatter(grad_shift_one, "img", scatter_dimension=0, tiled=True),
        lax.psum_scatter(grad_qkv, "img", scatter_dimension=0, tiled=True),
        lax.psum_scatter(grad_query_bias, "img", scatter_dimension=0, tiled=True),
        lax.psum_scatter(grad_value_bias, "img", scatter_dimension=0, tiled=True),
        lax.psum_scatter(grad_out, "img", scatter_dimension=0, tiled=True),
        lax.psum_scatter(grad_out_bias, "img", scatter_dimension=0, tiled=True),
        lax.psum_scatter(grad_gain_two, "img", scatter_dimension=0, tiled=True),
        lax.psum_scatter(grad_shift_two, "img", scatter_dimension=0, tiled=True),
        lax.psum_scatter(grad_up, "img", scatter_dimension=0, tiled=True),
        lax.psum_scatter(grad_up_bias, "img", scatter_dimension=0, tiled=True),
        lax.psum_scatter(grad_down, "img", scatter_dimension=0, tiled=True),
        lax.psum_scatter(grad_down_bias, "img", scatter_dimension=0, tiled=True),
    )
    summed_all = lax.psum(
        (
            shards_all[0],
            shards_all[1],
            shards_all[2],
            shards_all[3],
            shards_all[4],
            shards_all[5],
            shards_all[6],
            shards_all[7],
            shards_all[8],
            shards_all[9],
            shards_all[10],
            shards_all[11],
            shards_all[12],
        ),
        "seq",
    )
    return (
        output,
        input_grad,
        summed_all[0],
        summed_all[1],
        summed_all[2],
        summed_all[3],
        summed_all[4],
        summed_all[5],
        summed_all[6],
        summed_all[7],
        summed_all[8],
        summed_all[9],
        summed_all[10],
        summed_all[11],
        summed_all[12],
    )


LOW = jnp.bfloat16
F32 = jnp.float32
VMEM = 56 * 1024 * 1024
SMALL_PAD = 256


def cost(microseconds):
    return pl.CostEstimate(flops=int(microseconds * 1.15e9), bytes_accessed=1, transcendentals=0)


def dot_nt(left, right):
    return lax.dot_general(left, right, (((1,), (1,)), ((), ())), preferred_element_type=F32)


def dot_nn(left, right):
    return lax.dot_general(left, right, (((1,), (0,)), ((), ())), preferred_element_type=F32)


def dot_tn(left, right):
    return lax.dot_general(left, right, (((0,), (0,)), ((), ())), preferred_element_type=F32)


def attention_forward_kernel(scale, size, query_ref, key_ref, value_ref, mask_ref, out_ref, log_ref):
    real = mask_ref[...] > 0.5
    query = query_ref[...] * jnp.asarray(scale, LOW)
    key = jnp.where(real, key_ref[...], key_ref[0:1, :])
    value = value_ref[...]
    lane = lax.broadcasted_iota(jnp.int32, key.shape, 1)
    pieces = []
    for head in range(2):
        mine = (lane // size) == head
        scores = dot_nt(jnp.where(mine, key, jnp.zeros_like(key)), query)
        highest = jnp.max(scores, axis=0, keepdims=True)
        weights = jnp.exp(scores - highest).astype(LOW)
        extended = jnp.where(real, jnp.where(mine, value, jnp.ones_like(value)), jnp.zeros_like(value))
        mixed = dot_tn(extended, weights)
        own, other = head * size, (1 - head) * size
        totals = mixed[other : other + size, :]
        pieces.append(mixed[own : own + size, :] / totals)
        log_ref[0, head : head + 1, :] = highest + jnp.log(totals[0:1, :])
    out_ref[...] = jnp.concatenate(pieces, axis=0).T.astype(LOW)


def attention_forward(qkv, mask_column):
    rows, width = qkv.shape
    dim = width // 3
    size = dim // HEADS
    pairs = HEADS // 2
    block = (rows, 2 * size)
    return pl.pallas_call(
        functools.partial(attention_forward_kernel, size ** (-0.5), size),
        grid=(pairs,),
        in_specs=[
            pl.BlockSpec(block, lambda p: (0, p)),
            pl.BlockSpec(block, lambda p: (0, pairs + p)),
            pl.BlockSpec(block, lambda p: (0, 2 * pairs + p)),
            pl.BlockSpec((rows, 1), lambda p: (0, 0)),
        ],
        out_specs=[
            pl.BlockSpec(block, lambda p: (0, p)),
            pl.BlockSpec((1, 2, rows), lambda p: (p, 0, 0)),
        ],
        out_shape=[
            jax.ShapeDtypeStruct((rows, dim), LOW),
            jax.ShapeDtypeStruct((pairs, 2, rows), F32),
        ],
        compiler_params=pltpu.CompilerParams(vmem_limit_bytes=VMEM),
        cost_estimate=cost(13),
        name="attention_forward",
    )(qkv, qkv, qkv, mask_column)


def attention_backward_kernel(
    scale, size, query_ref, key_ref, value_ref, mask_ref, log_ref, grad_ref, dq_ref, dk_ref, dv_ref
):
    real = mask_ref[...] > 0.5
    query = query_ref[...] * jnp.asarray(scale, LOW)
    zeros = jnp.zeros_like(query)
    key_kept = jnp.where(real, key_ref[...], zeros)
    key = jnp.where(real, key_kept, key_ref[0:1, :])
    value = jnp.where(real, value_ref[...], zeros)
    grad = grad_ref[...]
    lane = lax.broadcasted_iota(jnp.int32, key.shape, 1)
    totals = None
    for head in range(2):
        mine = (lane // size) == head
        scores = dot_nt(jnp.where(mine, key, zeros), query)
        weights = jnp.exp(scores - log_ref[0, head : head + 1, :])
        grad_here = jnp.where(mine, grad, zeros)
        value_grad = dot_nn(weights.astype(LOW), grad_here)
        weight_grad = dot_nt(value, grad_here)
        centered = jnp.sum(weights * weight_grad, axis=0, keepdims=True)
        score_grad = (weights * (weight_grad - centered)).astype(LOW)
        key_grad = dot_nn(score_grad, jnp.where(mine, query, zeros))
        query_grad = dot_tn(jnp.where(mine, key_kept, zeros), score_grad)
        if totals is None:
            totals = (query_grad, key_grad, value_grad)
        else:
            totals = tuple(a + b for a, b in zip(totals, (query_grad, key_grad, value_grad)))
    query_grad, key_grad, value_grad = totals
    dq_ref[...] = (query_grad * scale).T.astype(LOW)
    dk_ref[...] = jnp.where(real, key_grad, 0.0).astype(LOW)
    dv_ref[...] = jnp.where(real, value_grad, 0.0).astype(LOW)


def attention_backward(qkv, mask_column, logs, grad, first, count):
    rows, width = qkv.shape
    dim = width // 3
    size = dim // HEADS
    pairs = HEADS // 2
    block = (rows, 2 * size)
    spec = pl.BlockSpec(block, lambda p: (0, first + p))
    out_spec = pl.BlockSpec(block, lambda p: (0, p))
    return pl.pallas_call(
        functools.partial(attention_backward_kernel, size ** (-0.5), size),
        grid=(count,),
        in_specs=[
            spec,
            pl.BlockSpec(block, lambda p: (0, pairs + first + p)),
            pl.BlockSpec(block, lambda p: (0, 2 * pairs + first + p)),
            pl.BlockSpec((rows, 1), lambda p: (0, 0)),
            pl.BlockSpec((1, 2, rows), lambda p: (first + p, 0, 0)),
            spec,
        ],
        out_specs=[out_spec] * 3,
        out_shape=[jax.ShapeDtypeStruct((rows, 2 * size * count), LOW)] * 3,
        compiler_params=pltpu.CompilerParams(vmem_limit_bytes=VMEM),
        cost_estimate=cost(1),
        name="attention_backward",
    )(qkv, qkv, qkv, mask_column, logs, grad)


def split_cores(total_ref, kept_ref, sent_ref, first, columns):
    core = lax.axis_index("img") % 2
    shard = kept_ref.shape[2]
    for pair in range(total_ref.shape[0] // (2 * shard)):
        z, x = first + pair // 2, pair % 2
        kept_ref[z, x, :, columns] = total_ref[pl.ds(pl.multiple_of((2 * pair + core) * shard, 16), shard), :]
        sent_ref[z, x, :, columns] = total_ref[pl.ds(pl.multiple_of((2 * pair + 1 - core) * shard, 16), shard), :]


def mlp_first_kernel(
    shape, second_ref, dz_ref, up_ref, up_bias_ref, down_ref,
    out_ref, kept_ref, sent_ref, pre_grad_ref, up_bias_grad_ref, down_grad_ref,
):
    step = pl.program_id(0)
    owners, pieces, dim = shape
    dz = dz_ref[...]
    down = jnp.concatenate(
        [down_ref[o, :, i * dim : (i + 1) * dim] for o in range(owners) for i in range(pieces)], axis=0
    )
    pre_act = dot_nn(second_ref[...], up_ref[...]) + up_bias_ref[...]
    hidden_grad = dot_nt(dz, down)
    cumulative = 0.5 + 0.5 * lax.erf(pre_act * (0.5 ** 0.5))
    density = jnp.exp(-0.5 * pre_act * pre_act) * 0.3989422804014327
    hidden = (pre_act * cumulative).astype(LOW)
    pre_grad = (hidden_grad * (cumulative + pre_act * density)).astype(LOW)
    pre_grad_ref[...] = pre_grad
    up_bias_grad_ref[...] = jnp.sum(pre_grad.astype(F32), axis=0, keepdims=True)
    out_part = dot_nn(hidden, down)
    down_grad_ref[...] = dot_tn(hidden, dz).astype(LOW)
    split_cores(down_grad_ref, kept_ref, sent_ref, 0, slice(None))

    @pl.when(step == 0)
    def _():
        out_ref[...] = out_part

    @pl.when(step > 0)
    def _():
        out_ref[...] += out_part


def mlp_first(second, dz, up_down, up_bias, owners):
    rows, dim = second.shape
    width = up_bias.shape[1]
    shard = dim // owners
    pieces = width // dim
    some = owners // pieces
    whole = pl.BlockSpec((rows, dim), lambda j: (0, 0))
    return pl.pallas_call(
        functools.partial(mlp_first_kernel, (some, pieces, dim)),
        grid=(pieces,),
        in_specs=[
            whole,
            whole,
            pl.BlockSpec((dim, dim), lambda j: (0, j)),
            pl.BlockSpec((1, dim), lambda j: (0, j)),
            pl.BlockSpec((some, shard, width), lambda j: (j, 0, 1)),
        ],
        out_specs=[
            whole,
            pl.BlockSpec((1, 2, width // owners, dim), lambda j: (j, 0, 0, 0)),
            pl.BlockSpec((1, 2, width // owners, dim), lambda j: (j, 0, 0, 0)),
            pl.BlockSpec((rows, dim), lambda j: (0, j)),
            pl.BlockSpec((1, dim), lambda j: (0, j)),
        ],
        out_shape=[
            jax.ShapeDtypeStruct((rows, dim), F32),
            jax.ShapeDtypeStruct((4, 2, width // owners, dim), LOW),
            jax.ShapeDtypeStruct((4, 2, width // owners, dim), LOW),
            jax.ShapeDtypeStruct((rows, width), LOW),
            jax.ShapeDtypeStruct((1, width), F32),
        ],
        scratch_shapes=[pltpu.VMEM((dim, dim), LOW)],
        compiler_params=pltpu.CompilerParams(vmem_limit_bytes=VMEM),
        cost_estimate=cost(19),
        name="mlp_first",
    )(second, dz, up_down, up_bias, up_down.reshape(owners, shard, 2 * width))


def mlp_second_kernel(second_ref, pre_grad_ref, up_ref, second_grad_ref, kept_ref, sent_ref, up_grad_ref):
    step = pl.program_id(0)
    pre_grad = pre_grad_ref[...]
    up_grad_ref[...] = dot_tn(second_ref[...], pre_grad).astype(LOW)
    split_cores(up_grad_ref, kept_ref, sent_ref, 0, slice(None))
    part = dot_nt(pre_grad, up_ref[...])

    @pl.when(step == 0)
    def _():
        second_grad_ref[...] = part

    @pl.when(step > 0)
    def _():
        second_grad_ref[...] += part


def mlp_second(second, pre_grad, up_down, owners):
    rows, dim = second.shape
    width = pre_grad.shape[1]
    shard = dim // owners
    whole = pl.BlockSpec((rows, dim), lambda j: (0, 0))
    split = pl.BlockSpec((4, 2, shard, dim), lambda j: (0, 0, 0, j))
    return pl.pallas_call(
        mlp_second_kernel,
        grid=(width // dim,),
        in_specs=[
            whole,
            pl.BlockSpec((rows, dim), lambda j: (0, j)),
            pl.BlockSpec((dim, dim), lambda j: (0, j)),
        ],
        out_specs=[whole, split, split],
        out_shape=[
            jax.ShapeDtypeStruct((rows, dim), F32),
            jax.ShapeDtypeStruct((4, 2, shard, width), LOW),
            jax.ShapeDtypeStruct((4, 2, shard, width), LOW),
        ],
        scratch_shapes=[pltpu.VMEM((dim, dim), LOW)],
        compiler_params=pltpu.CompilerParams(vmem_limit_bytes=VMEM),
        cost_estimate=cost(1),
        name="mlp_second",
    )(second, pre_grad, up_down)


def norm_parts(values):
    offset = values - jnp.mean(values, axis=-1, keepdims=True)
    inverse = lax.rsqrt(jnp.mean(offset * offset, axis=-1, keepdims=True) + epsilon)
    return offset * inverse, inverse


def norm_back(unit, inverse, gain, grad):
    scaled = grad * gain
    across = jnp.mean(scaled, axis=-1, keepdims=True)
    along = jnp.mean(scaled * unit, axis=-1, keepdims=True)
    return inverse * (scaled - across - unit * along)


def column_sums(values):
    return jnp.sum(values, axis=0, keepdims=True)


def middle_kernel(
    middle_ref, grad_ref, dz_ref, gain_ref, out_full_ref, merged_ref,
    middle_grad_ref, merged_grad_ref, out_grad_ref, small_ref,
):
    unit, inverse = norm_parts(middle_ref[...])
    grad = grad_ref[...]
    upstream = dz_ref[...].astype(F32)
    middle_grad = upstream + norm_back(unit, inverse, gain_ref[...], grad)
    middle_grad_ref[...] = middle_grad
    low = middle_grad.astype(LOW)
    merged_grad_ref[...] = dot_nt(low, out_full_ref[...]).astype(LOW)
    out_grad_ref[...] = dot_tn(merged_ref[...], low).astype(LOW)
    small_ref[0:1] = column_sums(low.astype(F32))
    small_ref[1:2] = column_sums(grad * unit)
    small_ref[2:3] = column_sums(grad)
    small_ref[3:4] = column_sums(upstream)


def middle_backward(middle, second_grad, dz, gain, first, merged):
    rows, dim = middle.shape
    whole = pl.BlockSpec((rows, dim), lambda j: (0, 0))
    return pl.pallas_call(
        middle_kernel,
        grid=(1,),
        in_specs=[
            whole,
            whole,
            whole,
            pl.BlockSpec((1, dim), lambda j: (0, 0)),
            pl.BlockSpec((dim, dim), lambda j: (0, 3)),
            whole,
        ],
        out_specs=[
            whole,
            whole,
            pl.BlockSpec((dim, dim), lambda j: (0, 0)),
            pl.BlockSpec((4, dim), lambda j: (0, 0)),
        ],
        out_shape=[
            jax.ShapeDtypeStruct((rows, dim), F32),
            jax.ShapeDtypeStruct((rows, dim), LOW),
            jax.ShapeDtypeStruct((dim, dim), LOW),
            jax.ShapeDtypeStruct((4, dim), F32),
        ],
        compiler_params=pltpu.CompilerParams(vmem_limit_bytes=VMEM),
        cost_estimate=cost(1),
        name="middle_backward",
    )(middle, second_grad, dz, gain, first, merged)


def last_kernel(
    inputs_ref, gain_ref, shift_ref, q_low, k_low, v_low, q_high, k_high, v_high, qkv_full_ref,
    middle_grad_ref, out_grad_ref, small_ref, up_bias_ref, input_grad_ref, kept_ref, sent_ref, total_ref,
):
    unit, inverse = norm_parts(inputs_ref[...].astype(F32))
    gain = gain_ref[...]
    normed = (unit * gain + shift_ref[...]).astype(LOW)
    grads = [ref[...] for ref in (q_low, q_high, k_low, k_high, v_low, v_high)]
    qkv_grad = jnp.concatenate(grads, axis=1)
    dim = unit.shape[1]
    normed_grad = dot_nt(qkv_grad, qkv_full_ref[...])
    input_grad_ref[...] = middle_grad_ref[...] + norm_back(unit, inverse, gain, normed_grad)
    total_ref[:, : 3 * dim] = dot_tn(normed, qkv_grad).astype(LOW)
    total_ref[:, 3 * dim : 4 * dim] = out_grad_ref[...]
    bias_of = column_sums(qkv_grad.astype(F32))
    rows = [column_sums(normed_grad * unit), column_sums(normed_grad), bias_of[:, :dim], bias_of[:, 2 * dim :]]
    rows += [small_ref[...], up_bias_ref[...]]
    taken = sum(row.shape[0] for row in rows)
    rows.append(jnp.zeros((128 - taken, dim), F32))
    total_ref[:, 4 * dim : 4 * dim + 128] = jnp.concatenate(rows, axis=0).T.astype(LOW)
    total_ref[:, 4 * dim + 128 :] = jnp.zeros((dim, SMALL_PAD - 128), LOW)
    split_cores(total_ref, kept_ref, sent_ref, 0, slice(None))


def last_backward(inputs, gain, shift, grads_low, grads_high, first, middle_grad, out_grad, small, up_bias, owners):
    rows, dim = inputs.shape
    columns = 4 * dim + SMALL_PAD

    def whole(*shape):
        return pl.BlockSpec(shape, lambda j: (0,) * len(shape))

    split = jax.ShapeDtypeStruct((4, 2, dim // owners, columns), LOW)
    return pl.pallas_call(
        last_kernel,
        grid=(1,),
        in_specs=[whole(rows, dim), whole(1, dim), whole(1, dim)]
        + [whole(*g.shape) for g in (*grads_low, *grads_high)]
        + [whole(dim, 3 * dim), whole(rows, dim), whole(dim, dim), whole(*small.shape), whole(*up_bias.shape)],
        out_specs=[whole(rows, dim), whole(*split.shape), whole(*split.shape)],
        out_shape=[jax.ShapeDtypeStruct((rows, dim), F32), split, split],
        scratch_shapes=[pltpu.VMEM((dim, columns), LOW)],
        compiler_params=pltpu.CompilerParams(vmem_limit_bytes=VMEM),
        cost_estimate=cost(1),
        name="last_backward",
    )(inputs, gain, shift, *grads_low, *grads_high, first, middle_grad, out_grad, small, up_bias)


def own_and_away(blocks):
    here = lax.axis_index("seq")
    own = lax.dynamic_index_in_dim(blocks, here, 0, keepdims=False)
    return own, lax.dynamic_index_in_dim(blocks, 1 - here, 0, keepdims=False)


def both_images(own, back):
    here = lax.axis_index("seq")
    back = back.astype(F32)
    return jnp.where(here == 0, jnp.stack([own, back]), jnp.stack([back, own]))


def gather(block):
    return lax.all_gather(block, "img", axis=0, tiled=True)


def place():
    img = lax.axis_index("img")
    return img // 4, (img // 2) % 2, img % 2, lax.axis_index("seq")


def swap(block, z=0, x=0, core=0, y=0):
    bits = z * 8 + x * 4 + core * 2 + y
    return lax.ppermute(block, ("img", "seq"), [(i, i ^ bits) for i in range(32)])


def assemble_kernel(small_at, *refs):
    refs, out_ref, small_ref = refs[:-2], refs[-2], refs[-1]
    here_z, here_x, here_core, here_y = place()
    half = out_ref.shape[2] // 2
    for index, ref in enumerate(refs):
        x, y, core = index // 4 % 2, index // 2 % 2, index % 2
        columns = pl.ds(pl.multiple_of((here_y ^ y) * half, half), half)
        for z in range(4):
            owner = (here_z ^ z) * 4 + (here_x ^ x) * 2 + (here_core ^ core)
            out_ref[owner, :, columns] = ref[z]
    small = jnp.concatenate([out_ref[i, :, small_at : small_at + 128] for i in range(16)], axis=0)
    small_ref[...] = small.astype(F32).T[:16]


def gather_links(block, rows):
    shard, columns = block.shape
    half = columns // 2
    own = lax.dynamic_slice_in_dim(block, lax.axis_index("seq") * half, half, 1)
    rows = swap(rows, y=1)
    line = jnp.stack([own] + [swap(own, z=z) for z in (1, 2, 3)])
    line, rows = tie(line, rows)
    across = swap(line, x=1)
    plane = [line, swap(line, y=1), across, swap(across, y=1)]
    refs = []
    for part in plane:
        refs += [part, swap(part, core=1)]
    whole, small = pl.pallas_call(
        functools.partial(assemble_kernel, columns - SMALL_PAD),
        out_shape=[
            jax.ShapeDtypeStruct((16, shard, columns), LOW),
            jax.ShapeDtypeStruct((16, 16 * shard), F32),
        ],
        compiler_params=pltpu.CompilerParams(vmem_limit_bytes=VMEM),
        name="assemble",
    )(*refs)
    return whole.reshape(16 * shard, columns), small, rows


def total(pieces):
    result = pieces[0].astype(F32)
    for piece in pieces[1:]:
        result = result + piece.astype(F32)
    return result.astype(LOW)


def plane_pieces(paired):
    _, x, _, y = place()
    rows, half = paired.shape[2], paired.shape[3] // 2

    def part(x_index, y_index):
        return lax.dynamic_slice(paired, (0, x_index, 0, y_index * half), (4, 1, rows, half))[:, 0]

    return [part(x, y), part(1 - x, y), part(x, 1 - y), part(1 - x, 1 - y)]


def plane_swaps(pieces):
    return [pieces[0], swap(pieces[1], x=1), swap(pieces[2], y=1), swap(pieces[3], x=1, y=1)]


def line_pieces(line):
    z = place()[0]
    return [lax.dynamic_index_in_dim(line, z ^ step, 0, keepdims=False) for step in range(4)]


def line_swaps(pieces):
    return [pieces[0]] + [swap(pieces[step], z=step) for step in (1, 2, 3)]


def join_halves(own, other):
    here = lax.axis_index("seq")
    return jnp.where(
        here == 0, jnp.concatenate([own, other], axis=1), jnp.concatenate([other, own], axis=1)
    ).astype(F32)


def tie(*values):
    return lax.optimization_barrier(values)


def image_body(
    tokens, token_mask, ln1_gain, ln1_bias, w_qkv, bias_q, bias_v, w_out, bias_out,
    ln2_gain, ln2_bias, w_up, bias_up, w_down, bias_down, cotangent,
):
    shard_rows, dim = tokens.shape[1:]
    owners = lax.axis_size("img")
    shard = dim // owners
    width = bias_up.shape[0] * owners
    pieces = width // dim

    up_down = gather(
        jnp.concatenate([w_up, w_down.reshape(pieces, shard, dim).swapaxes(0, 1).reshape(shard, width)], axis=1)
    )
    rows_small = jnp.concatenate(
        [jnp.stack([ln1_gain, ln1_bias, bias_q, bias_v, bias_out, ln2_gain, ln2_bias, bias_down])]
        + [bias_up.reshape(pieces, shard)]
    )
    count = rows_small.shape[0]
    padding = jnp.pad(rows_small.T, ((0, 0), (0, SMALL_PAD - count)))
    mask_rows = jnp.broadcast_to(
        jnp.pad(token_mask.astype(LOW), ((0, 0), (0, dim - shard_rows)))[:, None, :], (2, 16, dim)
    )
    own, away = own_and_away(jnp.concatenate([tokens, mask_rows], axis=1))
    first, small, away = gather_links(jnp.concatenate([w_qkv, w_out, padding], axis=1), away)
    masked = jnp.where(token_mask[..., None] > 0, cotangent, jnp.zeros_like(cotangent))
    own_in, away_in = own_and_away(masked)
    first, away_in = tie(first, away_in)
    down_in = jnp.concatenate([own_in, swap(away_in, y=1)], axis=0)
    qkv_full, out_full = first[:, : 3 * dim], first[:, 3 * dim : 4 * dim]
    gain_one, shift_one, query_bias, value_bias, out_bias, gain_two, shift_two, down_bias = [
        small[i : i + 1] for i in range(8)
    ]
    up_bias = small[8:count].reshape(pieces, owners, shard).swapaxes(0, 1).reshape(1, width)

    both = jnp.stack([own, away])
    inputs_low = both[:, :shard_rows].reshape(2 * shard_rows, dim)
    inputs = inputs_low.astype(F32)
    mask_column = both[:, shard_rows, :shard_rows].astype(F32).reshape(2 * shard_rows, 1)
    unit_one, _ = norm_parts(inputs)
    normed = (unit_one * gain_one + shift_one).astype(LOW)
    qkv_bias = jnp.concatenate([query_bias, jnp.zeros_like(query_bias), value_bias], axis=1)
    qkv = (dot_nn(normed, qkv_full) + qkv_bias).astype(LOW)
    merged, logs = attention_forward(qkv, mask_column)
    middle = inputs + dot_nn(merged, out_full) + out_bias
    unit_two, _ = norm_parts(middle)
    second = (unit_two * gain_two + shift_two).astype(LOW)
    mlp_out, down_kept, down_sent, pre_grad, grad_up_bias = mlp_first(second, down_in, up_down, up_bias, owners)
    output = middle + mlp_out + down_bias
    output_own, output_away = output[:shard_rows], output[shard_rows:].astype(LOW)
    pre_grad, output_away, down_sent = tie(pre_grad, output_away, down_sent)
    output_back, down_sent = swap(output_away, y=1), swap(down_sent, core=1)
    second_grad, up_kept, up_sent = mlp_second(second, pre_grad, up_down, owners)
    second_grad, up_kept, up_sent, output_back, down_sent = tie(second_grad, up_kept, up_sent, output_back, down_sent)
    down_pieces = plane_pieces(total([down_kept, down_sent]))
    second_grad, up_sent, *down_pieces = tie(second_grad, up_sent, *down_pieces)
    down_pieces, up_sent = plane_swaps(down_pieces), swap(up_sent, core=1)
    middle_grad, merged_grad, grad_out, small_grads = middle_backward(
        middle, second_grad, down_in, gain_two, first, merged
    )
    middle_grad, merged_grad, grad_out, small_grads, up_sent = tie(
        middle_grad, merged_grad, grad_out, small_grads, up_sent
    )
    up_pieces = plane_pieces(total([up_kept, up_sent]))
    merged_grad, *up_pieces = tie(merged_grad, *up_pieces)
    up_pieces = plane_swaps(up_pieces)
    pairs = HEADS // 2
    grads_low = attention_backward(qkv, mask_column, logs, merged_grad, 0, pairs // 2)
    tied = tie(merged_grad, *grads_low, *down_pieces)
    merged_grad, grads_low, down_pieces = tied[0], tied[1:4], tied[4:]
    down_pieces = line_pieces(total(down_pieces))
    merged_grad, *down_pieces = tie(merged_grad, *down_pieces)
    down_pieces = line_swaps(down_pieces)
    grads_high = attention_backward(qkv, mask_column, logs, merged_grad, pairs // 2, pairs - pairs // 2)
    tied = tie(*grads_high, *down_pieces)
    grads_high, down_own = tied[:3], total(tied[3:])
    up_bias_rows = grad_up_bias.reshape(owners, pieces, shard).swapaxes(0, 1).reshape(pieces, dim)
    up_bias_rows, down_own = tie(up_bias_rows, down_own)
    down_other = swap(down_own, y=1)
    input_grad, last_kept, last_sent = last_backward(
        inputs_low, gain_one, shift_one, grads_low, grads_high, first, middle_grad, grad_out, small_grads,
        up_bias_rows, owners,
    )
    tied = tie(input_grad, last_kept, last_sent, down_other, *up_pieces)
    input_grad, last_kept, last_sent, down_other = tied[:4]
    up_pieces = line_pieces(total(tied[4:]))
    last_sent = swap(last_sent, core=1)
    last_pieces = plane_pieces(total([last_kept, last_sent]))
    tied = tie(*last_pieces, *up_pieces)
    last_pieces, up_pieces = plane_swaps(tied[:4]), line_swaps(tied[4:])
    tied = tie(input_grad, *last_pieces, *up_pieces)
    input_grad, last_pieces, up_own = tied[0], line_pieces(total(tied[1:5])), total(tied[5:])
    input_away = input_grad[shard_rows:].astype(LOW)
    tied = tie(input_away, up_own, *last_pieces)
    input_away, up_own, last_pieces = tied[0], tied[1], tied[2:]
    last_pieces = line_swaps(last_pieces)
    input_back, up_other = swap(input_away, y=1), swap(up_own, y=1)
    last_own = total(last_pieces)
    last_sum = join_halves(last_own, swap(last_own, y=1))
    smalls = last_sum[:, 4 * dim : 4 * dim + count].T
    return (
        both_images(output_own, output_back), both_images(input_grad[:shard_rows], input_back),
        smalls[0], smalls[1], last_sum[:, : 3 * dim], smalls[2], smalls[3], last_sum[:, 3 * dim : 4 * dim],
        smalls[4], smalls[5], smalls[6], join_halves(up_own, up_other), smalls[8:].reshape(-1),
        join_halves(down_own, down_other), smalls[7],
    )


def solution(mesh):
    in_specs = (
        P("img", "seq", None),
        P("img", "seq"),
        P("img"),
        P("img"),
        P("img", None),
        P("img"),
        P("img"),
        P("img", None),
        P("img"),
        P("img"),
        P("img"),
        P("img", None),
        P("img"),
        P("img", None),
        P("img"),
        P("img", "seq", None),
    )
    out_specs = (
        P("img", "seq", None),
        P("img", "seq", None),
        P("img"),
        P("img"),
        P("img", None),
        P("img"),
        P("img"),
        P("img", None),
        P("img"),
        P("img"),
        P("img"),
        P("img", None),
        P("img"),
        P("img", None),
        P("img"),
    )
    def body(*blocks):
        one_each = blocks[0].shape[0] == mesh.shape["seq"] == 2
        plan = image_body if one_each and mesh.shape["img"] == 16 else general_body
        return plan(*blocks)

    return jax.shard_map(body, mesh=mesh, in_specs=in_specs, out_specs=out_specs, check_vma=False)
```

```python
import functools
import jax
import jax.numpy as jnp
from jax import lax
from jax.experimental import pallas as pl
from jax.experimental.pallas import tpu as pltpu
from jax.sharding import PartitionSpec as P

HEADS = 12
epsilon = 1e-06


def layer_norm(values, gain, shift):
    center = jnp.mean(values, axis=-1, keepdims=True)
    offset = values - center
    spread = jnp.mean(offset * offset, axis=-1, keepdims=True)
    return offset * lax.rsqrt(spread + epsilon) * gain + shift


def gelu_exact(pre_value):
    return jax.nn.gelu(pre_value, approximate=False)


def split_heads(tensor, head_count):
    images, row_count, columns = tensor.shape
    head_size = columns // head_count
    moved = tensor.reshape(images, row_count, head_count, head_size).transpose(0, 2, 1, 3)
    return moved.reshape(images * head_count, row_count, head_size)


def join_heads(tensor, images):
    combined, row_count, head_size = tensor.shape
    heads_here = combined // images
    moved = tensor.reshape(images, heads_here, row_count, head_size).transpose(0, 2, 1, 3)
    return moved.reshape(images, row_count, heads_here * head_size)


def attend_forward(query_head, key_head, value_head, key_mask):
    scaling = query_head.shape[-1] ** (-0.5)
    row_count = query_head.shape[0]
    blocks = max(1, 2 * row_count // key_head.shape[0])

    def one_block(query_block):
        scores = (
            jnp.einsum("qd,kd->qk", query_block, key_head, preferred_element_type=jnp.float32)
            * scaling
        )
        scores = jnp.where(key_mask[None, :] > 0.5, scores, -1000000000.0)
        highest = jnp.max(scores, axis=-1, keepdims=True)
        weights = jnp.exp(scores - highest)
        totals = jnp.sum(weights, axis=-1, keepdims=True)
        mixed = jnp.dot(
            (weights / totals).astype(jnp.bfloat16), value_head, preferred_element_type=jnp.float32
        )
        return (mixed, (highest + jnp.log(totals))[:, 0])

    mixed, log_sums = lax.map(one_block, query_head.reshape(blocks, row_count // blocks, -1))
    return (mixed.reshape(row_count, -1), log_sums.reshape(row_count))


def attend_backward(query_head, key_head, value_head, key_mask, log_sums, out_grad):
    scaling = query_head.shape[-1] ** (-0.5)
    row_count = query_head.shape[0]
    blocks = max(1, 2 * row_count // key_head.shape[0])
    block_rows = row_count // blocks

    def one_block(carry, pieces):
        key_grad, value_grad = carry
        query_block, log_block, grad_block = pieces
        scores = (
            jnp.einsum("qd,kd->qk", query_block, key_head, preferred_element_type=jnp.float32)
            * scaling
        )
        scores = jnp.where(key_mask[None, :] > 0.5, scores, -1000000000.0)
        weights = jnp.exp(scores - log_block[:, None])
        value_grad = value_grad + jnp.einsum(
            "qk,qd->kd",
            weights.astype(jnp.bfloat16),
            grad_block,
            preferred_element_type=jnp.float32,
        )
        weight_grad = jnp.einsum(
            "qd,kd->qk", grad_block, value_head, preferred_element_type=jnp.float32
        )
        centered = jnp.sum(weights * weight_grad, axis=-1, keepdims=True)
        score_grad = (weights * (weight_grad - centered)).astype(jnp.bfloat16)
        query_grad = jnp.dot(score_grad, key_head, preferred_element_type=jnp.float32) * scaling
        key_grad = (
            key_grad
            + jnp.einsum("qk,qd->kd", score_grad, query_block, preferred_element_type=jnp.float32)
            * scaling
        )
        return ((key_grad, value_grad), query_grad)

    zeros_init = jnp.zeros(key_head.shape, jnp.float32)
    (key_grad, value_grad), query_grad = lax.scan(
        one_block,
        (zeros_init, zeros_init),
        (
            query_head.reshape(blocks, block_rows, -1),
            log_sums.reshape(blocks, block_rows),
            out_grad.reshape(blocks, block_rows, -1),
        ),
    )
    return (query_grad.reshape(row_count, -1), key_grad, value_grad)


def heads_forward(query_heads, key_heads, value_heads, key_masks):
    return lax.map(
        lambda pieces: attend_forward(pieces[0], pieces[1], pieces[2], pieces[3]),
        (query_heads, key_heads, value_heads, key_masks),
    )


def heads_backward(query_heads, key_heads, value_heads, key_masks, log_sums, out_grads):
    return lax.map(
        lambda pieces: attend_backward(
            pieces[0], pieces[1], pieces[2], pieces[3], pieces[4], pieces[5]
        ),
        (query_heads, key_heads, value_heads, key_masks, log_sums, out_grads),
    )


def column_sum(tensor):
    return jnp.sum(tensor.astype(jnp.float32), axis=(0, 1))


def general_body(
    tokens,
    token_mask,
    ln1_gain,
    ln1_bias,
    w_qkv,
    bias_q,
    bias_v,
    w_out,
    bias_out,
    ln2_gain,
    ln2_bias,
    w_up,
    bias_up,
    w_down,
    bias_down,
    cotangent,
):
    (
        gain_one,
        shift_one,
        qkv_full,
        query_bias,
        value_bias,
        out_full,
        out_bias,
        gain_two,
        shift_two,
        up_full,
        up_bias,
        down_full,
        down_bias,
    ) = (
        lax.all_gather(ln1_gain, "img", axis=0, tiled=True),
        lax.all_gather(ln1_bias, "img", axis=0, tiled=True),
        lax.all_gather(w_qkv, "img", axis=0, tiled=True),
        lax.all_gather(bias_q, "img", axis=0, tiled=True),
        lax.all_gather(bias_v, "img", axis=0, tiled=True),
        lax.all_gather(w_out, "img", axis=0, tiled=True),
        lax.all_gather(bias_out, "img", axis=0, tiled=True),
        lax.all_gather(ln2_gain, "img", axis=0, tiled=True),
        lax.all_gather(ln2_bias, "img", axis=0, tiled=True),
        lax.all_gather(w_up, "img", axis=0, tiled=True),
        lax.all_gather(bias_up, "img", axis=0, tiled=True),
        lax.all_gather(w_down, "img", axis=0, tiled=True),
        lax.all_gather(bias_down, "img", axis=0, tiled=True),
    )
    images, shard_rows, model_dim = tokens.shape
    seq_parts = lax.axis_size("seq")
    inputs = tokens.astype(jnp.float32)
    mask_float = token_mask.astype(jnp.float32)
    normed, norm_one_pull = jax.vjp(
        layer_norm, inputs, gain_one.astype(jnp.float32), shift_one.astype(jnp.float32)
    )
    normed_low = normed.astype(jnp.bfloat16)
    projected = jnp.einsum("bsd,de->bse", normed_low, qkv_full, preferred_element_type=jnp.float32)
    query_tok = (projected[..., :model_dim] + query_bias.astype(jnp.float32)).astype(jnp.bfloat16)
    key_tok = projected[..., model_dim : 2 * model_dim].astype(jnp.bfloat16)
    value_tok = (projected[..., 2 * model_dim :] + value_bias.astype(jnp.float32)).astype(
        jnp.bfloat16
    )
    mask_low = token_mask.astype(jnp.bfloat16)
    local_heads = HEADS // seq_parts
    stacked = jnp.stack([query_tok, key_tok, value_tok], axis=2)
    mask_tile = jnp.broadcast_to(mask_low[:, :, None, None], (images, shard_rows, 1, seq_parts))
    stacked_heads, mask_heads = (
        lax.all_to_all(stacked, "seq", split_axis=3, concat_axis=1, tiled=True),
        lax.all_to_all(mask_tile, "seq", split_axis=3, concat_axis=1, tiled=True),
    )
    query_heads = split_heads(stacked_heads[:, :, 0], local_heads)
    key_heads = split_heads(stacked_heads[:, :, 1], local_heads)
    value_heads = split_heads(stacked_heads[:, :, 2], local_heads)
    key_masks = jnp.repeat(mask_heads[:, :, 0, 0].astype(jnp.float32), local_heads, axis=0)
    attended, log_sums = heads_forward(query_heads, key_heads, value_heads, key_masks)
    merged_heads = join_heads(attended, images).astype(jnp.bfloat16)
    merged = lax.all_to_all(merged_heads, "seq", split_axis=1, concat_axis=2, tiled=True)
    branch = jnp.einsum(
        "bsd,de->bse", merged, out_full, preferred_element_type=jnp.float32
    ) + out_bias.astype(jnp.float32)
    middle = inputs + branch
    second, norm_two_pull = jax.vjp(
        layer_norm, middle, gain_two.astype(jnp.float32), shift_two.astype(jnp.float32)
    )
    second_low = second.astype(jnp.bfloat16)
    pre_act = jnp.einsum(
        "bsd,df->bsf", second_low, up_full, preferred_element_type=jnp.float32
    ) + up_bias.astype(jnp.float32)
    hidden, gelu_pull = jax.vjp(gelu_exact, pre_act)
    hidden_low = hidden.astype(jnp.bfloat16)
    output = (
        middle
        + jnp.einsum("bsf,fd->bsd", hidden_low, down_full, preferred_element_type=jnp.float32)
        + down_bias.astype(jnp.float32)
    )
    upstream = cotangent.astype(jnp.float32) * mask_float[..., None]
    down_in = upstream.astype(jnp.bfloat16)
    grad_down = jnp.einsum("bsf,bsd->fd", hidden_low, down_in, preferred_element_type=jnp.float32)
    grad_down_bias = column_sum(down_in)
    hidden_grad = jnp.einsum("bsd,fd->bsf", down_in, down_full, preferred_element_type=jnp.float32)
    pre_grad = gelu_pull(hidden_grad)[0].astype(jnp.bfloat16)
    grad_up = jnp.einsum("bsd,bsf->df", second_low, pre_grad, preferred_element_type=jnp.float32)
    grad_up_bias = column_sum(pre_grad)
    second_grad = jnp.einsum("bsf,df->bsd", pre_grad, up_full, preferred_element_type=jnp.float32)
    middle_ln_grad, grad_gain_two, grad_shift_two = norm_two_pull(second_grad)
    middle_grad = upstream + middle_ln_grad
    branch_grad = middle_grad.astype(jnp.bfloat16)
    grad_out = jnp.einsum("bsd,bse->de", merged, branch_grad, preferred_element_type=jnp.float32)
    grad_out_bias = column_sum(branch_grad)
    merged_grad = jnp.einsum(
        "bse,de->bsd", branch_grad, out_full, preferred_element_type=jnp.float32
    ).astype(jnp.bfloat16)
    grad_heads_in = lax.all_to_all(merged_grad, "seq", split_axis=2, concat_axis=1, tiled=True)
    query_grad, key_grad, value_grad = heads_backward(
        query_heads,
        key_heads,
        value_heads,
        key_masks,
        log_sums,
        split_heads(grad_heads_in, local_heads),
    )
    triple = jnp.stack(
        [
            join_heads(query_grad, images),
            join_heads(key_grad, images),
            join_heads(value_grad, images),
        ],
        axis=2,
    ).astype(jnp.bfloat16)
    qkv_grad = lax.all_to_all(triple, "seq", split_axis=1, concat_axis=3, tiled=True)
    qkv_flat = qkv_grad.reshape(images, shard_rows, 3 * model_dim)
    grad_qkv = jnp.einsum("bsd,bse->de", normed_low, qkv_flat, preferred_element_type=jnp.float32)
    grad_query_bias = column_sum(qkv_grad[:, :, 0])
    grad_value_bias = column_sum(qkv_grad[:, :, 2])
    normed_grad = jnp.einsum("bse,de->bsd", qkv_flat, qkv_full, preferred_element_type=jnp.float32)
    input_ln_grad, grad_gain_one, grad_shift_one = norm_one_pull(normed_grad)
    input_grad = middle_grad + input_ln_grad
    shards_all = (
        lax.psum_scatter(grad_gain_one, "img", scatter_dimension=0, tiled=True),
        lax.psum_scatter(grad_shift_one, "img", scatter_dimension=0, tiled=True),
        lax.psum_scatter(grad_qkv, "img", scatter_dimension=0, tiled=True),
        lax.psum_scatter(grad_query_bias, "img", scatter_dimension=0, tiled=True),
        lax.psum_scatter(grad_value_bias, "img", scatter_dimension=0, tiled=True),
        lax.psum_scatter(grad_out, "img", scatter_dimension=0, tiled=True),
        lax.psum_scatter(grad_out_bias, "img", scatter_dimension=0, tiled=True),
        lax.psum_scatter(grad_gain_two, "img", scatter_dimension=0, tiled=True),
        lax.psum_scatter(grad_shift_two, "img", scatter_dimension=0, tiled=True),
        lax.psum_scatter(grad_up, "img", scatter_dimension=0, tiled=True),
        lax.psum_scatter(grad_up_bias, "img", scatter_dimension=0, tiled=True),
        lax.psum_scatter(grad_down, "img", scatter_dimension=0, tiled=True),
        lax.psum_scatter(grad_down_bias, "img", scatter_dimension=0, tiled=True),
    )
    summed_all = lax.psum(
        (
            shards_all[0],
            shards_all[1],
            shards_all[2],
            shards_all[3],
            shards_all[4],
            shards_all[5],
            shards_all[6],
            shards_all[7],
            shards_all[8],
            shards_all[9],
            shards_all[10],
            shards_all[11],
            shards_all[12],
        ),
        "seq",
    )
    return (
        output,
        input_grad,
        summed_all[0],
        summed_all[1],
        summed_all[2],
        summed_all[3],
        summed_all[4],
        summed_all[5],
        summed_all[6],
        summed_all[7],
        summed_all[8],
        summed_all[9],
        summed_all[10],
        summed_all[11],
        summed_all[12],
    )


LOW = jnp.bfloat16
F32 = jnp.float32
VMEM = 56 * 1024 * 1024
SMALL_PAD = 256


def cost(microseconds):
    return pl.CostEstimate(flops=int(microseconds * 1.15e9), bytes_accessed=1, transcendentals=0)


def dot_nt(left, right):
    return lax.dot_general(left, right, (((1,), (1,)), ((), ())), preferred_element_type=F32)


def dot_nn(left, right):
    return lax.dot_general(left, right, (((1,), (0,)), ((), ())), preferred_element_type=F32)


def dot_tn(left, right):
    return lax.dot_general(left, right, (((0,), (0,)), ((), ())), preferred_element_type=F32)


def attention_forward_kernel(
    scale, size, inputs_ref, gain_ref, shift_ref, q_weight_ref, k_weight_ref, v_weight_ref, q_bias_ref, v_bias_ref,
    mask_ref, out_ref, log_ref, query_ref, key_ref, value_ref, normed_ref,
):
    @pl.when(pl.program_id(0) == 0)
    def _():
        unit, _ = norm_parts(inputs_ref[...].astype(F32))
        normed_ref[...] = (unit * gain_ref[...] + shift_ref[...]).astype(LOW)

    weight = jnp.concatenate([q_weight_ref[...], k_weight_ref[...], v_weight_ref[...]], axis=1)
    projected = dot_nn(normed_ref[...], weight)
    query_ref[...] = (projected[:, : 2 * size] + q_bias_ref[...]).astype(LOW)
    key_ref[...] = projected[:, 2 * size : 4 * size].astype(LOW)
    value_ref[...] = (projected[:, 4 * size :] + v_bias_ref[...]).astype(LOW)
    real = mask_ref[...] > 0.5
    query = query_ref[...] * jnp.asarray(scale, LOW)
    key = jnp.where(real, key_ref[...], key_ref[0:1, :])
    value = value_ref[...]
    lane = lax.broadcasted_iota(jnp.int32, key.shape, 1)
    pieces = []
    for head in range(2):
        mine = (lane // size) == head
        scores = dot_nt(jnp.where(mine, key, jnp.zeros_like(key)), query)
        highest = jnp.max(scores, axis=0, keepdims=True)
        weights = jnp.exp(scores - highest).astype(LOW)
        extended = jnp.where(real, jnp.where(mine, value, jnp.ones_like(value)), jnp.zeros_like(value))
        mixed = dot_tn(extended, weights)
        own, other = head * size, (1 - head) * size
        totals = mixed[other : other + size, :]
        pieces.append(mixed[own : own + size, :] / totals)
        log_ref[0, head : head + 1, :] = highest + jnp.log(totals[0:1, :])
    out_ref[...] = jnp.concatenate(pieces, axis=0).T.astype(LOW)


def attention_forward(inputs, gain, shift, first, query_bias, value_bias, mask_column):
    rows, dim = inputs.shape
    size = dim // HEADS
    pairs = HEADS // 2
    spec = pl.BlockSpec((rows, 2 * size), lambda p: (0, p))
    bias = pl.BlockSpec((1, 2 * size), lambda p: (0, p))
    row = pl.BlockSpec((1, dim), lambda p: (0, 0))
    return pl.pallas_call(
        functools.partial(attention_forward_kernel, size ** (-0.5), size),
        grid=(pairs,),
        in_specs=[
            pl.BlockSpec((rows, dim), lambda p: (0, 0)),
            row,
            row,
            pl.BlockSpec((dim, 2 * size), lambda p: (0, p)),
            pl.BlockSpec((dim, 2 * size), lambda p: (0, pairs + p)),
            pl.BlockSpec((dim, 2 * size), lambda p: (0, 2 * pairs + p)),
            bias,
            bias,
            pl.BlockSpec((rows, 1), lambda p: (0, 0)),
        ],
        out_specs=[spec, pl.BlockSpec((1, 2, rows), lambda p: (p, 0, 0)), spec, spec, spec],
        out_shape=[
            jax.ShapeDtypeStruct((rows, dim), LOW),
            jax.ShapeDtypeStruct((pairs, 2, rows), F32),
            jax.ShapeDtypeStruct((rows, dim), LOW),
            jax.ShapeDtypeStruct((rows, dim), LOW),
            jax.ShapeDtypeStruct((rows, dim), LOW),
        ],
        scratch_shapes=[pltpu.VMEM((rows, dim), LOW)],
        compiler_params=pltpu.CompilerParams(vmem_limit_bytes=VMEM),
        cost_estimate=cost(16),
        name="attention_forward",
    )(inputs, gain, shift, first, first, first, query_bias, value_bias, mask_column)


def attention_backward_kernel(
    scale, size, query_ref, key_ref, value_ref, mask_ref, log_ref, grad_ref, dq_ref, dk_ref, dv_ref
):
    real = mask_ref[...] > 0.5
    query = query_ref[...] * jnp.asarray(scale, LOW)
    zeros = jnp.zeros_like(query)
    key_kept = jnp.where(real, key_ref[...], zeros)
    key = jnp.where(real, key_kept, key_ref[0:1, :])
    value = jnp.where(real, value_ref[...], zeros)
    grad = grad_ref[...]
    lane = lax.broadcasted_iota(jnp.int32, key.shape, 1)
    totals = None
    for head in range(2):
        mine = (lane // size) == head
        scores = dot_nt(jnp.where(mine, key, zeros), query)
        weights = jnp.exp(scores - log_ref[0, head : head + 1, :])
        grad_here = jnp.where(mine, grad, zeros)
        value_grad = dot_nn(weights.astype(LOW), grad_here)
        weight_grad = dot_nt(value, grad_here)
        centered = jnp.sum(weights * weight_grad, axis=0, keepdims=True)
        score_grad = (weights * (weight_grad - centered)).astype(LOW)
        key_grad = dot_nn(score_grad, jnp.where(mine, query, zeros))
        query_grad = dot_tn(jnp.where(mine, key_kept, zeros), score_grad)
        if totals is None:
            totals = (query_grad, key_grad, value_grad)
        else:
            totals = tuple(a + b for a, b in zip(totals, (query_grad, key_grad, value_grad)))
    query_grad, key_grad, value_grad = totals
    dq_ref[...] = (query_grad * scale).T.astype(LOW)
    dk_ref[...] = jnp.where(real, key_grad, 0.0).astype(LOW)
    dv_ref[...] = jnp.where(real, value_grad, 0.0).astype(LOW)


def attention_backward(qkv, mask_column, logs, grad, first, count):
    rows, dim = grad.shape
    size = dim // HEADS
    block = (rows, 2 * size)
    spec = pl.BlockSpec(block, lambda p: (0, first + p))
    out_spec = pl.BlockSpec(block, lambda p: (0, p))
    return pl.pallas_call(
        functools.partial(attention_backward_kernel, size ** (-0.5), size),
        grid=(count,),
        in_specs=[
            spec,
            spec,
            spec,
            pl.BlockSpec((rows, 1), lambda p: (0, 0)),
            pl.BlockSpec((1, 2, rows), lambda p: (first + p, 0, 0)),
            spec,
        ],
        out_specs=[out_spec] * 3,
        out_shape=[jax.ShapeDtypeStruct((rows, 2 * size * count), LOW)] * 3,
        compiler_params=pltpu.CompilerParams(vmem_limit_bytes=VMEM),
        cost_estimate=cost(1),
        name="attention_backward",
    )(*qkv, mask_column, logs, grad)


def split_cores(total_ref, kept_ref, sent_ref, first, columns):
    core = lax.axis_index("img") % 2
    shard = kept_ref.shape[2]
    for pair in range(total_ref.shape[0] // (2 * shard)):
        z, x = first + pair // 2, pair % 2
        kept_ref[z, x, :, columns] = total_ref[pl.ds(pl.multiple_of((2 * pair + core) * shard, 16), shard), :]
        sent_ref[z, x, :, columns] = total_ref[pl.ds(pl.multiple_of((2 * pair + 1 - core) * shard, 16), shard), :]


def mlp_first_kernel(
    shape, second_ref, dz_ref, up_ref, up_bias_ref, down_ref, middle_ref, down_bias_ref,
    out_ref, kept_ref, sent_ref, pre_grad_ref, up_bias_grad_ref, down_grad_ref,
):
    step = pl.program_id(0)
    owners, pieces, dim = shape
    dz = dz_ref[...]
    down = jnp.concatenate(
        [down_ref[o, :, i * dim : (i + 1) * dim] for o in range(owners) for i in range(pieces)], axis=0
    )
    pre_act = dot_nn(second_ref[...], up_ref[...]) + up_bias_ref[...]
    hidden_grad = dot_nt(dz, down)
    cumulative = 0.5 + 0.5 * lax.erf(pre_act * (0.5 ** 0.5))
    density = jnp.exp(-0.5 * pre_act * pre_act) * 0.3989422804014327
    hidden = (pre_act * cumulative).astype(LOW)
    pre_grad = (hidden_grad * (cumulative + pre_act * density)).astype(LOW)
    pre_grad_ref[...] = pre_grad
    bias_grad = jnp.sum(pre_grad.astype(F32), axis=0, keepdims=True)
    turned = jnp.broadcast_to(bias_grad, (128, bias_grad.shape[1])).T
    shard = kept_ref.shape[2]
    lane = lax.broadcasted_iota(jnp.int32, (shard, 128), 1)
    for o in range(owners):
        tile = jnp.zeros((shard, 128), F32)
        for i in range(pieces):
            start = (o * pieces + i) * shard
            tile = jnp.where(lane == i, turned[start : start + shard], tile)
        up_bias_grad_ref[o * shard : (o + 1) * shard, :] = tile.astype(LOW)
    out_part = dot_nn(hidden, down)
    down_grad_ref[...] = dot_tn(hidden, dz).astype(LOW)
    core = lax.axis_index("img") % 2
    for x in range(2):
        for ref, side in ((kept_ref, core), (sent_ref, 1 - core)):
            for i in range(pieces):
                start = pl.multiple_of(((2 * x + side) * pieces + i) * shard, 16)
                ref[0, x, :, i * dim : (i + 1) * dim] = down_grad_ref[pl.ds(start, shard), :]

    @pl.when(step == 0)
    def _():
        out_ref[...] = middle_ref[...] + down_bias_ref[...] + out_part

    @pl.when(step > 0)
    def _():
        out_ref[...] += out_part


def mlp_first(second, dz, up_down, up_bias, middle, down_bias, owners):
    rows, dim = second.shape
    width = up_bias.shape[1]
    shard = dim // owners
    pieces = width // dim
    some = owners // pieces
    whole = pl.BlockSpec((rows, dim), lambda j: (0, 0))
    return pl.pallas_call(
        functools.partial(mlp_first_kernel, (some, pieces, dim)),
        grid=(pieces,),
        in_specs=[
            whole,
            whole,
            pl.BlockSpec((dim, dim), lambda j: (0, j)),
            pl.BlockSpec((1, dim), lambda j: (0, j)),
            pl.BlockSpec((some, shard, width), lambda j: (j, 0, 1)),
            whole,
            pl.BlockSpec((1, dim), lambda j: (0, 0)),
        ],
        out_specs=[
            whole,
            pl.BlockSpec((1, 2, shard, width), lambda j: (j, 0, 0, 0)),
            pl.BlockSpec((1, 2, shard, width), lambda j: (j, 0, 0, 0)),
            pl.BlockSpec((rows, dim), lambda j: (0, j)),
            pl.BlockSpec((some * shard, 128), lambda j: (j, 0)),
        ],
        out_shape=[
            jax.ShapeDtypeStruct((rows, dim), F32),
            jax.ShapeDtypeStruct((4, 2, shard, width), LOW),
            jax.ShapeDtypeStruct((4, 2, shard, width), LOW),
            jax.ShapeDtypeStruct((rows, width), LOW),
            jax.ShapeDtypeStruct((dim, 128), LOW),
        ],
        scratch_shapes=[pltpu.VMEM((dim, dim), LOW)],
        compiler_params=pltpu.CompilerParams(vmem_limit_bytes=VMEM),
        cost_estimate=cost(19),
        name="mlp_first",
    )(second, dz, up_down, up_bias, up_down.reshape(owners, shard, 2 * width), middle, down_bias)


def mlp_second_kernel(second_ref, pre_grad_ref, up_ref, second_grad_ref, kept_ref, sent_ref, up_grad_ref):
    step = pl.program_id(0)
    pre_grad = pre_grad_ref[...]
    up_grad_ref[...] = dot_tn(second_ref[...], pre_grad).astype(LOW)
    split_cores(up_grad_ref, kept_ref, sent_ref, 0, slice(None))
    part = dot_nt(pre_grad, up_ref[...])

    @pl.when(step == 0)
    def _():
        second_grad_ref[...] = part

    @pl.when(step > 0)
    def _():
        second_grad_ref[...] += part


def mlp_second(second, pre_grad, up_down, owners):
    rows, dim = second.shape
    width = pre_grad.shape[1]
    shard = dim // owners
    whole = pl.BlockSpec((rows, dim), lambda j: (0, 0))
    split = pl.BlockSpec((4, 2, shard, dim), lambda j: (0, 0, 0, j))
    return pl.pallas_call(
        mlp_second_kernel,
        grid=(width // dim,),
        in_specs=[
            whole,
            pl.BlockSpec((rows, dim), lambda j: (0, j)),
            pl.BlockSpec((dim, dim), lambda j: (0, j)),
        ],
        out_specs=[whole, split, split],
        out_shape=[
            jax.ShapeDtypeStruct((rows, dim), F32),
            jax.ShapeDtypeStruct((4, 2, shard, width), LOW),
            jax.ShapeDtypeStruct((4, 2, shard, width), LOW),
        ],
        scratch_shapes=[pltpu.VMEM((dim, dim), LOW)],
        compiler_params=pltpu.CompilerParams(vmem_limit_bytes=VMEM),
        cost_estimate=cost(1),
        name="mlp_second",
    )(second, pre_grad, up_down)


def norm_parts(values):
    offset = values - jnp.mean(values, axis=-1, keepdims=True)
    inverse = lax.rsqrt(jnp.mean(offset * offset, axis=-1, keepdims=True) + epsilon)
    return offset * inverse, inverse


def norm_back(unit, inverse, gain, grad):
    scaled = grad * gain
    across = jnp.mean(scaled, axis=-1, keepdims=True)
    along = jnp.mean(scaled * unit, axis=-1, keepdims=True)
    return inverse * (scaled - across - unit * along)


def column_sums(values):
    return jnp.sum(values, axis=0, keepdims=True)


def middle_kernel(
    middle_ref, grad_ref, dz_ref, gain_ref, out_full_ref, merged_ref,
    middle_grad_ref, merged_grad_ref, kept_ref, sent_ref, small_ref, out_grad_ref,
):
    unit, inverse = norm_parts(middle_ref[...])
    grad = grad_ref[...]
    upstream = dz_ref[...].astype(F32)
    middle_grad = upstream + norm_back(unit, inverse, gain_ref[...], grad)
    middle_grad_ref[...] = middle_grad
    low = middle_grad.astype(LOW)
    merged_grad_ref[...] = dot_nt(low, out_full_ref[...]).astype(LOW)
    out_grad_ref[...] = dot_tn(merged_ref[...], low).astype(LOW)
    split_cores(out_grad_ref, kept_ref, sent_ref, 0, slice(None))
    small_ref[0:1] = column_sums(low.astype(F32))
    small_ref[1:2] = column_sums(grad * unit)
    small_ref[2:3] = column_sums(grad)
    small_ref[3:4] = column_sums(upstream)


def middle_backward(middle, second_grad, dz, gain, first, merged, owners):
    rows, dim = middle.shape
    split = (4, 2, dim // owners, dim)
    whole = pl.BlockSpec((rows, dim), lambda j: (0, 0))
    return pl.pallas_call(
        middle_kernel,
        grid=(1,),
        in_specs=[
            whole,
            whole,
            whole,
            pl.BlockSpec((1, dim), lambda j: (0, 0)),
            pl.BlockSpec((dim, dim), lambda j: (0, 3)),
            whole,
        ],
        out_specs=[
            whole,
            whole,
            pl.BlockSpec(split, lambda j: (0, 0, 0, 0)),
            pl.BlockSpec(split, lambda j: (0, 0, 0, 0)),
            pl.BlockSpec((4, dim), lambda j: (0, 0)),
        ],
        out_shape=[
            jax.ShapeDtypeStruct((rows, dim), F32),
            jax.ShapeDtypeStruct((rows, dim), LOW),
            jax.ShapeDtypeStruct(split, LOW),
            jax.ShapeDtypeStruct(split, LOW),
            jax.ShapeDtypeStruct((4, dim), F32),
        ],
        scratch_shapes=[pltpu.VMEM((dim, dim), LOW)],
        compiler_params=pltpu.CompilerParams(vmem_limit_bytes=VMEM),
        cost_estimate=cost(1),
        name="middle_backward",
    )(middle, second_grad, dz, gain, first, merged)


def last_kernel(
    inputs_ref, gain_ref, shift_ref, q_low, k_low, v_low, q_high, k_high, v_high, qkv_full_ref,
    middle_grad_ref, small_ref, up_bias_ref, input_grad_ref, kept_ref, sent_ref, total_ref,
):
    unit, inverse = norm_parts(inputs_ref[...].astype(F32))
    gain = gain_ref[...]
    normed = (unit * gain + shift_ref[...]).astype(LOW)
    grads = [ref[...] for ref in (q_low, q_high, k_low, k_high, v_low, v_high)]
    qkv_grad = jnp.concatenate(grads, axis=1)
    dim = unit.shape[1]
    normed_grad = dot_nt(qkv_grad, qkv_full_ref[...])
    input_grad_ref[...] = middle_grad_ref[...] + norm_back(unit, inverse, gain, normed_grad)
    total_ref[:, : 3 * dim] = dot_tn(normed, qkv_grad).astype(LOW)
    bias_of = column_sums(qkv_grad.astype(F32))
    rows = [column_sums(normed_grad * unit), column_sums(normed_grad), bias_of[:, :dim], bias_of[:, 2 * dim :]]
    rows += [small_ref[...]]
    taken = sum(row.shape[0] for row in rows)
    rows.append(jnp.zeros((128 - taken, dim), F32))
    total_ref[:, 3 * dim : 3 * dim + 128] = jnp.concatenate(rows, axis=0).T.astype(LOW)
    total_ref[:, 3 * dim + 128 :] = up_bias_ref[...]
    split_cores(total_ref, kept_ref, sent_ref, 0, slice(None))


def last_backward(inputs, gain, shift, grads_low, grads_high, first, middle_grad, small, up_bias, owners):
    rows, dim = inputs.shape
    columns = 3 * dim + SMALL_PAD

    def whole(*shape):
        return pl.BlockSpec(shape, lambda j: (0,) * len(shape))

    split = jax.ShapeDtypeStruct((4, 2, dim // owners, columns), LOW)
    return pl.pallas_call(
        last_kernel,
        grid=(1,),
        in_specs=[whole(rows, dim), whole(1, dim), whole(1, dim)]
        + [whole(*g.shape) for g in (*grads_low, *grads_high)]
        + [whole(dim, 3 * dim), whole(rows, dim), whole(*small.shape), whole(*up_bias.shape)],
        out_specs=[whole(rows, dim), whole(*split.shape), whole(*split.shape)],
        out_shape=[jax.ShapeDtypeStruct((rows, dim), F32), split, split],
        scratch_shapes=[pltpu.VMEM((dim, columns), LOW)],
        compiler_params=pltpu.CompilerParams(vmem_limit_bytes=VMEM),
        cost_estimate=cost(1),
        name="last_backward",
    )(inputs, gain, shift, *grads_low, *grads_high, first, middle_grad, small, up_bias)


def own_and_away(blocks):
    here = lax.axis_index("seq")
    own = lax.dynamic_index_in_dim(blocks, here, 0, keepdims=False)
    return own, lax.dynamic_index_in_dim(blocks, 1 - here, 0, keepdims=False)


def both_images(own, back):
    here = lax.axis_index("seq")
    back = back.astype(F32)
    return jnp.where(here == 0, jnp.stack([own, back]), jnp.stack([back, own]))


def gather(block):
    return lax.all_gather(block, "img", axis=0, tiled=True)


def place():
    img = lax.axis_index("img")
    return img // 4, (img // 2) % 2, img % 2, lax.axis_index("seq")


def swap(block, z=0, x=0, core=0, y=0):
    bits = z * 8 + x * 4 + core * 2 + y
    return lax.ppermute(block, ("img", "seq"), [(i, i ^ bits) for i in range(32)])


def assemble_kernel(small_at, *refs):
    refs, out_ref, small_ref = refs[:-2], refs[-2], refs[-1]
    here_z, here_x, here_core, here_y = place()
    half = out_ref.shape[2] // 2
    for index, ref in enumerate(refs):
        first, x, y, core = index // 8, index // 4 % 2, index // 2 % 2, index % 2
        columns = pl.ds(pl.multiple_of((here_y ^ y) * half, half), half)
        for i in range(ref.shape[0]):
            owner = (here_z ^ (first + i)) * 4 + (here_x ^ x) * 2 + (here_core ^ core)
            out_ref[owner, :, columns] = ref[i]
    small = jnp.concatenate([out_ref[i, :, small_at : small_at + 128] for i in range(16)], axis=0)
    small_ref[...] = small.astype(F32).T[:16]


def gather_links(block, rows, later):
    shard, columns = block.shape
    half = columns // 2
    own = lax.dynamic_slice_in_dim(block, lax.axis_index("seq") * half, half, 1)[None]
    rows = swap(rows, y=1)
    line = [swap(own, z=z) for z in (1, 2, 3)]
    own_x, own_y = swap(own, x=1), swap(own, y=1)
    rest = jnp.concatenate(line)
    rest, rows, own_x, own_y = tie(rest, rows, own_x, own_y)
    rest_x = swap(rest, x=1)
    refs = []
    for part in (own, own_y, own_x, swap(own_x, y=1), rest, swap(rest, y=1), rest_x, swap(rest_x, y=1)):
        refs += [part, swap(part, core=1)]
    whole, small = pl.pallas_call(
        functools.partial(assemble_kernel, columns - SMALL_PAD),
        out_shape=[
            jax.ShapeDtypeStruct((16, shard, columns), LOW),
            jax.ShapeDtypeStruct((16, 16 * shard), F32),
        ],
        compiler_params=pltpu.CompilerParams(vmem_limit_bytes=VMEM),
        name="assemble",
    )(*refs)
    return whole.reshape(16 * shard, columns), small, rows, later


def total(pieces):
    result = pieces[0].astype(F32)
    for piece in pieces[1:]:
        result = result + piece.astype(F32)
    return result.astype(LOW)


def plane_pieces(paired):
    _, x, _, y = place()
    rows, half = paired.shape[2], paired.shape[3] // 2

    def part(x_index, y_index):
        return lax.dynamic_slice(paired, (0, x_index, 0, y_index * half), (4, 1, rows, half))[:, 0]

    return [part(x, y), part(1 - x, y), part(x, 1 - y), part(1 - x, 1 - y)]


def plane_swaps(pieces):
    return [pieces[0], swap(pieces[1], x=1), swap(pieces[2], y=1), swap(pieces[3], x=1, y=1)]


def line_pieces(line):
    z = place()[0]
    return [lax.dynamic_index_in_dim(line, z ^ step, 0, keepdims=False) for step in range(4)]


def half_line(line, bit):
    return lax.dynamic_slice_in_dim(line, bit * (line.shape[0] // 2), line.shape[0] // 2, 0)


def line_swaps(pieces):
    return [pieces[0]] + [swap(pieces[step], z=step) for step in (1, 2, 3)]


def join_halves(own, other):
    here = lax.axis_index("seq")
    return jnp.where(
        here == 0, jnp.concatenate([own, other], axis=1), jnp.concatenate([other, own], axis=1)
    ).astype(F32)


def tie(*values):
    return lax.optimization_barrier(values)


def image_body(
    tokens, token_mask, ln1_gain, ln1_bias, w_qkv, bias_q, bias_v, w_out, bias_out,
    ln2_gain, ln2_bias, w_up, bias_up, w_down, bias_down, cotangent,
):
    shard_rows, dim = tokens.shape[1:]
    owners = lax.axis_size("img")
    shard = dim // owners
    width = bias_up.shape[0] * owners
    pieces = width // dim

    up_down = jnp.concatenate(
        [w_up, w_down.reshape(pieces, shard, dim).swapaxes(0, 1).reshape(shard, width)], axis=1
    )
    rows_small = jnp.concatenate(
        [jnp.stack([ln1_gain, ln1_bias, bias_q, bias_v, bias_out, ln2_gain, ln2_bias, bias_down])]
        + [bias_up.reshape(pieces, shard)]
    )
    count = rows_small.shape[0]
    padding = jnp.pad(rows_small.T, ((0, 0), (0, SMALL_PAD - count)))
    mask_rows = jnp.broadcast_to(
        jnp.pad(token_mask.astype(LOW), ((0, 0), (0, dim - shard_rows)))[:, None, :], (2, 16, dim)
    )
    own, away = own_and_away(jnp.concatenate([tokens, mask_rows], axis=1))
    first, small, away, up_down = gather_links(jnp.concatenate([w_qkv, w_out, padding], axis=1), away, up_down)
    up_down = gather(up_down)
    masked = jnp.where(token_mask[..., None] > 0, cotangent, jnp.zeros_like(cotangent))
    own_in, away_in = own_and_away(masked)
    first, away_in = tie(first, away_in)
    down_in = jnp.concatenate([own_in, swap(away_in, y=1)], axis=0)
    out_full = first[:, 3 * dim : 4 * dim]
    gain_one, shift_one, query_bias, value_bias, out_bias, gain_two, shift_two, down_bias = [
        small[i : i + 1] for i in range(8)
    ]
    up_bias = small[8:count].reshape(pieces, owners, shard).swapaxes(0, 1).reshape(1, width)

    both = jnp.stack([own, away])
    inputs_low = both[:, :shard_rows].reshape(2 * shard_rows, dim)
    inputs = inputs_low.astype(F32)
    mask_column = both[:, shard_rows, :shard_rows].astype(F32).reshape(2 * shard_rows, 1)
    merged, logs, *qkv = attention_forward(
        inputs_low, gain_one, shift_one, first, query_bias, value_bias, mask_column
    )
    middle = inputs + dot_nn(merged, out_full) + out_bias
    unit_two, _ = norm_parts(middle)
    second = (unit_two * gain_two + shift_two).astype(LOW)
    output, down_kept, down_sent, pre_grad, grad_up_bias = mlp_first(
        second, down_in, up_down, up_bias, middle, down_bias, owners
    )
    output_own, output_away = output[:shard_rows], output[shard_rows:].astype(LOW)
    pre_grad, output_away, down_sent = tie(pre_grad, output_away, down_sent)
    output_back, down_sent = swap(output_away, y=1), swap(down_sent, core=1)
    second_grad, up_kept, up_sent = mlp_second(second, pre_grad, up_down, owners)
    second_grad, up_kept, up_sent, output_back, down_sent = tie(second_grad, up_kept, up_sent, output_back, down_sent)
    down_pieces = plane_pieces(total([down_kept, down_sent]))
    second_grad, up_sent, *down_pieces = tie(second_grad, up_sent, *down_pieces)
    down_pieces, up_sent = plane_swaps(down_pieces), swap(up_sent, core=1)
    middle_grad, merged_grad, out_kept, out_sent, small_grads = middle_backward(
        middle, second_grad, down_in, gain_two, first, merged, owners
    )
    middle_grad, merged_grad, out_kept, out_sent, small_grads, up_sent = tie(
        middle_grad, merged_grad, out_kept, out_sent, small_grads, up_sent
    )
    out_sent = swap(out_sent, core=1)
    up_paired = total([up_kept, up_sent])
    merged_grad, up_paired = tie(merged_grad, up_paired)
    pairs = HEADS // 2
    grads_low = attention_backward(qkv, mask_column, logs, merged_grad, 0, pairs // 2)
    tied = tie(merged_grad, out_sent, *grads_low)
    merged_grad, grads_low = tied[0], tied[2:]
    up_pieces = [
        jnp.concatenate(both, axis=2)
        for both in zip(plane_pieces(up_paired), plane_pieces(total([out_kept, tied[1]])))
    ]
    tied = tie(merged_grad, *down_pieces, *up_pieces)
    merged_grad, down_line, up_pieces = tied[0], total(tied[1:5]), tied[5:]
    z = place()[0]
    merged_grad, down_away, *up_pieces = tie(merged_grad, half_line(down_line, 1 - z // 2), *up_pieces)
    down_away, up_pieces = swap(down_away, z=2), plane_swaps(up_pieces)
    grads_high = attention_backward(qkv, mask_column, logs, merged_grad, pairs // 2, pairs - pairs // 2)
    *grads_high, down_away = tie(*grads_high, down_away)
    down_two = total([half_line(down_line, z // 2), down_away])
    grad_up_bias, down_away = tie(grad_up_bias, half_line(down_two, 1 - z % 2))
    down_away = swap(down_away, z=1)
    input_grad, last_kept, last_sent = last_backward(
        inputs_low, gain_one, shift_one, grads_low, grads_high, first, middle_grad, small_grads, grad_up_bias, owners
    )
    tied = tie(input_grad, last_kept, last_sent, down_away, *up_pieces)
    input_grad, last_kept, last_sent, down_away = tied[:4]
    up_line = total(tied[4:])
    input_away = input_grad[shard_rows:].astype(LOW)
    last_sent = swap(last_sent, core=1)
    last_pieces = plane_pieces(total([last_kept, last_sent]))
    tied = tie(*last_pieces, *line_pieces(up_line))
    last_pieces, up_pieces = plane_swaps(tied[:4]), line_swaps(tied[4:])
    down_own = total([half_line(down_two, z % 2), down_away])[0]
    mlp_own = jnp.concatenate([down_own, total(up_pieces)], axis=1)
    tied = tie(input_away, *last_pieces)
    input_away, last_pieces = tied[0], line_pieces(total(tied[1:]))
    tied = tie(input_away, mlp_own, *last_pieces)
    input_away, mlp_own, last_pieces = tied[0], tied[1], line_swaps(tied[2:])
    mlp_other, input_back = swap(mlp_own, y=1), swap(input_away, y=1)
    tied = tie(mlp_other, input_back, *last_pieces)
    mlp_other, input_back, last_pieces = tied[0], tied[1], tied[2:]
    last_own = total(last_pieces)
    last_sum = join_halves(last_own, swap(last_own, y=1))
    down_sum = join_halves(mlp_own[:, : width // 2], mlp_other[:, : width // 2])
    up_sum = join_halves(mlp_own[:, width // 2 : width], mlp_other[:, width // 2 : width])
    out_sum = join_halves(mlp_own[:, width:], mlp_other[:, width:])
    smalls = last_sum[:, 3 * dim : 3 * dim + 8].T
    return (
        both_images(output_own, output_back), both_images(input_grad[:shard_rows], input_back),
        smalls[0], smalls[1], last_sum[:, : 3 * dim], smalls[2], smalls[3], out_sum,
        smalls[4], smalls[5], smalls[6], up_sum, last_sum[:, 3 * dim + 128 : 3 * dim + 128 + pieces].T.reshape(-1),
        down_sum.reshape(shard, pieces, dim).swapaxes(0, 1).reshape(pieces * shard, dim), smalls[7],
    )


def solution(mesh):
    in_specs = (
        P("img", "seq", None),
        P("img", "seq"),
        P("img"),
        P("img"),
        P("img", None),
        P("img"),
        P("img"),
        P("img", None),
        P("img"),
        P("img"),
        P("img"),
        P("img", None),
        P("img"),
        P("img", None),
        P("img"),
        P("img", "seq", None),
    )
    out_specs = (
        P("img", "seq", None),
        P("img", "seq", None),
        P("img"),
        P("img"),
        P("img", None),
        P("img"),
        P("img"),
        P("img", None),
        P("img"),
        P("img"),
        P("img"),
        P("img", None),
        P("img"),
        P("img", None),
        P("img"),
    )
    def body(*blocks):
        one_each = blocks[0].shape[0] == mesh.shape["seq"] == 2
        plan = image_body if one_each and mesh.shape["img"] == 16 else general_body
        return plan(*blocks)

    return jax.shard_map(body, mesh=mesh, in_specs=in_specs, out_specs=out_specs, check_vma=False)
```

```python
import functools
import jax
import jax.numpy as jnp
from jax import lax
from jax.experimental import pallas as pl
from jax.experimental.pallas import tpu as pltpu
from jax.sharding import PartitionSpec as P

HEADS = 12
epsilon = 1e-06


def layer_norm(values, gain, shift):
    center = jnp.mean(values, axis=-1, keepdims=True)
    offset = values - center
    spread = jnp.mean(offset * offset, axis=-1, keepdims=True)
    return offset * lax.rsqrt(spread + epsilon) * gain + shift


def gelu_exact(pre_value):
    return jax.nn.gelu(pre_value, approximate=False)


def split_heads(tensor, head_count):
    images, row_count, columns = tensor.shape
    head_size = columns // head_count
    moved = tensor.reshape(images, row_count, head_count, head_size).transpose(0, 2, 1, 3)
    return moved.reshape(images * head_count, row_count, head_size)


def join_heads(tensor, images):
    combined, row_count, head_size = tensor.shape
    heads_here = combined // images
    moved = tensor.reshape(images, heads_here, row_count, head_size).transpose(0, 2, 1, 3)
    return moved.reshape(images, row_count, heads_here * head_size)


def attend_forward(query_head, key_head, value_head, key_mask):
    scaling = query_head.shape[-1] ** (-0.5)
    row_count = query_head.shape[0]
    blocks = max(1, 2 * row_count // key_head.shape[0])

    def one_block(query_block):
        scores = (
            jnp.einsum("qd,kd->qk", query_block, key_head, preferred_element_type=jnp.float32)
            * scaling
        )
        scores = jnp.where(key_mask[None, :] > 0.5, scores, -1000000000.0)
        highest = jnp.max(scores, axis=-1, keepdims=True)
        weights = jnp.exp(scores - highest)
        totals = jnp.sum(weights, axis=-1, keepdims=True)
        mixed = jnp.dot(
            (weights / totals).astype(jnp.bfloat16), value_head, preferred_element_type=jnp.float32
        )
        return (mixed, (highest + jnp.log(totals))[:, 0])

    mixed, log_sums = lax.map(one_block, query_head.reshape(blocks, row_count // blocks, -1))
    return (mixed.reshape(row_count, -1), log_sums.reshape(row_count))


def attend_backward(query_head, key_head, value_head, key_mask, log_sums, out_grad):
    scaling = query_head.shape[-1] ** (-0.5)
    row_count = query_head.shape[0]
    blocks = max(1, 2 * row_count // key_head.shape[0])
    block_rows = row_count // blocks

    def one_block(carry, pieces):
        key_grad, value_grad = carry
        query_block, log_block, grad_block = pieces
        scores = (
            jnp.einsum("qd,kd->qk", query_block, key_head, preferred_element_type=jnp.float32)
            * scaling
        )
        scores = jnp.where(key_mask[None, :] > 0.5, scores, -1000000000.0)
        weights = jnp.exp(scores - log_block[:, None])
        value_grad = value_grad + jnp.einsum(
            "qk,qd->kd",
            weights.astype(jnp.bfloat16),
            grad_block,
            preferred_element_type=jnp.float32,
        )
        weight_grad = jnp.einsum(
            "qd,kd->qk", grad_block, value_head, preferred_element_type=jnp.float32
        )
        centered = jnp.sum(weights * weight_grad, axis=-1, keepdims=True)
        score_grad = (weights * (weight_grad - centered)).astype(jnp.bfloat16)
        query_grad = jnp.dot(score_grad, key_head, preferred_element_type=jnp.float32) * scaling
        key_grad = (
            key_grad
            + jnp.einsum("qk,qd->kd", score_grad, query_block, preferred_element_type=jnp.float32)
            * scaling
        )
        return ((key_grad, value_grad), query_grad)

    zeros_init = jnp.zeros(key_head.shape, jnp.float32)
    (key_grad, value_grad), query_grad = lax.scan(
        one_block,
        (zeros_init, zeros_init),
        (
            query_head.reshape(blocks, block_rows, -1),
            log_sums.reshape(blocks, block_rows),
            out_grad.reshape(blocks, block_rows, -1),
        ),
    )
    return (query_grad.reshape(row_count, -1), key_grad, value_grad)


def heads_forward(query_heads, key_heads, value_heads, key_masks):
    return lax.map(
        lambda pieces: attend_forward(pieces[0], pieces[1], pieces[2], pieces[3]),
        (query_heads, key_heads, value_heads, key_masks),
    )


def heads_backward(query_heads, key_heads, value_heads, key_masks, log_sums, out_grads):
    return lax.map(
        lambda pieces: attend_backward(
            pieces[0], pieces[1], pieces[2], pieces[3], pieces[4], pieces[5]
        ),
        (query_heads, key_heads, value_heads, key_masks, log_sums, out_grads),
    )


def column_sum(tensor):
    return jnp.sum(tensor.astype(jnp.float32), axis=(0, 1))


def general_body(
    tokens,
    token_mask,
    ln1_gain,
    ln1_bias,
    w_qkv,
    bias_q,
    bias_v,
    w_out,
    bias_out,
    ln2_gain,
    ln2_bias,
    w_up,
    bias_up,
    w_down,
    bias_down,
    cotangent,
):
    (
        gain_one,
        shift_one,
        qkv_full,
        query_bias,
        value_bias,
        out_full,
        out_bias,
        gain_two,
        shift_two,
        up_full,
        up_bias,
        down_full,
        down_bias,
    ) = (
        lax.all_gather(ln1_gain, "img", axis=0, tiled=True),
        lax.all_gather(ln1_bias, "img", axis=0, tiled=True),
        lax.all_gather(w_qkv, "img", axis=0, tiled=True),
        lax.all_gather(bias_q, "img", axis=0, tiled=True),
        lax.all_gather(bias_v, "img", axis=0, tiled=True),
        lax.all_gather(w_out, "img", axis=0, tiled=True),
        lax.all_gather(bias_out, "img", axis=0, tiled=True),
        lax.all_gather(ln2_gain, "img", axis=0, tiled=True),
        lax.all_gather(ln2_bias, "img", axis=0, tiled=True),
        lax.all_gather(w_up, "img", axis=0, tiled=True),
        lax.all_gather(bias_up, "img", axis=0, tiled=True),
        lax.all_gather(w_down, "img", axis=0, tiled=True),
        lax.all_gather(bias_down, "img", axis=0, tiled=True),
    )
    images, shard_rows, model_dim = tokens.shape
    seq_parts = lax.axis_size("seq")
    inputs = tokens.astype(jnp.float32)
    mask_float = token_mask.astype(jnp.float32)
    normed, norm_one_pull = jax.vjp(
        layer_norm, inputs, gain_one.astype(jnp.float32), shift_one.astype(jnp.float32)
    )
    normed_low = normed.astype(jnp.bfloat16)
    projected = jnp.einsum("bsd,de->bse", normed_low, qkv_full, preferred_element_type=jnp.float32)
    query_tok = (projected[..., :model_dim] + query_bias.astype(jnp.float32)).astype(jnp.bfloat16)
    key_tok = projected[..., model_dim : 2 * model_dim].astype(jnp.bfloat16)
    value_tok = (projected[..., 2 * model_dim :] + value_bias.astype(jnp.float32)).astype(
        jnp.bfloat16
    )
    mask_low = token_mask.astype(jnp.bfloat16)
    local_heads = HEADS // seq_parts
    stacked = jnp.stack([query_tok, key_tok, value_tok], axis=2)
    mask_tile = jnp.broadcast_to(mask_low[:, :, None, None], (images, shard_rows, 1, seq_parts))
    stacked_heads, mask_heads = (
        lax.all_to_all(stacked, "seq", split_axis=3, concat_axis=1, tiled=True),
        lax.all_to_all(mask_tile, "seq", split_axis=3, concat_axis=1, tiled=True),
    )
    query_heads = split_heads(stacked_heads[:, :, 0], local_heads)
    key_heads = split_heads(stacked_heads[:, :, 1], local_heads)
    value_heads = split_heads(stacked_heads[:, :, 2], local_heads)
    key_masks = jnp.repeat(mask_heads[:, :, 0, 0].astype(jnp.float32), local_heads, axis=0)
    attended, log_sums = heads_forward(query_heads, key_heads, value_heads, key_masks)
    merged_heads = join_heads(attended, images).astype(jnp.bfloat16)
    merged = lax.all_to_all(merged_heads, "seq", split_axis=1, concat_axis=2, tiled=True)
    branch = jnp.einsum(
        "bsd,de->bse", merged, out_full, preferred_element_type=jnp.float32
    ) + out_bias.astype(jnp.float32)
    middle = inputs + branch
    second, norm_two_pull = jax.vjp(
        layer_norm, middle, gain_two.astype(jnp.float32), shift_two.astype(jnp.float32)
    )
    second_low = second.astype(jnp.bfloat16)
    pre_act = jnp.einsum(
        "bsd,df->bsf", second_low, up_full, preferred_element_type=jnp.float32
    ) + up_bias.astype(jnp.float32)
    hidden, gelu_pull = jax.vjp(gelu_exact, pre_act)
    hidden_low = hidden.astype(jnp.bfloat16)
    output = (
        middle
        + jnp.einsum("bsf,fd->bsd", hidden_low, down_full, preferred_element_type=jnp.float32)
        + down_bias.astype(jnp.float32)
    )
    upstream = cotangent.astype(jnp.float32) * mask_float[..., None]
    down_in = upstream.astype(jnp.bfloat16)
    grad_down = jnp.einsum("bsf,bsd->fd", hidden_low, down_in, preferred_element_type=jnp.float32)
    grad_down_bias = column_sum(down_in)
    hidden_grad = jnp.einsum("bsd,fd->bsf", down_in, down_full, preferred_element_type=jnp.float32)
    pre_grad = gelu_pull(hidden_grad)[0].astype(jnp.bfloat16)
    grad_up = jnp.einsum("bsd,bsf->df", second_low, pre_grad, preferred_element_type=jnp.float32)
    grad_up_bias = column_sum(pre_grad)
    second_grad = jnp.einsum("bsf,df->bsd", pre_grad, up_full, preferred_element_type=jnp.float32)
    middle_ln_grad, grad_gain_two, grad_shift_two = norm_two_pull(second_grad)
    middle_grad = upstream + middle_ln_grad
    branch_grad = middle_grad.astype(jnp.bfloat16)
    grad_out = jnp.einsum("bsd,bse->de", merged, branch_grad, preferred_element_type=jnp.float32)
    grad_out_bias = column_sum(branch_grad)
    merged_grad = jnp.einsum(
        "bse,de->bsd", branch_grad, out_full, preferred_element_type=jnp.float32
    ).astype(jnp.bfloat16)
    grad_heads_in = lax.all_to_all(merged_grad, "seq", split_axis=2, concat_axis=1, tiled=True)
    query_grad, key_grad, value_grad = heads_backward(
        query_heads,
        key_heads,
        value_heads,
        key_masks,
        log_sums,
        split_heads(grad_heads_in, local_heads),
    )
    triple = jnp.stack(
        [
            join_heads(query_grad, images),
            join_heads(key_grad, images),
            join_heads(value_grad, images),
        ],
        axis=2,
    ).astype(jnp.bfloat16)
    qkv_grad = lax.all_to_all(triple, "seq", split_axis=1, concat_axis=3, tiled=True)
    qkv_flat = qkv_grad.reshape(images, shard_rows, 3 * model_dim)
    grad_qkv = jnp.einsum("bsd,bse->de", normed_low, qkv_flat, preferred_element_type=jnp.float32)
    grad_query_bias = column_sum(qkv_grad[:, :, 0])
    grad_value_bias = column_sum(qkv_grad[:, :, 2])
    normed_grad = jnp.einsum("bse,de->bsd", qkv_flat, qkv_full, preferred_element_type=jnp.float32)
    input_ln_grad, grad_gain_one, grad_shift_one = norm_one_pull(normed_grad)
    input_grad = middle_grad + input_ln_grad
    shards_all = (
        lax.psum_scatter(grad_gain_one, "img", scatter_dimension=0, tiled=True),
        lax.psum_scatter(grad_shift_one, "img", scatter_dimension=0, tiled=True),
        lax.psum_scatter(grad_qkv, "img", scatter_dimension=0, tiled=True),
        lax.psum_scatter(grad_query_bias, "img", scatter_dimension=0, tiled=True),
        lax.psum_scatter(grad_value_bias, "img", scatter_dimension=0, tiled=True),
        lax.psum_scatter(grad_out, "img", scatter_dimension=0, tiled=True),
        lax.psum_scatter(grad_out_bias, "img", scatter_dimension=0, tiled=True),
        lax.psum_scatter(grad_gain_two, "img", scatter_dimension=0, tiled=True),
        lax.psum_scatter(grad_shift_two, "img", scatter_dimension=0, tiled=True),
        lax.psum_scatter(grad_up, "img", scatter_dimension=0, tiled=True),
        lax.psum_scatter(grad_up_bias, "img", scatter_dimension=0, tiled=True),
        lax.psum_scatter(grad_down, "img", scatter_dimension=0, tiled=True),
        lax.psum_scatter(grad_down_bias, "img", scatter_dimension=0, tiled=True),
    )
    summed_all = lax.psum(
        (
            shards_all[0],
            shards_all[1],
            shards_all[2],
            shards_all[3],
            shards_all[4],
            shards_all[5],
            shards_all[6],
            shards_all[7],
            shards_all[8],
            shards_all[9],
            shards_all[10],
            shards_all[11],
            shards_all[12],
        ),
        "seq",
    )
    return (
        output,
        input_grad,
        summed_all[0],
        summed_all[1],
        summed_all[2],
        summed_all[3],
        summed_all[4],
        summed_all[5],
        summed_all[6],
        summed_all[7],
        summed_all[8],
        summed_all[9],
        summed_all[10],
        summed_all[11],
        summed_all[12],
    )


LOW = jnp.bfloat16
F32 = jnp.float32
VMEM = 56 * 1024 * 1024
SMALL_PAD = 256


def cost(microseconds):
    return pl.CostEstimate(flops=int(microseconds * 1.15e9), bytes_accessed=1, transcendentals=0)


def dot_nt(left, right):
    return lax.dot_general(left, right, (((1,), (1,)), ((), ())), preferred_element_type=F32)


def dot_nn(left, right):
    return lax.dot_general(left, right, (((1,), (0,)), ((), ())), preferred_element_type=F32)


def dot_tn(left, right):
    return lax.dot_general(left, right, (((0,), (0,)), ((), ())), preferred_element_type=F32)


def attention_forward_kernel(
    scale, size, inputs_ref, small_ref, q_weight_ref, k_weight_ref, v_weight_ref, bias_ref, out_weight_ref, mask_ref,
    out_ref, log_ref, query_ref, key_ref, value_ref, middle_ref, second_ref, normed_ref, merged_ref,
):
    @pl.when(pl.program_id(0) == 0)
    def _():
        unit, _ = norm_parts(inputs_ref[...].astype(F32))
        normed_ref[...] = (unit * small_ref[0:1] + small_ref[1:2]).astype(LOW)

    weight = jnp.concatenate([q_weight_ref[...], k_weight_ref[...], v_weight_ref[...]], axis=1)
    projected = dot_nn(normed_ref[...], weight)
    query_ref[...] = (projected[:, : 2 * size] + bias_ref[2:3]).astype(LOW)
    key_ref[...] = projected[:, 2 * size : 4 * size].astype(LOW)
    value_ref[...] = (projected[:, 4 * size :] + bias_ref[3:4]).astype(LOW)
    real = mask_ref[...] > 0.5
    query = query_ref[...] * jnp.asarray(scale, LOW)
    key = jnp.where(real, key_ref[...], key_ref[0:1, :])
    value = value_ref[...]
    lane = lax.broadcasted_iota(jnp.int32, key.shape, 1)
    pieces = []
    for head in range(2):
        mine = (lane // size) == head
        scores = dot_nt(jnp.where(mine, key, jnp.zeros_like(key)), query)
        highest = jnp.max(scores, axis=0, keepdims=True)
        weights = jnp.exp(scores - highest).astype(LOW)
        extended = jnp.where(real, jnp.where(mine, value, jnp.ones_like(value)), jnp.zeros_like(value))
        mixed = dot_tn(extended, weights)
        own, other = head * size, (1 - head) * size
        totals = mixed[other : other + size, :]
        pieces.append(mixed[own : own + size, :] / totals)
        log_ref[0, head : head + 1, :] = highest + jnp.log(totals[0:1, :])
    out = jnp.concatenate(pieces, axis=0).T.astype(LOW)
    out_ref[...] = out
    for pair in range(HEADS // 2):

        @pl.when(pl.program_id(0) == pair)
        def _():
            merged_ref[:, 2 * size * pair : 2 * size * (pair + 1)] = out

    @pl.when(pl.program_id(0) == HEADS // 2 - 1)
    def _():
        middle = inputs_ref[...].astype(F32) + dot_nn(merged_ref[...], out_weight_ref[...]) + small_ref[4:5]
        middle_ref[...] = middle
        unit, _ = norm_parts(middle)
        second_ref[...] = (unit * small_ref[5:6] + small_ref[6:7]).astype(LOW)


def attention_forward(inputs, small, first, mask_column):
    rows, dim = inputs.shape
    size = dim // HEADS
    pairs = HEADS // 2
    spec = pl.BlockSpec((rows, 2 * size), lambda p: (0, p))
    whole = pl.BlockSpec((rows, dim), lambda p: (0, 0))
    return pl.pallas_call(
        functools.partial(attention_forward_kernel, size ** (-0.5), size),
        grid=(pairs,),
        in_specs=[
            whole,
            pl.BlockSpec(small.shape, lambda p: (0, 0)),
            pl.BlockSpec((dim, 2 * size), lambda p: (0, p)),
            pl.BlockSpec((dim, 2 * size), lambda p: (0, pairs + p)),
            pl.BlockSpec((dim, 2 * size), lambda p: (0, 2 * pairs + p)),
            pl.BlockSpec((small.shape[0], 2 * size), lambda p: (0, p)),
            pl.BlockSpec((dim, dim), lambda p: (0, 3)),
            pl.BlockSpec((rows, 1), lambda p: (0, 0)),
        ],
        out_specs=[spec, pl.BlockSpec((1, 2, rows), lambda p: (p, 0, 0)), spec, spec, spec, whole, whole],
        out_shape=[
            jax.ShapeDtypeStruct((rows, dim), LOW),
            jax.ShapeDtypeStruct((pairs, 2, rows), F32),
            jax.ShapeDtypeStruct((rows, dim), LOW),
            jax.ShapeDtypeStruct((rows, dim), LOW),
            jax.ShapeDtypeStruct((rows, dim), LOW),
            jax.ShapeDtypeStruct((rows, dim), F32),
            jax.ShapeDtypeStruct((rows, dim), LOW),
        ],
        scratch_shapes=[pltpu.VMEM((rows, dim), LOW), pltpu.VMEM((rows, dim), LOW)],
        compiler_params=pltpu.CompilerParams(vmem_limit_bytes=VMEM),
        cost_estimate=cost(18),
        name="attention_forward",
    )(inputs, small, first, first, first, small, first, mask_column)


def attention_backward_kernel(
    scale, size, query_ref, key_ref, value_ref, mask_ref, log_ref, grad_ref, dq_ref, dk_ref, dv_ref
):
    real = mask_ref[...] > 0.5
    query = query_ref[...] * jnp.asarray(scale, LOW)
    zeros = jnp.zeros_like(query)
    key_kept = jnp.where(real, key_ref[...], zeros)
    key = jnp.where(real, key_kept, key_ref[0:1, :])
    value = jnp.where(real, value_ref[...], zeros)
    grad = grad_ref[...]
    lane = lax.broadcasted_iota(jnp.int32, key.shape, 1)
    totals = None
    for head in range(2):
        mine = (lane // size) == head
        scores = dot_nt(jnp.where(mine, key, zeros), query)
        weights = jnp.exp(scores - log_ref[0, head : head + 1, :])
        grad_here = jnp.where(mine, grad, zeros)
        value_grad = dot_nn(weights.astype(LOW), grad_here)
        weight_grad = dot_nt(value, grad_here)
        centered = jnp.sum(weights * weight_grad, axis=0, keepdims=True)
        score_grad = (weights * (weight_grad - centered)).astype(LOW)
        key_grad = dot_nn(score_grad, jnp.where(mine, query, zeros))
        query_grad = dot_tn(jnp.where(mine, key_kept, zeros), score_grad)
        if totals is None:
            totals = (query_grad, key_grad, value_grad)
        else:
            totals = tuple(a + b for a, b in zip(totals, (query_grad, key_grad, value_grad)))
    query_grad, key_grad, value_grad = totals
    dq_ref[...] = (query_grad * scale).T.astype(LOW)
    dk_ref[...] = jnp.where(real, key_grad, 0.0).astype(LOW)
    dv_ref[...] = jnp.where(real, value_grad, 0.0).astype(LOW)


def attention_backward(qkv, mask_column, logs, grad, first, count):
    rows, dim = grad.shape
    size = dim // HEADS
    block = (rows, 2 * size)
    spec = pl.BlockSpec(block, lambda p: (0, first + p))
    out_spec = pl.BlockSpec(block, lambda p: (0, p))
    return pl.pallas_call(
        functools.partial(attention_backward_kernel, size ** (-0.5), size),
        grid=(count,),
        in_specs=[
            spec,
            spec,
            spec,
            pl.BlockSpec((rows, 1), lambda p: (0, 0)),
            pl.BlockSpec((1, 2, rows), lambda p: (first + p, 0, 0)),
            spec,
        ],
        out_specs=[out_spec] * 3,
        out_shape=[jax.ShapeDtypeStruct((rows, 2 * size * count), LOW)] * 3,
        compiler_params=pltpu.CompilerParams(vmem_limit_bytes=VMEM),
        cost_estimate=cost(1),
        name="attention_backward",
    )(*qkv, mask_column, logs, grad)


def split_cores(total_ref, kept_ref, sent_ref, first, columns):
    core = lax.axis_index("img") % 2
    shard = kept_ref.shape[2]
    for pair in range(total_ref.shape[0] // (2 * shard)):
        z, x = first + pair // 2, pair % 2
        kept_ref[z, x, :, columns] = total_ref[pl.ds(pl.multiple_of((2 * pair + core) * shard, 16), shard), :]
        sent_ref[z, x, :, columns] = total_ref[pl.ds(pl.multiple_of((2 * pair + 1 - core) * shard, 16), shard), :]


def mlp_first_kernel(
    shape, second_ref, dz_ref, up_ref, up_bias_ref, down_ref, middle_ref, small_ref,
    out_ref, kept_ref, sent_ref, pre_grad_ref, up_bias_grad_ref, down_grad_ref,
):
    step = pl.program_id(0)
    owners, pieces, dim = shape
    dz = dz_ref[...]
    down = jnp.concatenate(
        [down_ref[o, :, i * dim : (i + 1) * dim] for o in range(owners) for i in range(pieces)], axis=0
    )
    pre_act = dot_nn(second_ref[...], up_ref[...]) + up_bias_ref[...]
    hidden_grad = dot_nt(dz, down)
    cumulative = 0.5 + 0.5 * lax.erf(pre_act * (0.5 ** 0.5))
    density = jnp.exp(-0.5 * pre_act * pre_act) * 0.3989422804014327
    hidden = (pre_act * cumulative).astype(LOW)
    pre_grad = (hidden_grad * (cumulative + pre_act * density)).astype(LOW)
    pre_grad_ref[...] = pre_grad
    bias_grad = jnp.sum(pre_grad.astype(F32), axis=0, keepdims=True)
    turned = jnp.broadcast_to(bias_grad, (128, bias_grad.shape[1])).T
    shard = kept_ref.shape[2]
    lane = lax.broadcasted_iota(jnp.int32, (shard, 128), 1)
    for o in range(owners):
        tile = jnp.zeros((shard, 128), F32)
        for i in range(pieces):
            start = (o * pieces + i) * shard
            tile = jnp.where(lane == i, turned[start : start + shard], tile)
        up_bias_grad_ref[o * shard : (o + 1) * shard, :] = tile.astype(LOW)
    out_part = dot_nn(hidden, down)
    down_grad_ref[...] = dot_tn(hidden, dz).astype(LOW)
    core = lax.axis_index("img") % 2
    for x in range(2):
        for ref, side in ((kept_ref, core), (sent_ref, 1 - core)):
            for i in range(pieces):
                start = pl.multiple_of(((2 * x + side) * pieces + i) * shard, 16)
                ref[0, x, :, i * dim : (i + 1) * dim] = down_grad_ref[pl.ds(start, shard), :]

    @pl.when(step == 0)
    def _():
        out_ref[...] = middle_ref[...] + small_ref[7:8] + out_part

    @pl.when(step > 0)
    def _():
        out_ref[...] += out_part


def mlp_first(second, dz, up_down, up_bias, middle, small, owners):
    rows, dim = second.shape
    width = up_bias.shape[1]
    shard = dim // owners
    pieces = width // dim
    some = owners // pieces
    whole = pl.BlockSpec((rows, dim), lambda j: (0, 0))
    return pl.pallas_call(
        functools.partial(mlp_first_kernel, (some, pieces, dim)),
        grid=(pieces,),
        in_specs=[
            whole,
            whole,
            pl.BlockSpec((dim, dim), lambda j: (0, j)),
            pl.BlockSpec((1, dim), lambda j: (0, j)),
            pl.BlockSpec((some, shard, width), lambda j: (j, 0, 1)),
            whole,
            pl.BlockSpec(small.shape, lambda j: (0, 0)),
        ],
        out_specs=[
            whole,
            pl.BlockSpec((1, 2, shard, width), lambda j: (j, 0, 0, 0)),
            pl.BlockSpec((1, 2, shard, width), lambda j: (j, 0, 0, 0)),
            pl.BlockSpec((rows, dim), lambda j: (0, j)),
            pl.BlockSpec((some * shard, 128), lambda j: (j, 0)),
        ],
        out_shape=[
            jax.ShapeDtypeStruct((rows, dim), F32),
            jax.ShapeDtypeStruct((4, 2, shard, width), LOW),
            jax.ShapeDtypeStruct((4, 2, shard, width), LOW),
            jax.ShapeDtypeStruct((rows, width), LOW),
            jax.ShapeDtypeStruct((dim, 128), LOW),
        ],
        scratch_shapes=[pltpu.VMEM((dim, dim), LOW)],
        compiler_params=pltpu.CompilerParams(vmem_limit_bytes=VMEM),
        cost_estimate=cost(19),
        name="mlp_first",
    )(second, dz, up_down, up_bias, up_down.reshape(owners, shard, 2 * width), middle, small)


def mlp_second_kernel(second_ref, pre_grad_ref, up_ref, second_grad_ref, kept_ref, sent_ref, up_grad_ref):
    step = pl.program_id(0)
    pre_grad = pre_grad_ref[...]
    up_grad_ref[...] = dot_tn(second_ref[...], pre_grad).astype(LOW)
    split_cores(up_grad_ref, kept_ref, sent_ref, 0, slice(None))
    part = dot_nt(pre_grad, up_ref[...])

    @pl.when(step == 0)
    def _():
        second_grad_ref[...] = part

    @pl.when(step > 0)
    def _():
        second_grad_ref[...] += part


def mlp_second(second, pre_grad, up_down, owners):
    rows, dim = second.shape
    width = pre_grad.shape[1]
    shard = dim // owners
    whole = pl.BlockSpec((rows, dim), lambda j: (0, 0))
    split = pl.BlockSpec((4, 2, shard, dim), lambda j: (0, 0, 0, j))
    return pl.pallas_call(
        mlp_second_kernel,
        grid=(width // dim,),
        in_specs=[
            whole,
            pl.BlockSpec((rows, dim), lambda j: (0, j)),
            pl.BlockSpec((dim, dim), lambda j: (0, j)),
        ],
        out_specs=[whole, split, split],
        out_shape=[
            jax.ShapeDtypeStruct((rows, dim), F32),
            jax.ShapeDtypeStruct((4, 2, shard, width), LOW),
            jax.ShapeDtypeStruct((4, 2, shard, width), LOW),
        ],
        scratch_shapes=[pltpu.VMEM((dim, dim), LOW)],
        compiler_params=pltpu.CompilerParams(vmem_limit_bytes=VMEM),
        cost_estimate=cost(1),
        name="mlp_second",
    )(second, pre_grad, up_down)


def norm_parts(values):
    offset = values - jnp.mean(values, axis=-1, keepdims=True)
    inverse = lax.rsqrt(jnp.mean(offset * offset, axis=-1, keepdims=True) + epsilon)
    return offset * inverse, inverse


def norm_back(unit, inverse, gain, grad):
    scaled = grad * gain
    across = jnp.mean(scaled, axis=-1, keepdims=True)
    along = jnp.mean(scaled * unit, axis=-1, keepdims=True)
    return inverse * (scaled - across - unit * along)


def column_sums(values):
    return jnp.sum(values, axis=0, keepdims=True)


def middle_kernel(
    middle_ref, grad_ref, dz_ref, rows_ref, out_full_ref, merged_ref,
    middle_grad_ref, merged_grad_ref, kept_ref, sent_ref, small_ref, out_grad_ref,
):
    unit, inverse = norm_parts(middle_ref[...])
    grad = grad_ref[...]
    upstream = dz_ref[...].astype(F32)
    middle_grad = upstream + norm_back(unit, inverse, rows_ref[5:6], grad)
    middle_grad_ref[...] = middle_grad
    low = middle_grad.astype(LOW)
    merged_grad_ref[...] = dot_nt(low, out_full_ref[...]).astype(LOW)
    out_grad_ref[...] = dot_tn(merged_ref[...], low).astype(LOW)
    split_cores(out_grad_ref, kept_ref, sent_ref, 0, slice(None))
    small_ref[0:1] = column_sums(low.astype(F32))
    small_ref[1:2] = column_sums(grad * unit)
    small_ref[2:3] = column_sums(grad)
    small_ref[3:4] = column_sums(upstream)


def middle_backward(middle, second_grad, dz, small, first, merged, owners):
    rows, dim = middle.shape
    split = (4, 2, dim // owners, dim)
    whole = pl.BlockSpec((rows, dim), lambda j: (0, 0))
    return pl.pallas_call(
        middle_kernel,
        grid=(1,),
        in_specs=[
            whole,
            whole,
            whole,
            pl.BlockSpec(small.shape, lambda j: (0, 0)),
            pl.BlockSpec((dim, dim), lambda j: (0, 3)),
            whole,
        ],
        out_specs=[
            whole,
            whole,
            pl.BlockSpec(split, lambda j: (0, 0, 0, 0)),
            pl.BlockSpec(split, lambda j: (0, 0, 0, 0)),
            pl.BlockSpec((4, dim), lambda j: (0, 0)),
        ],
        out_shape=[
            jax.ShapeDtypeStruct((rows, dim), F32),
            jax.ShapeDtypeStruct((rows, dim), LOW),
            jax.ShapeDtypeStruct(split, LOW),
            jax.ShapeDtypeStruct(split, LOW),
            jax.ShapeDtypeStruct((4, dim), F32),
        ],
        scratch_shapes=[pltpu.VMEM((dim, dim), LOW)],
        compiler_params=pltpu.CompilerParams(vmem_limit_bytes=VMEM),
        cost_estimate=cost(1),
        name="middle_backward",
    )(middle, second_grad, dz, small, first, merged)


def last_kernel(
    inputs_ref, rows_ref, q_low, k_low, v_low, q_high, k_high, v_high, qkv_full_ref,
    middle_grad_ref, small_ref, up_bias_ref, input_grad_ref, kept_ref, sent_ref, total_ref,
):
    unit, inverse = norm_parts(inputs_ref[...].astype(F32))
    gain = rows_ref[0:1]
    normed = (unit * gain + rows_ref[1:2]).astype(LOW)
    grads = [ref[...] for ref in (q_low, q_high, k_low, k_high, v_low, v_high)]
    qkv_grad = jnp.concatenate(grads, axis=1)
    dim = unit.shape[1]
    normed_grad = dot_nt(qkv_grad, qkv_full_ref[...])
    input_grad_ref[...] = middle_grad_ref[...] + norm_back(unit, inverse, gain, normed_grad)
    total_ref[:, : 3 * dim] = dot_tn(normed, qkv_grad).astype(LOW)
    bias_of = column_sums(qkv_grad.astype(F32))
    rows = [column_sums(normed_grad * unit), column_sums(normed_grad), bias_of[:, :dim], bias_of[:, 2 * dim :]]
    rows += [small_ref[...]]
    taken = sum(row.shape[0] for row in rows)
    rows.append(jnp.zeros((128 - taken, dim), F32))
    total_ref[:, 3 * dim : 3 * dim + 128] = jnp.concatenate(rows, axis=0).T.astype(LOW)
    total_ref[:, 3 * dim + 128 :] = up_bias_ref[...]
    split_cores(total_ref, kept_ref, sent_ref, 0, slice(None))


def last_backward(inputs, small_rows, grads_low, grads_high, first, middle_grad, small, up_bias, owners):
    rows, dim = inputs.shape
    columns = 3 * dim + SMALL_PAD

    def whole(*shape):
        return pl.BlockSpec(shape, lambda j: (0,) * len(shape))

    split = jax.ShapeDtypeStruct((4, 2, dim // owners, columns), LOW)
    return pl.pallas_call(
        last_kernel,
        grid=(1,),
        in_specs=[whole(rows, dim), whole(*small_rows.shape)]
        + [whole(*g.shape) for g in (*grads_low, *grads_high)]
        + [whole(dim, 3 * dim), whole(rows, dim), whole(*small.shape), whole(*up_bias.shape)],
        out_specs=[whole(rows, dim), whole(*split.shape), whole(*split.shape)],
        out_shape=[jax.ShapeDtypeStruct((rows, dim), F32), split, split],
        scratch_shapes=[pltpu.VMEM((dim, columns), LOW)],
        compiler_params=pltpu.CompilerParams(vmem_limit_bytes=VMEM),
        cost_estimate=cost(1),
        name="last_backward",
    )(inputs, small_rows, *grads_low, *grads_high, first, middle_grad, small, up_bias)


def own_and_away(blocks):
    here = lax.axis_index("seq")
    own = lax.dynamic_index_in_dim(blocks, here, 0, keepdims=False)
    return own, lax.dynamic_index_in_dim(blocks, 1 - here, 0, keepdims=False)


def both_images(own, back):
    here = lax.axis_index("seq")
    back = back.astype(F32)
    return jnp.where(here == 0, jnp.stack([own, back]), jnp.stack([back, own]))


def gather(block):
    return lax.all_gather(block, "img", axis=0, tiled=True)


def place():
    img = lax.axis_index("img")
    return img // 4, (img // 2) % 2, img % 2, lax.axis_index("seq")


def swap(block, z=0, x=0, core=0, y=0):
    bits = z * 8 + x * 4 + core * 2 + y
    return lax.ppermute(block, ("img", "seq"), [(i, i ^ bits) for i in range(32)])


def assemble_kernel(small_at, *refs):
    refs, out_ref, small_ref = refs[:-2], refs[-2], refs[-1]
    here_z, here_x, here_core, here_y = place()
    half = out_ref.shape[2] // 2
    for index, ref in enumerate(refs):
        first, x, y, core = index // 8, index // 4 % 2, index // 2 % 2, index % 2
        columns = pl.ds(pl.multiple_of((here_y ^ y) * half, half), half)
        for i in range(ref.shape[0]):
            owner = (here_z ^ (first + i)) * 4 + (here_x ^ x) * 2 + (here_core ^ core)
            out_ref[owner, :, columns] = ref[i]
    small = jnp.concatenate([out_ref[i, :, small_at : small_at + 128] for i in range(16)], axis=0)
    small_ref[...] = small.astype(F32).T[:16]


def gather_links(block, rows, later):
    shard, columns = block.shape
    half = columns // 2
    own = lax.dynamic_slice_in_dim(block, lax.axis_index("seq") * half, half, 1)[None]
    rows = swap(rows, y=1)
    line = [swap(own, z=z) for z in (1, 2, 3)]
    own_x, own_y = swap(own, x=1), swap(own, y=1)
    rest = jnp.concatenate(line)
    rest, rows, own_x, own_y = tie(rest, rows, own_x, own_y)
    rest_x = swap(rest, x=1)
    refs = []
    for part in (own, own_y, own_x, swap(own_x, y=1), rest, swap(rest, y=1), rest_x, swap(rest_x, y=1)):
        refs += [part, swap(part, core=1)]
    whole, small = pl.pallas_call(
        functools.partial(assemble_kernel, columns - SMALL_PAD),
        out_shape=[
            jax.ShapeDtypeStruct((16, shard, columns), LOW),
            jax.ShapeDtypeStruct((16, 16 * shard), F32),
        ],
        compiler_params=pltpu.CompilerParams(vmem_limit_bytes=VMEM),
        name="assemble",
    )(*refs)
    return whole.reshape(16 * shard, columns), small, rows, later


def total(pieces):
    result = pieces[0].astype(F32)
    for piece in pieces[1:]:
        result = result + piece.astype(F32)
    return result.astype(LOW)


def plane_pieces(paired):
    _, x, _, y = place()
    rows, half = paired.shape[2], paired.shape[3] // 2

    def part(x_index, y_index):
        return lax.dynamic_slice(paired, (0, x_index, 0, y_index * half), (4, 1, rows, half))[:, 0]

    return [part(x, y), part(1 - x, y), part(x, 1 - y), part(1 - x, 1 - y)]


def plane_swaps(pieces):
    return [pieces[0], swap(pieces[1], x=1), swap(pieces[2], y=1), swap(pieces[3], x=1, y=1)]


def line_pieces(line):
    z = place()[0]
    return [lax.dynamic_index_in_dim(line, z ^ step, 0, keepdims=False) for step in range(4)]


def half_line(line, bit):
    return lax.dynamic_slice_in_dim(line, bit * (line.shape[0] // 2), line.shape[0] // 2, 0)


def line_swaps(pieces):
    return [pieces[0]] + [swap(pieces[step], z=step) for step in (1, 2, 3)]


def join_halves(own, other):
    here = lax.axis_index("seq")
    return jnp.where(
        here == 0, jnp.concatenate([own, other], axis=1), jnp.concatenate([other, own], axis=1)
    ).astype(F32)


def tie(*values):
    return lax.optimization_barrier(values)


def image_body(
    tokens, token_mask, ln1_gain, ln1_bias, w_qkv, bias_q, bias_v, w_out, bias_out,
    ln2_gain, ln2_bias, w_up, bias_up, w_down, bias_down, cotangent,
):
    shard_rows, dim = tokens.shape[1:]
    owners = lax.axis_size("img")
    shard = dim // owners
    width = bias_up.shape[0] * owners
    pieces = width // dim

    up_down = jnp.concatenate(
        [w_up, w_down.reshape(pieces, shard, dim).swapaxes(0, 1).reshape(shard, width)], axis=1
    )
    rows_small = jnp.concatenate(
        [jnp.stack([ln1_gain, ln1_bias, bias_q, bias_v, bias_out, ln2_gain, ln2_bias, bias_down])]
        + [bias_up.reshape(pieces, shard)]
    )
    count = rows_small.shape[0]
    padding = jnp.pad(rows_small.T, ((0, 0), (0, SMALL_PAD - count)))
    mask_rows = jnp.broadcast_to(
        jnp.pad(token_mask.astype(LOW), ((0, 0), (0, dim - shard_rows)))[:, None, :], (2, 16, dim)
    )
    own, away = own_and_away(jnp.concatenate([tokens, mask_rows], axis=1))
    first, small, away, up_down = gather_links(jnp.concatenate([w_qkv, w_out, padding], axis=1), away, up_down)
    up_down = gather(up_down)
    masked = jnp.where(token_mask[..., None] > 0, cotangent, jnp.zeros_like(cotangent))
    own_in, away_in = own_and_away(masked)
    first, away_in = tie(first, away_in)
    down_in = jnp.concatenate([own_in, swap(away_in, y=1)], axis=0)
    up_bias = small[8:count].reshape(pieces, owners, shard).swapaxes(0, 1).reshape(1, width)

    both = jnp.stack([own, away])
    inputs_low = both[:, :shard_rows].reshape(2 * shard_rows, dim)
    mask_column = both[:, shard_rows, :shard_rows].astype(F32).reshape(2 * shard_rows, 1)
    merged, logs, *qkv, middle, second = attention_forward(inputs_low, small, first, mask_column)
    output, down_kept, down_sent, pre_grad, grad_up_bias = mlp_first(
        second, down_in, up_down, up_bias, middle, small, owners
    )
    output_own, output_away = output[:shard_rows], output[shard_rows:].astype(LOW)
    pre_grad, output_away, down_sent = tie(pre_grad, output_away, down_sent)
    output_back, down_sent = swap(output_away, y=1), swap(down_sent, core=1)
    second_grad, up_kept, up_sent = mlp_second(second, pre_grad, up_down, owners)
    second_grad, up_kept, up_sent, output_back, down_sent = tie(second_grad, up_kept, up_sent, output_back, down_sent)
    down_pieces = plane_pieces(total([down_kept, down_sent]))
    second_grad, up_sent, *down_pieces = tie(second_grad, up_sent, *down_pieces)
    down_pieces, up_sent = plane_swaps(down_pieces), swap(up_sent, core=1)
    middle_grad, merged_grad, out_kept, out_sent, small_grads = middle_backward(
        middle, second_grad, down_in, small, first, merged, owners
    )
    middle_grad, merged_grad, out_kept, out_sent, small_grads, up_sent = tie(
        middle_grad, merged_grad, out_kept, out_sent, small_grads, up_sent
    )
    out_sent = swap(out_sent, core=1)
    up_paired = total([up_kept, up_sent])
    merged_grad, up_paired = tie(merged_grad, up_paired)
    pairs = HEADS // 2
    grads_low = attention_backward(qkv, mask_column, logs, merged_grad, 0, pairs // 2)
    tied = tie(merged_grad, out_sent, *grads_low)
    merged_grad, grads_low = tied[0], tied[2:]
    up_pieces = [
        jnp.concatenate(both, axis=2)
        for both in zip(plane_pieces(up_paired), plane_pieces(total([out_kept, tied[1]])))
    ]
    tied = tie(merged_grad, *down_pieces, *up_pieces)
    merged_grad, down_line, up_pieces = tied[0], total(tied[1:5]), tied[5:]
    z = place()[0]
    merged_grad, down_away, *up_pieces = tie(merged_grad, half_line(down_line, 1 - z // 2), *up_pieces)
    down_away, up_pieces = swap(down_away, z=2), plane_swaps(up_pieces)
    grads_high = attention_backward(qkv, mask_column, logs, merged_grad, pairs // 2, pairs - pairs // 2)
    *grads_high, down_away = tie(*grads_high, down_away)
    down_two = total([half_line(down_line, z // 2), down_away])
    grad_up_bias, down_away = tie(grad_up_bias, half_line(down_two, 1 - z % 2))
    down_away = swap(down_away, z=1)
    input_grad, last_kept, last_sent = last_backward(
        inputs_low, small, grads_low, grads_high, first, middle_grad, small_grads, grad_up_bias, owners
    )
    tied = tie(input_grad, last_kept, last_sent, down_away, *up_pieces)
    input_grad, last_kept, last_sent, down_away = tied[:4]
    up_line = total(tied[4:])
    input_away = input_grad[shard_rows:].astype(LOW)
    last_sent = swap(last_sent, core=1)
    last_pieces = plane_pieces(total([last_kept, last_sent]))
    tied = tie(*last_pieces, *line_pieces(up_line))
    last_pieces, up_pieces = plane_swaps(tied[:4]), line_swaps(tied[4:])
    down_own = total([half_line(down_two, z % 2), down_away])[0]
    mlp_own = jnp.concatenate([down_own, total(up_pieces)], axis=1)
    tied = tie(input_away, *last_pieces)
    input_away, last_pieces = tied[0], line_pieces(total(tied[1:]))
    tied = tie(input_away, mlp_own, *last_pieces)
    input_away, mlp_own, last_pieces = tied[0], tied[1], line_swaps(tied[2:])
    mlp_other, input_back = swap(mlp_own, y=1), swap(input_away, y=1)
    tied = tie(mlp_other, input_back, *last_pieces)
    mlp_other, input_back, last_pieces = tied[0], tied[1], tied[2:]
    last_own = total(last_pieces)
    last_sum = join_halves(last_own, swap(last_own, y=1))
    down_sum = join_halves(mlp_own[:, : width // 2], mlp_other[:, : width // 2])
    up_sum = join_halves(mlp_own[:, width // 2 : width], mlp_other[:, width // 2 : width])
    out_sum = join_halves(mlp_own[:, width:], mlp_other[:, width:])
    smalls = last_sum[:, 3 * dim : 3 * dim + 8].T
    return (
        both_images(output_own, output_back), both_images(input_grad[:shard_rows], input_back),
        smalls[0], smalls[1], last_sum[:, : 3 * dim], smalls[2], smalls[3], out_sum,
        smalls[4], smalls[5], smalls[6], up_sum, last_sum[:, 3 * dim + 128 : 3 * dim + 128 + pieces].T.reshape(-1),
        down_sum.reshape(shard, pieces, dim).swapaxes(0, 1).reshape(pieces * shard, dim), smalls[7],
    )


def solution(mesh):
    in_specs = (
        P("img", "seq", None),
        P("img", "seq"),
        P("img"),
        P("img"),
        P("img", None),
        P("img"),
        P("img"),
        P("img", None),
        P("img"),
        P("img"),
        P("img"),
        P("img", None),
        P("img"),
        P("img", None),
        P("img"),
        P("img", "seq", None),
    )
    out_specs = (
        P("img", "seq", None),
        P("img", "seq", None),
        P("img"),
        P("img"),
        P("img", None),
        P("img"),
        P("img"),
        P("img", None),
        P("img"),
        P("img"),
        P("img"),
        P("img", None),
        P("img"),
        P("img", None),
        P("img"),
    )
    def body(*blocks):
        one_each = blocks[0].shape[0] == mesh.shape["seq"] == 2
        plan = image_body if one_each and mesh.shape["img"] == 16 else general_body
        return plan(*blocks)

    return jax.shard_map(body, mesh=mesh, in_specs=in_specs, out_specs=out_specs, check_vma=False)
```

```python
import functools
import jax
import jax.numpy as jnp
from jax import lax
from jax.experimental import pallas as pl
from jax.experimental.pallas import tpu as pltpu
from jax.sharding import PartitionSpec as P

HEADS = 12
epsilon = 1e-06


def layer_norm(values, gain, shift):
    center = jnp.mean(values, axis=-1, keepdims=True)
    offset = values - center
    spread = jnp.mean(offset * offset, axis=-1, keepdims=True)
    return offset * lax.rsqrt(spread + epsilon) * gain + shift


def gelu_exact(pre_value):
    return jax.nn.gelu(pre_value, approximate=False)


def split_heads(tensor, head_count):
    images, row_count, columns = tensor.shape
    head_size = columns // head_count
    moved = tensor.reshape(images, row_count, head_count, head_size).transpose(0, 2, 1, 3)
    return moved.reshape(images * head_count, row_count, head_size)


def join_heads(tensor, images):
    combined, row_count, head_size = tensor.shape
    heads_here = combined // images
    moved = tensor.reshape(images, heads_here, row_count, head_size).transpose(0, 2, 1, 3)
    return moved.reshape(images, row_count, heads_here * head_size)


def attend_forward(query_head, key_head, value_head, key_mask):
    scaling = query_head.shape[-1] ** (-0.5)
    row_count = query_head.shape[0]
    blocks = max(1, 2 * row_count // key_head.shape[0])

    def one_block(query_block):
        scores = (
            jnp.einsum("qd,kd->qk", query_block, key_head, preferred_element_type=jnp.float32)
            * scaling
        )
        scores = jnp.where(key_mask[None, :] > 0.5, scores, -1000000000.0)
        highest = jnp.max(scores, axis=-1, keepdims=True)
        weights = jnp.exp(scores - highest)
        totals = jnp.sum(weights, axis=-1, keepdims=True)
        mixed = jnp.dot(
            (weights / totals).astype(jnp.bfloat16), value_head, preferred_element_type=jnp.float32
        )
        return (mixed, (highest + jnp.log(totals))[:, 0])

    mixed, log_sums = lax.map(one_block, query_head.reshape(blocks, row_count // blocks, -1))
    return (mixed.reshape(row_count, -1), log_sums.reshape(row_count))


def attend_backward(query_head, key_head, value_head, key_mask, log_sums, out_grad):
    scaling = query_head.shape[-1] ** (-0.5)
    row_count = query_head.shape[0]
    blocks = max(1, 2 * row_count // key_head.shape[0])
    block_rows = row_count // blocks

    def one_block(carry, pieces):
        key_grad, value_grad = carry
        query_block, log_block, grad_block = pieces
        scores = (
            jnp.einsum("qd,kd->qk", query_block, key_head, preferred_element_type=jnp.float32)
            * scaling
        )
        scores = jnp.where(key_mask[None, :] > 0.5, scores, -1000000000.0)
        weights = jnp.exp(scores - log_block[:, None])
        value_grad = value_grad + jnp.einsum(
            "qk,qd->kd",
            weights.astype(jnp.bfloat16),
            grad_block,
            preferred_element_type=jnp.float32,
        )
        weight_grad = jnp.einsum(
            "qd,kd->qk", grad_block, value_head, preferred_element_type=jnp.float32
        )
        centered = jnp.sum(weights * weight_grad, axis=-1, keepdims=True)
        score_grad = (weights * (weight_grad - centered)).astype(jnp.bfloat16)
        query_grad = jnp.dot(score_grad, key_head, preferred_element_type=jnp.float32) * scaling
        key_grad = (
            key_grad
            + jnp.einsum("qk,qd->kd", score_grad, query_block, preferred_element_type=jnp.float32)
            * scaling
        )
        return ((key_grad, value_grad), query_grad)

    zeros_init = jnp.zeros(key_head.shape, jnp.float32)
    (key_grad, value_grad), query_grad = lax.scan(
        one_block,
        (zeros_init, zeros_init),
        (
            query_head.reshape(blocks, block_rows, -1),
            log_sums.reshape(blocks, block_rows),
            out_grad.reshape(blocks, block_rows, -1),
        ),
    )
    return (query_grad.reshape(row_count, -1), key_grad, value_grad)


def heads_forward(query_heads, key_heads, value_heads, key_masks):
    return lax.map(
        lambda pieces: attend_forward(pieces[0], pieces[1], pieces[2], pieces[3]),
        (query_heads, key_heads, value_heads, key_masks),
    )


def heads_backward(query_heads, key_heads, value_heads, key_masks, log_sums, out_grads):
    return lax.map(
        lambda pieces: attend_backward(
            pieces[0], pieces[1], pieces[2], pieces[3], pieces[4], pieces[5]
        ),
        (query_heads, key_heads, value_heads, key_masks, log_sums, out_grads),
    )


def column_sum(tensor):
    return jnp.sum(tensor.astype(jnp.float32), axis=(0, 1))


def general_body(
    tokens,
    token_mask,
    ln1_gain,
    ln1_bias,
    w_qkv,
    bias_q,
    bias_v,
    w_out,
    bias_out,
    ln2_gain,
    ln2_bias,
    w_up,
    bias_up,
    w_down,
    bias_down,
    cotangent,
):
    (
        gain_one,
        shift_one,
        qkv_full,
        query_bias,
        value_bias,
        out_full,
        out_bias,
        gain_two,
        shift_two,
        up_full,
        up_bias,
        down_full,
        down_bias,
    ) = (
        lax.all_gather(ln1_gain, "img", axis=0, tiled=True),
        lax.all_gather(ln1_bias, "img", axis=0, tiled=True),
        lax.all_gather(w_qkv, "img", axis=0, tiled=True),
        lax.all_gather(bias_q, "img", axis=0, tiled=True),
        lax.all_gather(bias_v, "img", axis=0, tiled=True),
        lax.all_gather(w_out, "img", axis=0, tiled=True),
        lax.all_gather(bias_out, "img", axis=0, tiled=True),
        lax.all_gather(ln2_gain, "img", axis=0, tiled=True),
        lax.all_gather(ln2_bias, "img", axis=0, tiled=True),
        lax.all_gather(w_up, "img", axis=0, tiled=True),
        lax.all_gather(bias_up, "img", axis=0, tiled=True),
        lax.all_gather(w_down, "img", axis=0, tiled=True),
        lax.all_gather(bias_down, "img", axis=0, tiled=True),
    )
    images, shard_rows, model_dim = tokens.shape
    seq_parts = lax.axis_size("seq")
    inputs = tokens.astype(jnp.float32)
    mask_float = token_mask.astype(jnp.float32)
    normed, norm_one_pull = jax.vjp(
        layer_norm, inputs, gain_one.astype(jnp.float32), shift_one.astype(jnp.float32)
    )
    normed_low = normed.astype(jnp.bfloat16)
    projected = jnp.einsum("bsd,de->bse", normed_low, qkv_full, preferred_element_type=jnp.float32)
    query_tok = (projected[..., :model_dim] + query_bias.astype(jnp.float32)).astype(jnp.bfloat16)
    key_tok = projected[..., model_dim : 2 * model_dim].astype(jnp.bfloat16)
    value_tok = (projected[..., 2 * model_dim :] + value_bias.astype(jnp.float32)).astype(
        jnp.bfloat16
    )
    mask_low = token_mask.astype(jnp.bfloat16)
    local_heads = HEADS // seq_parts
    stacked = jnp.stack([query_tok, key_tok, value_tok], axis=2)
    mask_tile = jnp.broadcast_to(mask_low[:, :, None, None], (images, shard_rows, 1, seq_parts))
    stacked_heads, mask_heads = (
        lax.all_to_all(stacked, "seq", split_axis=3, concat_axis=1, tiled=True),
        lax.all_to_all(mask_tile, "seq", split_axis=3, concat_axis=1, tiled=True),
    )
    query_heads = split_heads(stacked_heads[:, :, 0], local_heads)
    key_heads = split_heads(stacked_heads[:, :, 1], local_heads)
    value_heads = split_heads(stacked_heads[:, :, 2], local_heads)
    key_masks = jnp.repeat(mask_heads[:, :, 0, 0].astype(jnp.float32), local_heads, axis=0)
    attended, log_sums = heads_forward(query_heads, key_heads, value_heads, key_masks)
    merged_heads = join_heads(attended, images).astype(jnp.bfloat16)
    merged = lax.all_to_all(merged_heads, "seq", split_axis=1, concat_axis=2, tiled=True)
    branch = jnp.einsum(
        "bsd,de->bse", merged, out_full, preferred_element_type=jnp.float32
    ) + out_bias.astype(jnp.float32)
    middle = inputs + branch
    second, norm_two_pull = jax.vjp(
        layer_norm, middle, gain_two.astype(jnp.float32), shift_two.astype(jnp.float32)
    )
    second_low = second.astype(jnp.bfloat16)
    pre_act = jnp.einsum(
        "bsd,df->bsf", second_low, up_full, preferred_element_type=jnp.float32
    ) + up_bias.astype(jnp.float32)
    hidden, gelu_pull = jax.vjp(gelu_exact, pre_act)
    hidden_low = hidden.astype(jnp.bfloat16)
    output = (
        middle
        + jnp.einsum("bsf,fd->bsd", hidden_low, down_full, preferred_element_type=jnp.float32)
        + down_bias.astype(jnp.float32)
    )
    upstream = cotangent.astype(jnp.float32) * mask_float[..., None]
    down_in = upstream.astype(jnp.bfloat16)
    grad_down = jnp.einsum("bsf,bsd->fd", hidden_low, down_in, preferred_element_type=jnp.float32)
    grad_down_bias = column_sum(down_in)
    hidden_grad = jnp.einsum("bsd,fd->bsf", down_in, down_full, preferred_element_type=jnp.float32)
    pre_grad = gelu_pull(hidden_grad)[0].astype(jnp.bfloat16)
    grad_up = jnp.einsum("bsd,bsf->df", second_low, pre_grad, preferred_element_type=jnp.float32)
    grad_up_bias = column_sum(pre_grad)
    second_grad = jnp.einsum("bsf,df->bsd", pre_grad, up_full, preferred_element_type=jnp.float32)
    middle_ln_grad, grad_gain_two, grad_shift_two = norm_two_pull(second_grad)
    middle_grad = upstream + middle_ln_grad
    branch_grad = middle_grad.astype(jnp.bfloat16)
    grad_out = jnp.einsum("bsd,bse->de", merged, branch_grad, preferred_element_type=jnp.float32)
    grad_out_bias = column_sum(branch_grad)
    merged_grad = jnp.einsum(
        "bse,de->bsd", branch_grad, out_full, preferred_element_type=jnp.float32
    ).astype(jnp.bfloat16)
    grad_heads_in = lax.all_to_all(merged_grad, "seq", split_axis=2, concat_axis=1, tiled=True)
    query_grad, key_grad, value_grad = heads_backward(
        query_heads,
        key_heads,
        value_heads,
        key_masks,
        log_sums,
        split_heads(grad_heads_in, local_heads),
    )
    triple = jnp.stack(
        [
            join_heads(query_grad, images),
            join_heads(key_grad, images),
            join_heads(value_grad, images),
        ],
        axis=2,
    ).astype(jnp.bfloat16)
    qkv_grad = lax.all_to_all(triple, "seq", split_axis=1, concat_axis=3, tiled=True)
    qkv_flat = qkv_grad.reshape(images, shard_rows, 3 * model_dim)
    grad_qkv = jnp.einsum("bsd,bse->de", normed_low, qkv_flat, preferred_element_type=jnp.float32)
    grad_query_bias = column_sum(qkv_grad[:, :, 0])
    grad_value_bias = column_sum(qkv_grad[:, :, 2])
    normed_grad = jnp.einsum("bse,de->bsd", qkv_flat, qkv_full, preferred_element_type=jnp.float32)
    input_ln_grad, grad_gain_one, grad_shift_one = norm_one_pull(normed_grad)
    input_grad = middle_grad + input_ln_grad
    shards_all = (
        lax.psum_scatter(grad_gain_one, "img", scatter_dimension=0, tiled=True),
        lax.psum_scatter(grad_shift_one, "img", scatter_dimension=0, tiled=True),
        lax.psum_scatter(grad_qkv, "img", scatter_dimension=0, tiled=True),
        lax.psum_scatter(grad_query_bias, "img", scatter_dimension=0, tiled=True),
        lax.psum_scatter(grad_value_bias, "img", scatter_dimension=0, tiled=True),
        lax.psum_scatter(grad_out, "img", scatter_dimension=0, tiled=True),
        lax.psum_scatter(grad_out_bias, "img", scatter_dimension=0, tiled=True),
        lax.psum_scatter(grad_gain_two, "img", scatter_dimension=0, tiled=True),
        lax.psum_scatter(grad_shift_two, "img", scatter_dimension=0, tiled=True),
        lax.psum_scatter(grad_up, "img", scatter_dimension=0, tiled=True),
        lax.psum_scatter(grad_up_bias, "img", scatter_dimension=0, tiled=True),
        lax.psum_scatter(grad_down, "img", scatter_dimension=0, tiled=True),
        lax.psum_scatter(grad_down_bias, "img", scatter_dimension=0, tiled=True),
    )
    summed_all = lax.psum(
        (
            shards_all[0],
            shards_all[1],
            shards_all[2],
            shards_all[3],
            shards_all[4],
            shards_all[5],
            shards_all[6],
            shards_all[7],
            shards_all[8],
            shards_all[9],
            shards_all[10],
            shards_all[11],
            shards_all[12],
        ),
        "seq",
    )
    return (
        output,
        input_grad,
        summed_all[0],
        summed_all[1],
        summed_all[2],
        summed_all[3],
        summed_all[4],
        summed_all[5],
        summed_all[6],
        summed_all[7],
        summed_all[8],
        summed_all[9],
        summed_all[10],
        summed_all[11],
        summed_all[12],
    )


LOW = jnp.bfloat16
F32 = jnp.float32
VMEM = 56 * 1024 * 1024
SMALL_PAD = 256


def cost(microseconds):
    return pl.CostEstimate(flops=int(microseconds * 1.15e9), bytes_accessed=1, transcendentals=0)


def dot_nt(left, right):
    return lax.dot_general(left, right, (((1,), (1,)), ((), ())), preferred_element_type=F32)


def dot_nn(left, right):
    return lax.dot_general(left, right, (((1,), (0,)), ((), ())), preferred_element_type=F32)


def dot_tn(left, right):
    return lax.dot_general(left, right, (((0,), (0,)), ((), ())), preferred_element_type=F32)


def attention_forward_kernel(
    scale, size, inputs_ref, small_ref, q_weight_ref, k_weight_ref, v_weight_ref, bias_ref, out_weight_ref, mask_ref,
    out_ref, log_ref, query_ref, key_ref, value_ref, middle_ref, second_ref, normed_ref, merged_ref,
):
    @pl.when(pl.program_id(0) == 0)
    def _():
        unit, _ = norm_parts(inputs_ref[...].astype(F32))
        normed_ref[...] = (unit * small_ref[0:1] + small_ref[1:2]).astype(LOW)

    weight = jnp.concatenate([q_weight_ref[...], k_weight_ref[...], v_weight_ref[...]], axis=1)
    projected = dot_nn(normed_ref[...], weight)
    query_ref[...] = (projected[:, : 2 * size] + bias_ref[2:3]).astype(LOW)
    key_ref[...] = projected[:, 2 * size : 4 * size].astype(LOW)
    value_ref[...] = (projected[:, 4 * size :] + bias_ref[3:4]).astype(LOW)
    real = mask_ref[...] > 0.5
    query = query_ref[...] * jnp.asarray(scale, LOW)
    key = jnp.where(real, key_ref[...], key_ref[0:1, :])
    value = value_ref[...]
    lane = lax.broadcasted_iota(jnp.int32, key.shape, 1)
    pieces = []
    for head in range(2):
        mine = (lane // size) == head
        scores = dot_nt(jnp.where(mine, key, jnp.zeros_like(key)), query)
        highest = jnp.max(scores, axis=0, keepdims=True)
        weights = jnp.exp(scores - highest).astype(LOW)
        extended = jnp.where(real, jnp.where(mine, value, jnp.ones_like(value)), jnp.zeros_like(value))
        mixed = dot_tn(extended, weights)
        own, other = head * size, (1 - head) * size
        totals = mixed[other : other + size, :]
        pieces.append(mixed[own : own + size, :] / totals)
        log_ref[0, head : head + 1, :] = highest + jnp.log(totals[0:1, :])
    out = jnp.concatenate(pieces, axis=0).T.astype(LOW)
    out_ref[...] = out
    for pair in range(HEADS // 2):

        @pl.when(pl.program_id(0) == pair)
        def _():
            merged_ref[:, 2 * size * pair : 2 * size * (pair + 1)] = out

    @pl.when(pl.program_id(0) == HEADS // 2 - 1)
    def _():
        middle = inputs_ref[...].astype(F32) + dot_nn(merged_ref[...], out_weight_ref[...]) + small_ref[4:5]
        middle_ref[...] = middle
        unit, _ = norm_parts(middle)
        second_ref[...] = (unit * small_ref[5:6] + small_ref[6:7]).astype(LOW)


def attention_forward(inputs, small, first, mask_column):
    rows, dim = inputs.shape
    size = dim // HEADS
    pairs = HEADS // 2
    spec = pl.BlockSpec((rows, 2 * size), lambda p: (0, p))
    whole = pl.BlockSpec((rows, dim), lambda p: (0, 0))
    return pl.pallas_call(
        functools.partial(attention_forward_kernel, size ** (-0.5), size),
        grid=(pairs,),
        in_specs=[
            whole,
            pl.BlockSpec(small.shape, lambda p: (0, 0)),
            pl.BlockSpec((dim, 2 * size), lambda p: (0, p)),
            pl.BlockSpec((dim, 2 * size), lambda p: (0, pairs + p)),
            pl.BlockSpec((dim, 2 * size), lambda p: (0, 2 * pairs + p)),
            pl.BlockSpec((small.shape[0], 2 * size), lambda p: (0, p)),
            pl.BlockSpec((dim, dim), lambda p: (0, 3)),
            pl.BlockSpec((rows, 1), lambda p: (0, 0)),
        ],
        out_specs=[spec, pl.BlockSpec((1, 2, rows), lambda p: (p, 0, 0)), spec, spec, spec, whole, whole],
        out_shape=[
            jax.ShapeDtypeStruct((rows, dim), LOW),
            jax.ShapeDtypeStruct((pairs, 2, rows), F32),
            jax.ShapeDtypeStruct((rows, dim), LOW),
            jax.ShapeDtypeStruct((rows, dim), LOW),
            jax.ShapeDtypeStruct((rows, dim), LOW),
            jax.ShapeDtypeStruct((rows, dim), F32),
            jax.ShapeDtypeStruct((rows, dim), LOW),
        ],
        scratch_shapes=[pltpu.VMEM((rows, dim), LOW), pltpu.VMEM((rows, dim), LOW)],
        compiler_params=pltpu.CompilerParams(vmem_limit_bytes=VMEM),
        cost_estimate=cost(18),
        name="attention_forward",
    )(inputs, small, first, first, first, small, first, mask_column)


def attention_backward_kernel(
    scale, size, query_ref, key_ref, value_ref, mask_ref, log_ref, grad_ref, dq_ref, dk_ref, dv_ref
):
    real = mask_ref[...] > 0.5
    query = query_ref[...] * jnp.asarray(scale, LOW)
    zeros = jnp.zeros_like(query)
    key_kept = jnp.where(real, key_ref[...], zeros)
    key = jnp.where(real, key_kept, key_ref[0:1, :])
    value = jnp.where(real, value_ref[...], zeros)
    grad = grad_ref[...]
    lane = lax.broadcasted_iota(jnp.int32, key.shape, 1)
    totals = None
    for head in range(2):
        mine = (lane // size) == head
        scores = dot_nt(jnp.where(mine, key, zeros), query)
        weights = jnp.exp(scores - log_ref[0, head : head + 1, :])
        grad_here = jnp.where(mine, grad, zeros)
        value_grad = dot_nn(weights.astype(LOW), grad_here)
        weight_grad = dot_nt(value, grad_here)
        centered = jnp.sum(weights * weight_grad, axis=0, keepdims=True)
        score_grad = (weights * (weight_grad - centered)).astype(LOW)
        key_grad = dot_nn(score_grad, jnp.where(mine, query, zeros))
        query_grad = dot_tn(jnp.where(mine, key_kept, zeros), score_grad)
        if totals is None:
            totals = (query_grad, key_grad, value_grad)
        else:
            totals = tuple(a + b for a, b in zip(totals, (query_grad, key_grad, value_grad)))
    query_grad, key_grad, value_grad = totals
    dq_ref[...] = (query_grad * scale).T.astype(LOW)
    dk_ref[...] = jnp.where(real, key_grad, 0.0).astype(LOW)
    dv_ref[...] = jnp.where(real, value_grad, 0.0).astype(LOW)


def attention_backward(qkv, mask_column, logs, grad, first, count):
    rows, dim = grad.shape
    size = dim // HEADS
    block = (rows, 2 * size)
    spec = pl.BlockSpec(block, lambda p: (0, first + p))
    out_spec = pl.BlockSpec(block, lambda p: (0, p))
    return pl.pallas_call(
        functools.partial(attention_backward_kernel, size ** (-0.5), size),
        grid=(count,),
        in_specs=[
            spec,
            spec,
            spec,
            pl.BlockSpec((rows, 1), lambda p: (0, 0)),
            pl.BlockSpec((1, 2, rows), lambda p: (first + p, 0, 0)),
            spec,
        ],
        out_specs=[out_spec] * 3,
        out_shape=[jax.ShapeDtypeStruct((rows, 2 * size * count), LOW)] * 3,
        compiler_params=pltpu.CompilerParams(vmem_limit_bytes=VMEM),
        cost_estimate=cost(1),
        name="attention_backward",
    )(*qkv, mask_column, logs, grad)


def split_cores(total_ref, kept_ref, sent_ref, first, columns):
    core = lax.axis_index("img") % 2
    shard = kept_ref.shape[2]
    for pair in range(total_ref.shape[0] // (2 * shard)):
        z, x = first + pair // 2, pair % 2
        kept_ref[z, x, :, columns] = total_ref[pl.ds(pl.multiple_of((2 * pair + core) * shard, 16), shard), :]
        sent_ref[z, x, :, columns] = total_ref[pl.ds(pl.multiple_of((2 * pair + 1 - core) * shard, 16), shard), :]


def mlp_first_kernel(
    shape, second_ref, dz_ref, up_ref, up_bias_ref, down_ref, middle_ref, small_ref,
    out_ref, away_ref, kept_ref, sent_ref, pre_grad_ref, up_bias_grad_ref, down_grad_ref,
):
    step = pl.program_id(0)
    owners, pieces, dim = shape
    dz = dz_ref[...]
    down = jnp.concatenate(
        [down_ref[o, :, i * dim : (i + 1) * dim] for o in range(owners) for i in range(pieces)], axis=0
    )
    pre_act = dot_nn(second_ref[...], up_ref[...]) + up_bias_ref[...]
    hidden_grad = dot_nt(dz, down)
    cumulative = 0.5 + 0.5 * lax.erf(pre_act * (0.5 ** 0.5))
    density = jnp.exp(-0.5 * pre_act * pre_act) * 0.3989422804014327
    hidden = (pre_act * cumulative).astype(LOW)
    pre_grad = (hidden_grad * (cumulative + pre_act * density)).astype(LOW)
    pre_grad_ref[...] = pre_grad
    bias_grad = jnp.sum(pre_grad.astype(F32), axis=0, keepdims=True)
    turned = jnp.broadcast_to(bias_grad, (128, bias_grad.shape[1])).T
    shard = kept_ref.shape[2]
    lane = lax.broadcasted_iota(jnp.int32, (shard, 128), 1)
    for o in range(owners):
        tile = jnp.zeros((shard, 128), F32)
        for i in range(pieces):
            start = (o * pieces + i) * shard
            tile = jnp.where(lane == i, turned[start : start + shard], tile)
        up_bias_grad_ref[o * shard : (o + 1) * shard, :] = tile.astype(LOW)
    out_part = dot_nn(hidden, down)
    down_grad_ref[...] = dot_tn(hidden, dz).astype(LOW)
    core = lax.axis_index("img") % 2
    for x in range(2):
        for ref, side in ((kept_ref, core), (sent_ref, 1 - core)):
            for i in range(pieces):
                start = pl.multiple_of(((2 * x + side) * pieces + i) * shard, 16)
                ref[0, x, :, i * dim : (i + 1) * dim] = down_grad_ref[pl.ds(start, shard), :]

    @pl.when(step == 0)
    def _():
        out_ref[...] = middle_ref[...] + small_ref[7:8] + out_part

    @pl.when(step > 0)
    def _():
        out_ref[...] += out_part

    @pl.when(step == pl.num_programs(0) - 1)
    def _():
        away_ref[...] = out_ref[away_ref.shape[0] :, :].astype(LOW)


def mlp_first(second, dz, up_down, up_bias, middle, small, owners):
    rows, dim = second.shape
    width = up_bias.shape[1]
    shard = dim // owners
    pieces = width // dim
    some = owners // pieces
    whole = pl.BlockSpec((rows, dim), lambda j: (0, 0))
    return pl.pallas_call(
        functools.partial(mlp_first_kernel, (some, pieces, dim)),
        grid=(pieces,),
        in_specs=[
            whole,
            whole,
            pl.BlockSpec((dim, dim), lambda j: (0, j)),
            pl.BlockSpec((1, dim), lambda j: (0, j)),
            pl.BlockSpec((some, shard, width), lambda j: (j, 0, 1)),
            whole,
            pl.BlockSpec(small.shape, lambda j: (0, 0)),
        ],
        out_specs=[
            whole,
            pl.BlockSpec((rows // 2, dim), lambda j: (0, 0)),
            pl.BlockSpec((1, 2, shard, width), lambda j: (j, 0, 0, 0)),
            pl.BlockSpec((1, 2, shard, width), lambda j: (j, 0, 0, 0)),
            pl.BlockSpec((rows, dim), lambda j: (0, j)),
            pl.BlockSpec((some * shard, 128), lambda j: (j, 0)),
        ],
        out_shape=[
            jax.ShapeDtypeStruct((rows, dim), F32),
            jax.ShapeDtypeStruct((rows // 2, dim), LOW),
            jax.ShapeDtypeStruct((4, 2, shard, width), LOW),
            jax.ShapeDtypeStruct((4, 2, shard, width), LOW),
            jax.ShapeDtypeStruct((rows, width), LOW),
            jax.ShapeDtypeStruct((dim, 128), LOW),
        ],
        scratch_shapes=[pltpu.VMEM((dim, dim), LOW)],
        compiler_params=pltpu.CompilerParams(vmem_limit_bytes=VMEM),
        cost_estimate=cost(19),
        name="mlp_first",
    )(second, dz, up_down, up_bias, up_down.reshape(owners, shard, 2 * width), middle, small)


def mlp_second_kernel(second_ref, pre_grad_ref, up_ref, second_grad_ref, kept_ref, sent_ref, up_grad_ref):
    step = pl.program_id(0)
    pre_grad = pre_grad_ref[...]
    up_grad_ref[...] = dot_tn(second_ref[...], pre_grad).astype(LOW)
    split_cores(up_grad_ref, kept_ref, sent_ref, 0, slice(None))
    part = dot_nt(pre_grad, up_ref[...])

    @pl.when(step == 0)
    def _():
        second_grad_ref[...] = part

    @pl.when(step > 0)
    def _():
        second_grad_ref[...] += part


def mlp_second(second, pre_grad, up_down, owners):
    rows, dim = second.shape
    width = pre_grad.shape[1]
    shard = dim // owners
    whole = pl.BlockSpec((rows, dim), lambda j: (0, 0))
    split = pl.BlockSpec((4, 2, shard, dim), lambda j: (0, 0, 0, j))
    return pl.pallas_call(
        mlp_second_kernel,
        grid=(width // dim,),
        in_specs=[
            whole,
            pl.BlockSpec((rows, dim), lambda j: (0, j)),
            pl.BlockSpec((dim, dim), lambda j: (0, j)),
        ],
        out_specs=[whole, split, split],
        out_shape=[
            jax.ShapeDtypeStruct((rows, dim), F32),
            jax.ShapeDtypeStruct((4, 2, shard, width), LOW),
            jax.ShapeDtypeStruct((4, 2, shard, width), LOW),
        ],
        scratch_shapes=[pltpu.VMEM((dim, dim), LOW)],
        compiler_params=pltpu.CompilerParams(vmem_limit_bytes=VMEM),
        cost_estimate=cost(1),
        name="mlp_second",
    )(second, pre_grad, up_down)


def norm_parts(values):
    offset = values - jnp.mean(values, axis=-1, keepdims=True)
    inverse = lax.rsqrt(jnp.mean(offset * offset, axis=-1, keepdims=True) + epsilon)
    return offset * inverse, inverse


def norm_back(unit, inverse, gain, grad):
    scaled = grad * gain
    across = jnp.mean(scaled, axis=-1, keepdims=True)
    along = jnp.mean(scaled * unit, axis=-1, keepdims=True)
    return inverse * (scaled - across - unit * along)


def column_sums(values):
    return jnp.sum(values, axis=0, keepdims=True)


def middle_kernel(
    middle_ref, grad_ref, dz_ref, rows_ref, out_full_ref, merged_ref,
    middle_grad_ref, merged_grad_ref, kept_ref, sent_ref, small_ref, out_grad_ref,
):
    unit, inverse = norm_parts(middle_ref[...])
    grad = grad_ref[...]
    upstream = dz_ref[...].astype(F32)
    middle_grad = upstream + norm_back(unit, inverse, rows_ref[5:6], grad)
    middle_grad_ref[...] = middle_grad
    low = middle_grad.astype(LOW)
    merged_grad_ref[...] = dot_nt(low, out_full_ref[...]).astype(LOW)
    out_grad_ref[...] = dot_tn(merged_ref[...], low).astype(LOW)
    split_cores(out_grad_ref, kept_ref, sent_ref, 0, slice(None))
    small_ref[0:1] = column_sums(low.astype(F32))
    small_ref[1:2] = column_sums(grad * unit)
    small_ref[2:3] = column_sums(grad)
    small_ref[3:4] = column_sums(upstream)


def middle_backward(middle, second_grad, dz, small, first, merged, owners):
    rows, dim = middle.shape
    split = (4, 2, dim // owners, dim)
    whole = pl.BlockSpec((rows, dim), lambda j: (0, 0))
    return pl.pallas_call(
        middle_kernel,
        grid=(1,),
        in_specs=[
            whole,
            whole,
            whole,
            pl.BlockSpec(small.shape, lambda j: (0, 0)),
            pl.BlockSpec((dim, dim), lambda j: (0, 3)),
            whole,
        ],
        out_specs=[
            whole,
            whole,
            pl.BlockSpec(split, lambda j: (0, 0, 0, 0)),
            pl.BlockSpec(split, lambda j: (0, 0, 0, 0)),
            pl.BlockSpec((4, dim), lambda j: (0, 0)),
        ],
        out_shape=[
            jax.ShapeDtypeStruct((rows, dim), F32),
            jax.ShapeDtypeStruct((rows, dim), LOW),
            jax.ShapeDtypeStruct(split, LOW),
            jax.ShapeDtypeStruct(split, LOW),
            jax.ShapeDtypeStruct((4, dim), F32),
        ],
        scratch_shapes=[pltpu.VMEM((dim, dim), LOW)],
        compiler_params=pltpu.CompilerParams(vmem_limit_bytes=VMEM),
        cost_estimate=cost(1),
        name="middle_backward",
    )(middle, second_grad, dz, small, first, merged)


def last_kernel(
    inputs_ref, rows_ref, q_low, k_low, v_low, q_high, k_high, v_high, qkv_full_ref,
    middle_grad_ref, small_ref, up_bias_ref,
    input_grad_ref, away_ref, kept_ref, sent_ref, total_ref,
):
    unit, inverse = norm_parts(inputs_ref[...].astype(F32))
    gain = rows_ref[0:1]
    normed = (unit * gain + rows_ref[1:2]).astype(LOW)
    grads = [ref[...] for ref in (q_low, q_high, k_low, k_high, v_low, v_high)]
    qkv_grad = jnp.concatenate(grads, axis=1)
    dim = unit.shape[1]
    normed_grad = dot_nt(qkv_grad, qkv_full_ref[...])
    input_grad = middle_grad_ref[...] + norm_back(unit, inverse, gain, normed_grad)
    input_grad_ref[...] = input_grad
    away_ref[...] = input_grad[away_ref.shape[0] :].astype(LOW)
    total_ref[:, : 3 * dim] = dot_tn(normed, qkv_grad).astype(LOW)
    bias_of = column_sums(qkv_grad.astype(F32))
    rows = [column_sums(normed_grad * unit), column_sums(normed_grad), bias_of[:, :dim], bias_of[:, 2 * dim :]]
    rows += [small_ref[...]]
    taken = sum(row.shape[0] for row in rows)
    rows.append(jnp.zeros((128 - taken, dim), F32))
    total_ref[:, 3 * dim : 3 * dim + 128] = jnp.concatenate(rows, axis=0).T.astype(LOW)
    total_ref[:, 3 * dim + 128 :] = up_bias_ref[...]
    split_cores(total_ref, kept_ref, sent_ref, 0, slice(None))


def last_backward(inputs, small_rows, grads_low, grads_high, first, middle_grad, small, up_bias, owners):
    rows, dim = inputs.shape
    columns = 3 * dim + SMALL_PAD

    def whole(*shape):
        return pl.BlockSpec(shape, lambda j: (0,) * len(shape))

    split = jax.ShapeDtypeStruct((4, 2, dim // owners, columns), LOW)
    return pl.pallas_call(
        last_kernel,
        grid=(1,),
        in_specs=[whole(rows, dim), whole(*small_rows.shape)]
        + [whole(*g.shape) for g in (*grads_low, *grads_high)]
        + [whole(dim, 3 * dim), whole(rows, dim), whole(*small.shape), whole(*up_bias.shape)],
        out_specs=[whole(rows, dim), whole(rows // 2, dim), whole(*split.shape), whole(*split.shape)],
        out_shape=[jax.ShapeDtypeStruct((rows, dim), F32), jax.ShapeDtypeStruct((rows // 2, dim), LOW), split, split],
        scratch_shapes=[pltpu.VMEM((dim, columns), LOW)],
        compiler_params=pltpu.CompilerParams(vmem_limit_bytes=VMEM),
        cost_estimate=cost(1),
        name="last_backward",
    )(inputs, small_rows, *grads_low, *grads_high, first, middle_grad, small, up_bias)


def own_and_away(blocks):
    here = lax.axis_index("seq")
    own = lax.dynamic_index_in_dim(blocks, here, 0, keepdims=False)
    return own, lax.dynamic_index_in_dim(blocks, 1 - here, 0, keepdims=False)


def both_images(own, back):
    here = lax.axis_index("seq")
    back = back.astype(F32)
    return jnp.where(here == 0, jnp.stack([own, back]), jnp.stack([back, own]))


def gather(block):
    return lax.all_gather(block, "img", axis=0, tiled=True)


def place():
    img = lax.axis_index("img")
    return img // 4, (img // 2) % 2, img % 2, lax.axis_index("seq")


def swap(block, z=0, x=0, core=0, y=0):
    bits = z * 8 + x * 4 + core * 2 + y
    return lax.ppermute(block, ("img", "seq"), [(i, i ^ bits) for i in range(32)])


def assemble_kernel(small_at, *refs):
    refs, out_ref, small_ref = refs[:-2], refs[-2], refs[-1]
    here_z, here_x, here_core, here_y = place()
    half = out_ref.shape[2] // 2
    for index, ref in enumerate(refs):
        first, x, y, core = index // 8, index // 4 % 2, index // 2 % 2, index % 2
        columns = pl.ds(pl.multiple_of((here_y ^ y) * half, half), half)
        for i in range(ref.shape[0]):
            owner = (here_z ^ (first + i)) * 4 + (here_x ^ x) * 2 + (here_core ^ core)
            out_ref[owner, :, columns] = ref[i]
    small = jnp.concatenate([out_ref[i, :, small_at : small_at + 128] for i in range(16)], axis=0)
    small_ref[...] = small.astype(F32).T[:16]


def gather_links(block, rows, later):
    shard, columns = block.shape
    half = columns // 2
    own = lax.dynamic_slice_in_dim(block, lax.axis_index("seq") * half, half, 1)[None]
    rows = swap(rows, y=1)
    line = [swap(own, z=z) for z in (1, 2, 3)]
    own_x, own_y = swap(own, x=1), swap(own, y=1)
    rest = jnp.concatenate(line)
    rest, rows, own_x, own_y = tie(rest, rows, own_x, own_y)
    rest_x = swap(rest, x=1)
    refs = []
    for part in (own, own_y, own_x, swap(own_x, y=1), rest, swap(rest, y=1), rest_x, swap(rest_x, y=1)):
        refs += [part, swap(part, core=1)]
    whole, small = pl.pallas_call(
        functools.partial(assemble_kernel, columns - SMALL_PAD),
        out_shape=[
            jax.ShapeDtypeStruct((16, shard, columns), LOW),
            jax.ShapeDtypeStruct((16, 16 * shard), F32),
        ],
        compiler_params=pltpu.CompilerParams(vmem_limit_bytes=VMEM),
        name="assemble",
    )(*refs)
    return whole.reshape(16 * shard, columns), small, rows, later


def total(pieces):
    result = pieces[0].astype(F32)
    for piece in pieces[1:]:
        result = result + piece.astype(F32)
    return result.astype(LOW)


def plane_pieces(paired):
    _, x, _, y = place()
    rows, half = paired.shape[2], paired.shape[3] // 2

    def part(x_index, y_index):
        return lax.dynamic_slice(paired, (0, x_index, 0, y_index * half), (4, 1, rows, half))[:, 0]

    return [part(x, y), part(1 - x, y), part(x, 1 - y), part(1 - x, 1 - y)]


def plane_swaps(pieces):
    return [pieces[0], swap(pieces[1], x=1), swap(pieces[2], y=1), swap(pieces[3], x=1, y=1)]


def line_pieces(line):
    z = place()[0]
    return [lax.dynamic_index_in_dim(line, z ^ step, 0, keepdims=False) for step in range(4)]


def half_line(line, bit):
    return lax.dynamic_slice_in_dim(line, bit * (line.shape[0] // 2), line.shape[0] // 2, 0)


def line_swaps(pieces):
    return [pieces[0]] + [swap(pieces[step], z=step) for step in (1, 2, 3)]


def join_halves(own, other):
    here = lax.axis_index("seq")
    return jnp.where(
        here == 0, jnp.concatenate([own, other], axis=1), jnp.concatenate([other, own], axis=1)
    ).astype(F32)


def tie(*values):
    return lax.optimization_barrier(values)


def image_body(
    tokens, token_mask, ln1_gain, ln1_bias, w_qkv, bias_q, bias_v, w_out, bias_out,
    ln2_gain, ln2_bias, w_up, bias_up, w_down, bias_down, cotangent,
):
    shard_rows, dim = tokens.shape[1:]
    owners = lax.axis_size("img")
    shard = dim // owners
    width = bias_up.shape[0] * owners
    pieces = width // dim

    up_down = jnp.concatenate(
        [w_up, w_down.reshape(pieces, shard, dim).swapaxes(0, 1).reshape(shard, width)], axis=1
    )
    rows_small = jnp.concatenate(
        [jnp.stack([ln1_gain, ln1_bias, bias_q, bias_v, bias_out, ln2_gain, ln2_bias, bias_down])]
        + [bias_up.reshape(pieces, shard)]
    )
    count = rows_small.shape[0]
    padding = jnp.pad(rows_small.T, ((0, 0), (0, SMALL_PAD - count)))
    mask_rows = jnp.broadcast_to(
        jnp.pad(token_mask.astype(LOW), ((0, 0), (0, dim - shard_rows)))[:, None, :], (2, 16, dim)
    )
    own, away = own_and_away(jnp.concatenate([tokens, mask_rows], axis=1))
    first, small, away, up_down = gather_links(jnp.concatenate([w_qkv, w_out, padding], axis=1), away, up_down)
    up_down = gather(up_down)
    masked = jnp.where(token_mask[..., None] > 0, cotangent, jnp.zeros_like(cotangent))
    own_in, away_in = own_and_away(masked)
    first, away_in = tie(first, away_in)
    down_in = jnp.concatenate([own_in, swap(away_in, y=1)], axis=0)
    up_bias = small[8:count].reshape(pieces, owners, shard).swapaxes(0, 1).reshape(1, width)

    both = jnp.stack([own, away])
    inputs_low = both[:, :shard_rows].reshape(2 * shard_rows, dim)
    mask_column = both[:, shard_rows, :shard_rows].astype(F32).reshape(2 * shard_rows, 1)
    merged, logs, *qkv, middle, second = attention_forward(inputs_low, small, first, mask_column)
    output, output_away, down_kept, down_sent, pre_grad, grad_up_bias = mlp_first(
        second, down_in, up_down, up_bias, middle, small, owners
    )
    output_own = output[:shard_rows]
    pre_grad, output_away, down_sent = tie(pre_grad, output_away, down_sent)
    output_back, down_sent = swap(output_away, y=1), swap(down_sent, core=1)
    second_grad, up_kept, up_sent = mlp_second(second, pre_grad, up_down, owners)
    second_grad, up_kept, up_sent, output_back, down_sent = tie(second_grad, up_kept, up_sent, output_back, down_sent)
    down_pieces = plane_pieces(total([down_kept, down_sent]))
    second_grad, up_sent, *down_pieces = tie(second_grad, up_sent, *down_pieces)
    down_pieces, up_sent = plane_swaps(down_pieces), swap(up_sent, core=1)
    middle_grad, merged_grad, out_kept, out_sent, small_grads = middle_backward(
        middle, second_grad, down_in, small, first, merged, owners
    )
    middle_grad, merged_grad, out_kept, out_sent, small_grads, up_sent = tie(
        middle_grad, merged_grad, out_kept, out_sent, small_grads, up_sent
    )
    out_sent = swap(out_sent, core=1)
    up_paired = total([up_kept, up_sent])
    merged_grad, up_paired = tie(merged_grad, up_paired)
    pairs = HEADS // 2
    grads_low = attention_backward(qkv, mask_column, logs, merged_grad, 0, pairs // 2)
    tied = tie(merged_grad, out_sent, *grads_low)
    merged_grad, grads_low = tied[0], tied[2:]
    up_pieces = [
        jnp.concatenate(both, axis=2)
        for both in zip(plane_pieces(up_paired), plane_pieces(total([out_kept, tied[1]])))
    ]
    tied = tie(merged_grad, *down_pieces, *up_pieces)
    merged_grad, down_line, up_pieces = tied[0], total(tied[1:5]), tied[5:]
    z = place()[0]
    merged_grad, down_away, *up_pieces = tie(merged_grad, half_line(down_line, 1 - z // 2), *up_pieces)
    down_away, up_pieces = swap(down_away, z=2), plane_swaps(up_pieces)
    grads_high = attention_backward(qkv, mask_column, logs, merged_grad, pairs // 2, pairs - pairs // 2)
    *grads_high, down_away = tie(*grads_high, down_away)
    down_two = total([half_line(down_line, z // 2), down_away])
    grad_up_bias, down_away = tie(grad_up_bias, half_line(down_two, 1 - z % 2))
    down_away = swap(down_away, z=1)
    input_grad, input_away, last_kept, last_sent = last_backward(
        inputs_low, small, grads_low, grads_high, first, middle_grad, small_grads, grad_up_bias, owners
    )
    tied = tie(input_grad, input_away, last_kept, last_sent, down_away, *up_pieces)
    input_grad, input_away, last_kept, last_sent, down_away = tied[:5]
    up_line = total(tied[5:])
    last_sent = swap(last_sent, core=1)
    last_pieces = plane_pieces(total([last_kept, last_sent]))
    tied = tie(*last_pieces, *line_pieces(up_line))
    last_pieces, up_pieces = plane_swaps(tied[:4]), line_swaps(tied[4:])
    down_own = total([half_line(down_two, z % 2), down_away])[0]
    mlp_own = jnp.concatenate([down_own, total(up_pieces)], axis=1)
    tied = tie(input_away, *last_pieces)
    input_away, last_pieces = tied[0], line_pieces(total(tied[1:]))
    tied = tie(input_away, mlp_own, *last_pieces)
    input_away, mlp_own, last_pieces = tied[0], tied[1], line_swaps(tied[2:])
    mlp_other, input_back = swap(mlp_own, y=1), swap(input_away, y=1)
    tied = tie(mlp_other, input_back, *last_pieces)
    mlp_other, input_back, last_pieces = tied[0], tied[1], tied[2:]
    last_own = total(last_pieces)
    last_sum = join_halves(last_own, swap(last_own, y=1))
    down_sum = join_halves(mlp_own[:, : width // 2], mlp_other[:, : width // 2])
    up_sum = join_halves(mlp_own[:, width // 2 : width], mlp_other[:, width // 2 : width])
    out_sum = join_halves(mlp_own[:, width:], mlp_other[:, width:])
    smalls = last_sum[:, 3 * dim : 3 * dim + 8].T
    return (
        both_images(output_own, output_back), both_images(input_grad[:shard_rows], input_back),
        smalls[0], smalls[1], last_sum[:, : 3 * dim], smalls[2], smalls[3], out_sum,
        smalls[4], smalls[5], smalls[6], up_sum, last_sum[:, 3 * dim + 128 : 3 * dim + 128 + pieces].T.reshape(-1),
        down_sum.reshape(shard, pieces, dim).swapaxes(0, 1).reshape(pieces * shard, dim), smalls[7],
    )


def solution(mesh):
    in_specs = (
        P("img", "seq", None),
        P("img", "seq"),
        P("img"),
        P("img"),
        P("img", None),
        P("img"),
        P("img"),
        P("img", None),
        P("img"),
        P("img"),
        P("img"),
        P("img", None),
        P("img"),
        P("img", None),
        P("img"),
        P("img", "seq", None),
    )
    out_specs = (
        P("img", "seq", None),
        P("img", "seq", None),
        P("img"),
        P("img"),
        P("img", None),
        P("img"),
        P("img"),
        P("img", None),
        P("img"),
        P("img"),
        P("img"),
        P("img", None),
        P("img"),
        P("img", None),
        P("img"),
    )
    def body(*blocks):
        one_each = blocks[0].shape[0] == mesh.shape["seq"] == 2
        plan = image_body if one_each and mesh.shape["img"] == 16 else general_body
        return plan(*blocks)

    return jax.shard_map(body, mesh=mesh, in_specs=in_specs, out_specs=out_specs, check_vma=False)
```
